32 devices in a mesh: groups: 2 (over y), dp: 4 (over x, core), mp: 4 (over z).
Axes of the slice: x: 2, y: 2, z: 4, core: 2. Of those that a mesh axis runs over, the one named last changes fastest.
Arguments:
- tokens: bfloat16 [8192, 5120], P(('groups', 'dp'), 'mp'), parts along dimension 0, may hold values from -6 to 6
- grad_out: bfloat16 [8192, 5120], P(('groups', 'dp'), 'mp'), parts along dimension 0, may hold values from -6 to 6
- gate_w: bfloat16 [5120, 13824], P(None, 'mp'), may hold values from -0.078125 to 0.078125
- up_w: bfloat16 [5120, 13824], P(None, 'mp'), may hold values from -0.078125 to 0.078125
- proj_in: bfloat16 [13824, 64], P('mp'), may hold values from -0.0546875 to 0.0546875
- proj_out: bfloat16 [5120, 64], P('mp'), may hold values from -0.078125 to 0.078125
- lengths: int32 [16], P(('groups', 'dp')), parts along dimension 0, may hold values from 1 to 512, as said below
- loss_mask: int32 [16, 512], P(('groups', 'dp')), parts along dimension 0, may hold values 0 or 1
- queries: bfloat16 [512, 4096], P('mp', 'dp'), may hold values from -0.375 to 0.375
Outputs:
- scores: float32 [16, 512], P(('groups', 'dp'), 'mp'), parts along dimension 0
The draws below stay inside these ranges and needn't reach their ends.
There are 2 independent parts, one for each index of `groups`. The reference program is written for one: setup_inputs(seed, part) draws one part's arguments, and reference() takes and returns one part's arrays. A program takes and returns all parts, laid end to end along the dimension named above; an argument that names none is the same for every part. Nothing has to cross between parts.
Inputs may be any that keep to these rules, and one draw needn't show every extreme that they name: `lengths`: some rollout of every window has all 512 tokens.
All inputs are finite; a program needn't handle non-finite values. No bound on the sum of `loss_mask` on one device may be relied on, other than what follows from the above.
Results may differ from the reference program's by a relative error of at most 0.0041.
Values may be sent and summed in bfloat16 or wider, within the bound.
No kernel may reach another device: no remote copies, remote signals or barrier semaphores. Data moves between devices by JAX's collectives and lax.ppermute only.
A program may use at most 192 MiB of HBM per device.

```python
import jax
import jax.numpy as jnp
from jax import lax

D = 5120
FF = 13824
RANK = 64
LEN = 512
ROLLOUTS = 8
TOKENS = 4096
NQ = 512
SKETCH = 4096


def draw_lengths(key, part):
    key = jax.random.fold_in(key, 11)
    drawn = jax.random.randint(key, (ROLLOUTS,), 1, LEN + 1, dtype=jnp.int32)
    return drawn.at[0].set(LEN)


def with_ends(entries, key, smallest, largest):
    longest = entries.shape.index(max(entries.shape))
    spots = []
    for shift in (0, 1):
        where = [jax.random.randint(jax.random.fold_in(key, axis), (), 0, length) for axis, length in enumerate(entries.shape)]
        where[longest] = (where[longest] + shift) % entries.shape[longest]
        spots.append(tuple(where))
    return entries.at[spots[0]].set(smallest).at[spots[1]].set(largest)


def block_scale(own_key, dims, shards, low, high):
    level = 1.0
    for axis_at, shards_of in shards:
        draws = jax.random.uniform(jax.random.fold_in(jax.random.fold_in(own_key, 6), axis_at), (shards_of,), jnp.float32, low / len(shards), high / len(shards))
        level = level * jnp.repeat(jnp.exp(draws), dims[axis_at] // shards_of).reshape((-1,) + (1,) * (len(dims) - 1 - axis_at))
    return level


def centred(rng, extent, spread, most, split=(), held_as=jnp.bfloat16):
    result = jax.random.normal(rng, extent, jnp.float32) * spread
    if len(split) > 0:
        result = block_scale(rng, extent, split, -0.22, 0.18) * result
    return jnp.clip(result, min=-most, max=most).astype(held_as)


def setup_inputs(seed: int = 0, part: int = 0) -> dict:
    key_of = jax.random.split(jax.random.key(seed), 10)
    part_keys = jax.random.split(jax.random.fold_in(key_of[9], part), 10)
    tokens = centred(part_keys[0], (TOKENS, D), 1.0, 6.0, ((0, 4), (1, 4)))
    grad_out = centred(part_keys[1], (TOKENS, D), 1.0, 6.0, ((0, 4), (1, 4)))
    gate_w = centred(key_of[2], (D, FF), D ** -0.5, 0.078125, ((1, 4),))
    up_w = centred(key_of[3], (D, FF), D ** -0.5, 0.078125, ((1, 4),))
    proj_in = centred(key_of[4], (FF, RANK), FF ** -0.5, 0.0546875, ((0, 4),))
    proj_out = centred(key_of[5], (D, RANK), D ** -0.5, 0.078125, ((0, 4),))
    lengths = draw_lengths(jax.random.fold_in(jax.random.fold_in(key_of[9], part), 71), part)
    loss_mask = with_ends((jax.random.randint(part_keys[7], (ROLLOUTS, LEN), 0, 4) < 3).astype(jnp.int32), jax.random.fold_in(part_keys[7], 1), 0, 1)
    queries = centred(key_of[8], (NQ, SKETCH), (SKETCH // 16) ** -0.5, 0.375, ((0, 4), (1, 4)))
    return dict(tokens=tokens, grad_out=grad_out, gate_w=gate_w, up_w=up_w, proj_in=proj_in, proj_out=proj_out, lengths=lengths, loss_mask=loss_mask, queries=queries)


def reference(tokens, grad_out, gate_w, up_w, proj_in, proj_out, lengths, loss_mask, queries):
    gate_sum = jnp.dot(tokens, gate_w, preferred_element_type=jnp.float32)
    up_sum = jnp.dot(tokens, up_w, preferred_element_type=jnp.float32)
    hidden = (jax.nn.silu(gate_sum) * up_sum).astype(jnp.bfloat16)
    act_proj = jnp.dot(hidden, proj_in, preferred_element_type=jnp.float32)
    grad_proj = jnp.dot(grad_out, proj_out, preferred_element_type=jnp.float32)
    positions = jnp.arange(LEN, dtype=jnp.int32)
    keep_mask = ((positions[None, :] < lengths[:, None]) & (loss_mask == 1)).astype(jnp.float32)
    weighted = grad_proj.reshape(ROLLOUTS, LEN, RANK) * keep_mask[:, :, None]
    sketch_sum = jnp.einsum('rti,rtj->rij', weighted, act_proj.reshape(ROLLOUTS, LEN, RANK), precision=lax.Precision.HIGHEST)
    norm_factor = 1.0 / jnp.sqrt(jnp.float32(LEN))
    sketch = (sketch_sum * norm_factor).reshape(ROLLOUTS, RANK * RANK).astype(jnp.bfloat16)
    return jnp.dot(sketch, queries.T, preferred_element_type=jnp.float32)
```

```python
import functools
import math

import jax
import jax.numpy as jnp
from jax import lax
from jax.experimental import pallas as pl
from jax.experimental.pallas import tpu as pltpu
from jax.sharding import PartitionSpec as P

BF16, F32 = jnp.bfloat16, jnp.float32
ROWS = 128
LINE = 4


def dot32(a, b):
    return jnp.dot(a, b, preferred_element_type=F32)


def mlp_kernel(slots, takes, ends, ids, *refs):
    refs = list(refs)
    xs, wgs, wus = refs[:slots], refs[slots : 2 * slots], refs[2 * slots : 3 * slots]
    rest = refs[3 * slots :]
    width = wgs[0].shape[1]
    both = None
    for x, wg, wu in zip(xs, wgs, wus):
        part = dot32(x[...], jnp.concatenate([wg[...], wu[...]], axis=1))
        both = part if both is None else both + part
    gate, up = both[:, :width], both[:, width:]
    if takes:
        gate, up = gate + rest[0][...], up + rest[1][...]
        rest = rest[2:]
    if not ends:
        rest[0][...], rest[1][...] = gate, up
        return
    proj, act = rest
    hidden = (gate / (1.0 + jnp.exp(-gate)) * up).astype(BF16)
    step = dot32(hidden, proj[...])

    @pl.when(pl.program_id(0) == 0)
    def _():
        act[...] = step

    @pl.when(pl.program_id(0) > 0)
    def _():
        act[...] += step


def mlp(ids, xs, gate_w, up_w, proj_in=None, sums=()):
    slots, (rows, depth) = len(xs), xs[0].shape
    units = gate_w.shape[1]
    tile = math.gcd(units, 384)
    ends = proj_in is not None
    whole = pl.BlockSpec((rows, depth), lambda j, ids: (0, 0))
    weight = [pl.BlockSpec((depth, tile), lambda j, ids, s=s: (ids[s], j)) for s in range(slots)]
    sums_spec = pl.BlockSpec((rows, tile), lambda j, ids: (0, j))
    in_specs = [whole] * slots + weight * 2 + [sums_spec] * len(sums)
    operands = [*xs, *[gate_w] * slots, *[up_w] * slots, *sums]
    if ends:
        rank = proj_in.shape[1]
        in_specs.append(pl.BlockSpec((tile, rank), lambda j, ids: (j, 0)))
        operands.append(proj_in)
        out_shape = jax.ShapeDtypeStruct((rows, rank), F32)
        out_specs = pl.BlockSpec((rows, rank), lambda j, ids: (0, 0))
    else:
        out_shape = (jax.ShapeDtypeStruct((rows, units), F32),) * 2
        out_specs = (sums_spec,) * 2
    flops = 4 * rows * depth * slots * units
    moved = 4 * depth * slots * units + 8 * rows * units * (len(sums) // 2 + (not ends)) + 2 * rows * depth * slots
    return pl.pallas_call(
        functools.partial(mlp_kernel, slots, bool(sums), ends),
        grid_spec=pltpu.PrefetchScalarGridSpec(
            num_scalar_prefetch=1, grid=(units // tile,), in_specs=in_specs, out_specs=out_specs
        ),
        out_shape=out_shape,
        compiler_params=pltpu.CompilerParams(
            dimension_semantics=("arbitrary",), vmem_limit_bytes=56 * 2**20
        ),
        cost_estimate=pl.CostEstimate(flops=flops, bytes_accessed=moved, transcendentals=rows * units * ends),
        name=f"mlp_{slots}_{int(bool(sums))}_{int(ends)}",
    )(ids, *operands)


def hop(x, pairs):
    return lax.ppermute(x, "mp", pairs)


SIDE = [(0, 1), (1, 0), (2, 3), (3, 2)]
MIDDLE = [(1, 2), (2, 1)]
OUT = [(1, 0), (2, 3)]
IN = [(0, 1), (3, 2)]


def blocks_of(x, middle, after=None):
    if after is not None:
        x, _ = lax.optimization_barrier((x, after))
    a = hop(x, SIDE)
    b = hop(x, MIDDLE)
    c = hop(b, OUT)
    d = hop(a, MIDDLE)
    e = hop(d, OUT)
    return [x, a, jnp.where(middle, b, c), jnp.where(middle, d, e)], c


def kept_part(count, tokens, grad_part, order, first, gate_w, up_w, proj_in):
    me = lax.axis_index("mp")
    middle = (me == 1) | (me == 2)
    ids = jnp.stack([me, me ^ 1, jnp.where(middle, me ^ 3, me ^ 2), jnp.where(middle, me ^ 2, me ^ 3)]).astype(jnp.int32)
    late = max(1, round(0.4 * count / 64)) * 64
    early = count - late
    pick = order[None, :] == jnp.arange(count, dtype=jnp.int32)[:, None]
    x1 = dot32(pick[:early].astype(BF16), tokens).astype(BF16)
    x2 = dot32(pick[early:].astype(BF16), tokens).astype(BF16)
    xs1, c1 = blocks_of(x1, middle)
    xs2, _ = blocks_of(x2, middle, after=c1)

    grad = jnp.dot(pick.astype(F32), grad_part, precision=lax.Precision.HIGHEST)
    grad = grad + hop(grad, IN)
    grad = grad + hop(grad, MIDDLE)
    grad = jnp.where(middle, grad, hop(grad, OUT))

    act1 = mlp(ids, xs1, gate_w, up_w, proj_in)
    sums = mlp(ids[:3], xs2[:3], gate_w, up_w)
    act2 = mlp(ids[3:], xs2[3:], gate_w, up_w, proj_in, sums)
    act = jnp.concatenate([act1, act2], axis=0)
    row = jnp.arange(count, dtype=jnp.int32)[:, None]
    split = jnp.stack([jnp.where(row < first, grad, 0.0), jnp.where(row < first, 0.0, grad)])
    return jnp.einsum("rti,tj->rij", split, act, precision=lax.Precision.HIGHEST)


def sketch_on_line(tokens, grad_out, gate_w, up_w, proj_in, proj_out, keep):
    seq_len = keep.shape[1]
    upto = jnp.triu(jnp.ones((seq_len, seq_len), BF16))
    place = dot32(keep.astype(BF16), upto).astype(jnp.int32)
    first, count = jnp.sum(keep[0].astype(jnp.int32)), jnp.sum(keep.astype(jnp.int32))
    before = jnp.stack([jnp.zeros_like(first), first])
    order = jnp.where(keep, place - 1 + before[:, None], -1).reshape(-1)
    grad_part = dot32(grad_out, proj_out)
    most = order.shape[0]
    cases = [
        functools.partial(kept_part, rows) for rows in range(ROWS, most + 1, ROWS)
    ]
    at = jnp.clip((count - 1) // ROWS, 0, len(cases) - 1)
    part = lax.switch(at, cases, tokens, grad_part, order, first, gate_w, up_w, proj_in)
    others = [hop(part, [(s, s ^ k) for s in range(LINE)]) for k in (1, 2, 3)]
    return part + others[0] + others[1] + others[2]


def sketch_in_general(tokens, grad_out, gate_w, up_w, proj_in, proj_out, keep):
    roll_count, seq_len = keep.shape
    rank = proj_in.shape[1]
    pieces = lax.all_gather(tokens, "mp", axis=1, tiled=True)
    hidden = (jax.nn.silu(dot32(pieces, gate_w)) * dot32(pieces, up_w)).astype(BF16)
    stacked = jnp.concatenate([dot32(grad_out, proj_out), dot32(hidden, proj_in)], axis=1)
    summed = lax.psum(stacked, "mp").reshape(roll_count, seq_len, 2 * rank)
    weighted = summed[:, :, :rank] * keep.astype(F32)[:, :, None]
    return jnp.einsum("rti,rtj->rij", weighted, summed[:, :, rank:], precision=lax.Precision.HIGHEST)


def local(planes, tokens, grad_out, gate_w, up_w, proj_in, proj_out, lengths, loss_mask, queries):
    roll_count, seq_len = loss_mask.shape
    all_queries = lax.all_gather(queries, "dp", axis=1, tiled=True)
    positions = jnp.arange(seq_len, dtype=jnp.int32)
    keep = (positions[None, :] < lengths[:, None]) & (loss_mask == 1)
    fits = planes == LINE and roll_count == 2 and gate_w.shape[1] % 128 == 0
    fits = fits and tokens.shape[1] % 128 == 0 and tokens.shape[0] % ROWS == 0
    form = sketch_on_line if fits else sketch_in_general
    sketch_sum = form(tokens, grad_out, gate_w, up_w, proj_in, proj_out, keep)
    norm_factor = 1.0 / jnp.sqrt(jnp.float32(seq_len))
    sketch = (sketch_sum.reshape(roll_count, -1) * norm_factor).astype(BF16)
    return jnp.einsum("rk,qk->rq", sketch, all_queries, preferred_element_type=F32)


def solution(mesh):
    placed = (
        P(("groups", "dp"), "mp"),
        P(("groups", "dp"), "mp"),
        P(None, "mp"),
        P(None, "mp"),
        P("mp", None),
        P("mp", None),
        P(("groups", "dp")),
        P(("groups", "dp"), None),
        P("mp", "dp"),
    )
    return jax.shard_map(
        functools.partial(local, mesh.shape["mp"]),
        mesh=mesh, in_specs=placed, out_specs=P(("groups", "dp"), "mp"), check_vma=False,
    )
```

```python
import functools

import jax
import jax.numpy as jnp
from jax import lax
from jax.experimental import pallas as pl
from jax.experimental.pallas import tpu as pltpu
from jax.sharding import PartitionSpec as P

BF16, F32, I32 = jnp.bfloat16, jnp.float32, jnp.int32
FIRST = 256
CAP = 192
TEAM = 4
PLANES = 4
MIB = 2**20


def dot32(a, b):
    return jnp.dot(a, b, preferred_element_type=F32)


def dot32_t(a, b):
    return lax.dot_general(a, b, (((1,), (1,)), ((), ())), preferred_element_type=F32)


def iota(shape, axis):
    return lax.broadcasted_iota(I32, shape, axis)


def ones_where(cond):
    return jnp.where(cond, 1.0, 0.0).astype(BF16)


def dealt(rest, most):
    keep = [jnp.minimum(m, most) for m in rest]
    spare_at, room_at, a, b = [], [], 0, 0
    for m, k in zip(rest, keep):
        spare_at.append(a)
        room_at.append(b)
        a, b = a + (m - k), b + (most - k)
    start, moved = {}, {}
    for s in range(TEAM):
        for t in range(TEAM):
            if s != t:
                low = jnp.maximum(spare_at[s], room_at[t])
                high = jnp.minimum(spare_at[s] + rest[s] - keep[s], room_at[t] + most - keep[t])
                start[s, t], moved[s, t] = low, jnp.maximum(high - low, 0)
    return keep, spare_at, room_at, start, moved


def plan(table):
    rest = [jnp.maximum(table[2 * s + 1] - FIRST, 0) for s in range(TEAM)]
    even = (rest[0] + rest[1] + rest[2] + rest[3] + (TEAM - 1)) // TEAM
    moved = dealt(rest, even)[4]
    largest = functools.reduce(jnp.maximum, moved.values())
    most = jnp.where(largest <= CAP, even, functools.reduce(jnp.maximum, rest))
    keep, spare_at, room_at, start, moved = dealt(rest, most)
    lots = {}
    for s in range(TEAM):
        lots[s, s] = (FIRST, 0, keep[s])
        for t in range(TEAM):
            if s != t:
                rank = FIRST + keep[s] + start[s, t] - spare_at[s]
                lots[s, t] = (rank, keep[t] + start[s, t] - room_at[t], moved[s, t])
    return most, lots


def chosen(lots, pairs):
    out = [0, 0, 0]
    for cond, pair in pairs:
        out = [jnp.where(cond, new, old) for new, old in zip(lots[pair], out)]
    return out


def first_kernel(team_at, lengths, loss_mask, tokens, order, table, rows):
    seq_len = loss_mask.shape[1]
    limit = jnp.where(iota(loss_mask.shape, 0) == 0, lengths[0], lengths[1])
    keep = (iota(loss_mask.shape, 1) < limit) & (loss_mask[...] == 1)
    upto = ones_where(iota((seq_len, seq_len), 0) <= iota((seq_len, seq_len), 1))
    kept = jnp.where(keep, 1.0, 0.0)
    place = dot32(kept.astype(BF16), upto)
    before = jnp.sum(kept[0:1], axis=1, keepdims=True)
    total = before + jnp.sum(kept[1:2], axis=1, keepdims=True)
    place = place - 1.0 + jnp.where(iota(place.shape, 0) == 0, 0.0, before)
    ranks = jnp.where(keep, place, -1.0).astype(I32)
    order[...] = ranks
    cell = jnp.where(iota(table.shape, 1) == 0, before, total)
    table[...] = jnp.where(iota(table.shape, 0) == team_at[0], cell, 0.0)
    at = iota((FIRST, seq_len), 0)
    found = dot32(ones_where(ranks[0:1] == at), tokens[:seq_len])
    found += dot32(ones_where(ranks[1:2] == at), tokens[seq_len:])
    rows[...] = found.astype(BF16)


def deal_kernel(table, team_at, order, tokens, grads, size, *hands):
    me, seq_len = team_at[0], order.shape[1]
    most, lots = plan(table)
    size[0] = most
    depth = tokens.shape[1]
    at = iota((CAP, seq_len), 0)
    for k, hand in zip(range(1, TEAM), hands):
        rank, _, number = chosen(lots, [(me == s, (s, s ^ k)) for s in range(TEAM)])
        valid = at < number
        for side in range(2):
            pick = ones_where((order[side : side + 1] - rank == at) & valid)
            span = slice(side * seq_len, (side + 1) * seq_len)
            found, grad = dot32(pick, tokens[span]), dot32_t(pick, grads[:, span])
            if side == 0:
                hand[:, :depth], hand[:, depth:] = found.astype(BF16), grad.astype(BF16)
            else:
                hand[:, :depth] += found.astype(BF16)
                hand[:, depth:] += grad.astype(BF16)


def place_kernel(table, team_at, order, tokens, grads, hand1, hand2, hand3, rows, grad1, grad2):
    me, seq_len = team_at[0], order.shape[1]
    _, lots = plan(table)
    depth, rank_size = tokens.shape[1], grad1.shape[1]
    kept = chosen(lots, [(me == s, (s, s)) for s in range(TEAM)])[2]
    step = FIRST
    at = iota((step, seq_len), 0)

    def summed(parts):
        return parts[:, :rank_size] + parts[:, rank_size:]

    first = dot32_t(ones_where(order[0:1] == at), grads[:, :seq_len])
    grad1[...] = summed(first + dot32_t(ones_where(order[1:2] == at), grads[:, seq_len:]))
    for base in range(0, rows.shape[0], step):
        block = slice(base, base + step)
        found, grad = 0.0, 0.0
        for side in range(2):
            pick = ones_where((order[side : side + 1] - (FIRST + base) == at) & (at + base < kept))
            span = slice(side * seq_len, (side + 1) * seq_len)
            found += dot32(pick, tokens[span])
            grad += dot32_t(pick, grads[:, span])
        for k, hand in ((1, hand1), (2, hand2), (3, hand3)):
            _, row, number = chosen(lots, [(me == t, (t ^ k, t)) for t in range(TEAM)])
            source = iota((step, CAP), 1)
            put = ones_where((iota((step, CAP), 0) + base - row == source) & (source < number))
            found += dot32(put, hand[:, :depth])
            grad += dot32(put, hand[:, depth:])
        rows[block] = found.astype(BF16)
        grad2[block] = summed(grad)


def mlp_kernel(units, x, gate_w, up_w, proj, act):
    at = pl.program_id(0)
    gate, up = dot32(x[...], gate_w[...]), dot32(x[...], up_w[...])
    hidden = gate / (1.0 + jnp.exp(-gate)) * up
    if units % gate.shape[1]:
        hidden = jnp.where(iota(hidden.shape, 1) + at * gate.shape[1] < units, hidden, 0.0)
    part = dot32(hidden.astype(BF16), proj[...])

    @pl.when(at == 0)
    def _():
        act[...] = part

    @pl.when(at > 0)
    def _():
        act[...] += part


def sketch_kernel(table, team_at, grads, act1, act2, out):
    me = team_at[0]
    _, lots = plan(table)
    lane = iota((1, grads.shape[1]), 1)
    parts = []
    for s in range(TEAM):
        rank, row, number = chosen(lots, [(me == t, (s, t)) for t in range(TEAM)])
        row = row + FIRST
        edge = jnp.clip(row + table[2 * s] - rank, row, row + number)
        own = (me == s) & (lane < FIRST)
        cut = table[2 * s]
        for low, high, early in ((row, edge, lane < cut), (edge, row + number, lane >= cut)):
            mine = ((lane >= low) & (lane < high)) | (own & early)
            parts.append(grads[...] * jnp.where(mine, 1.0, 0.0))
    act = jnp.concatenate([act1[...], act2[...]], axis=0)
    out[...] = jnp.dot(
        jnp.concatenate(parts, axis=0), act, precision=lax.Precision.HIGHEST, preferred_element_type=F32
    )


VMEM = pl.BlockSpec(memory_space=pltpu.VMEM)
SMEM = pl.BlockSpec(memory_space=pltpu.SMEM)


def call(kernel, name, specs, out_shape, out_specs, *args):
    return pl.pallas_call(
        kernel, out_shape=out_shape, in_specs=specs, out_specs=out_specs, name=name,
        compiler_params=pltpu.CompilerParams(vmem_limit_bytes=40 * MIB),
    )(*args)


def mlp(x, gate_w, up_w, proj_in):
    rows, depth = x.shape
    units, tile, rank = gate_w.shape[1], 256, proj_in.shape[1]
    weight = pl.BlockSpec((depth, tile), lambda j: (0, j))
    return pl.pallas_call(
        functools.partial(mlp_kernel, units),
        grid=(proj_in.shape[0] // tile,),
        in_specs=[
            pl.BlockSpec((rows, depth), lambda j: (0, 0)), weight, weight,
            pl.BlockSpec((tile, rank), lambda j: (j, 0)),
        ],
        out_specs=pl.BlockSpec((rows, rank), lambda j: (0, 0)),
        out_shape=jax.ShapeDtypeStruct((rows, rank), F32),
        compiler_params=pltpu.CompilerParams(
            dimension_semantics=("arbitrary",), vmem_limit_bytes=48 * MIB
        ),
        cost_estimate=pl.CostEstimate(
            flops=4 * rows * depth * units, bytes_accessed=4 * depth * units, transcendentals=rows * units
        ),
        name="mlp",
    )(x, gate_w, up_w, proj_in)


def gathered(x):
    return lax.all_gather(x, "mp", axis=1, tiled=True)


def rest_case(size, table, team_at, x1, rows, grad1, grad2, gate_w, up_w, proj_in):
    x2 = gathered(rows[:size])
    grads = lax.psum(jnp.concatenate([grad1, grad2[:size]], axis=0).T, "mp")
    act1 = mlp(x1, gate_w, up_w, proj_in)
    act2 = mlp(x2, gate_w, up_w, proj_in)
    out_shape = jax.ShapeDtypeStruct((2 * TEAM * grad1.shape[1], act1.shape[1]), F32)
    return call(sketch_kernel, "sketch", [SMEM] * 2 + [VMEM] * 3, out_shape, VMEM, table, team_at, grads, act1, act2)


def swap(x, axis, k, size=4):
    return lax.ppermute(x, axis, [(s, s ^ k) for s in range(size)])


def sketch_of_kept(tokens, grad_out, gate_w, up_w, proj_in, proj_out, lengths, loss_mask, all_queries):
    most, depth = tokens.shape
    rank = proj_in.shape[1]
    team_at = lax.axis_index("dp").astype(I32).reshape(1)
    order, cells, x1 = call(
        first_kernel, "first", [SMEM] * 2 + [VMEM] * 2,
        (
            jax.ShapeDtypeStruct(loss_mask.shape, I32),
            jax.ShapeDtypeStruct((8, 128), F32),
            jax.ShapeDtypeStruct((FIRST, depth), BF16),
        ),
        (VMEM,) * 3, team_at, lengths, loss_mask, tokens,
    )
    x1 = gathered(x1)
    cells = cells + swap(cells, "dp", 1) + swap(cells, "dp", 2) + swap(cells, "dp", 3)
    table = cells[:TEAM, :2].astype(I32).reshape(-1)
    grad_part = lax.dot_general(proj_out, grad_out, (((0,), (1,)), ((), ())), preferred_element_type=F32)
    high = grad_part.astype(BF16)
    grads = jnp.concatenate([high, (grad_part - high.astype(F32)).astype(BF16)], axis=0)
    hand = jax.ShapeDtypeStruct((CAP, depth + 2 * rank), BF16)
    size, *hands = call(
        deal_kernel, "deal", [SMEM] * 2 + [VMEM] * 3, (jax.ShapeDtypeStruct((1,), I32),) + (hand,) * 3,
        (SMEM,) + (VMEM,) * 3, table, team_at, order, tokens, grads,
    )
    hands = [swap(hand, "dp", k) for k, hand in zip((1, 2, 3), hands)]
    rows, grad1, grad2 = call(
        place_kernel, "place", [SMEM] * 2 + [VMEM] * 6,
        (
            jax.ShapeDtypeStruct((most - FIRST, depth), BF16),
            jax.ShapeDtypeStruct((FIRST, rank), F32),
            jax.ShapeDtypeStruct((most - FIRST, rank), F32),
        ),
        (VMEM,) * 3, table, team_at, order, tokens, grads, *hands,
    )
    rows, all_queries = lax.optimization_barrier((rows, all_queries))
    sizes = sorted({s for s in (64, 128, 192, 256, 320, 384, 512) if s < most - FIRST} | {most - FIRST})
    case = sum((size[0] > s).astype(I32) for s in sizes[:-1])
    padded = jnp.pad(proj_in, ((0, -proj_in.shape[0] % 256), (0, 0)))
    parts = lax.switch(
        case, [functools.partial(rest_case, s) for s in sizes],
        table, team_at, x1, rows, grad1, grad2, gate_w, up_w, padded,
    )
    parts = parts.reshape(TEAM, 2 * rank, rank)
    me = team_at[0]
    part = lax.dynamic_index_in_dim(parts, me, 0, False)
    for k in (1, 2, 3):
        part = part + swap(lax.dynamic_index_in_dim(parts, me ^ k, 0, False), "dp", k)
    return part + swap(part, "mp", 1) + swap(part, "mp", 2) + swap(part, "mp", 3), all_queries


def sketch_in_general(tokens, grad_out, gate_w, up_w, proj_in, proj_out, lengths, loss_mask, all_queries):
    roll_count, seq_len = loss_mask.shape
    rank = proj_in.shape[1]
    keep = (jnp.arange(seq_len, dtype=I32)[None, :] < lengths[:, None]) & (loss_mask == 1)
    pieces = gathered(tokens)
    hidden = (jax.nn.silu(dot32(pieces, gate_w)) * dot32(pieces, up_w)).astype(BF16)
    stacked = jnp.concatenate([dot32(grad_out, proj_out), dot32(hidden, proj_in)], axis=1)
    summed = lax.psum(stacked, "mp").reshape(roll_count, seq_len, 2 * rank)
    weighted = summed[:, :, :rank] * keep.astype(F32)[:, :, None]
    sums = jnp.einsum("rti,rtj->rij", weighted, summed[:, :, rank:], precision=lax.Precision.HIGHEST)
    return sums, all_queries


def local(team, planes, tokens, grad_out, gate_w, up_w, proj_in, proj_out, lengths, loss_mask, queries):
    roll_count, seq_len = loss_mask.shape
    all_queries = lax.all_gather(queries, "dp", axis=1, tiled=True)
    fits = team == TEAM and planes == PLANES and roll_count == 2 and seq_len % 256 == 0
    fits = fits and tokens.shape[1] % 128 == 0 and gate_w.shape[1] % 128 == 0 and proj_in.shape[1] == 64
    form = sketch_of_kept if fits else sketch_in_general
    sketch_sum, all_queries = form(
        tokens, grad_out, gate_w, up_w, proj_in, proj_out, lengths, loss_mask, all_queries
    )
    norm_factor = 1.0 / jnp.sqrt(jnp.float32(seq_len))
    sketch = (sketch_sum.reshape(roll_count, -1) * norm_factor).astype(BF16)
    return jnp.einsum("rk,qk->rq", sketch, all_queries, preferred_element_type=F32)


def solution(mesh):
    placed = (
        P(("groups", "dp"), "mp"),
        P(("groups", "dp"), "mp"),
        P(None, "mp"),
        P(None, "mp"),
        P("mp", None),
        P("mp", None),
        P(("groups", "dp")),
        P(("groups", "dp"), None),
        P("mp", "dp"),
    )
    return jax.shard_map(
        functools.partial(local, mesh.shape["dp"], mesh.shape["mp"]),
        mesh=mesh, in_specs=placed, out_specs=P(("groups", "dp"), "mp"), check_vma=False,
    )
```

```python
import functools

import jax
import jax.numpy as jnp
from jax import lax
from jax.experimental import pallas as pl
from jax.experimental.pallas import tpu as pltpu
from jax.sharding import PartitionSpec as P

BF16, F32, I32 = jnp.bfloat16, jnp.float32, jnp.int32
FIRST = 256
CAP = 192
TEAM = 4
PLANES = 4
MIB = 2**20


def dot32(a, b):
    return jnp.dot(a, b, preferred_element_type=F32)


def dot32_t(a, b):
    return lax.dot_general(a, b, (((1,), (1,)), ((), ())), preferred_element_type=F32)


def iota(shape, axis):
    return lax.broadcasted_iota(I32, shape, axis)


def ones_where(cond):
    return jnp.where(cond, 1.0, 0.0).astype(BF16)


def dealt(rest, most):
    keep = [jnp.minimum(m, most) for m in rest]
    spare_at, room_at, a, b = [], [], 0, 0
    for m, k in zip(rest, keep):
        spare_at.append(a)
        room_at.append(b)
        a, b = a + (m - k), b + (most - k)
    start, moved = {}, {}
    for s in range(TEAM):
        for t in range(TEAM):
            if s != t:
                low = jnp.maximum(spare_at[s], room_at[t])
                high = jnp.minimum(spare_at[s] + rest[s] - keep[s], room_at[t] + most - keep[t])
                start[s, t], moved[s, t] = low, jnp.maximum(high - low, 0)
    return keep, spare_at, room_at, start, moved


def plan(table):
    rest = [jnp.maximum(table[2 * s + 1] - FIRST, 0) for s in range(TEAM)]
    even = (rest[0] + rest[1] + rest[2] + rest[3] + (TEAM - 1)) // TEAM
    most = functools.reduce(jnp.maximum, rest)
    for tried in ((3 * most + even) // 4, (most + even) // 2, even):
        largest = functools.reduce(jnp.maximum, dealt(rest, tried)[4].values())
        most = jnp.where(largest <= CAP, tried, most)
    keep, spare_at, room_at, start, moved = dealt(rest, most)
    lots = {}
    for s in range(TEAM):
        lots[s, s] = (FIRST, 0, keep[s])
        for t in range(TEAM):
            if s != t:
                rank = FIRST + keep[s] + start[s, t] - spare_at[s]
                lots[s, t] = (rank, keep[t] + start[s, t] - room_at[t], moved[s, t])
    return most, lots


def chosen(lots, pairs):
    out = [0, 0, 0]
    for cond, pair in pairs:
        out = [jnp.where(cond, new, old) for new, old in zip(lots[pair], out)]
    return out


def first_kernel(team_at, lengths, loss_mask, tokens, order, table, rows):
    seq_len = loss_mask.shape[1]
    limit = jnp.where(iota(loss_mask.shape, 0) == 0, lengths[0], lengths[1])
    keep = (iota(loss_mask.shape, 1) < limit) & (loss_mask[...] == 1)
    upto = ones_where(iota((seq_len, seq_len), 0) <= iota((seq_len, seq_len), 1))
    kept = jnp.where(keep, 1.0, 0.0)
    place = dot32(kept.astype(BF16), upto)
    before = jnp.sum(kept[0:1], axis=1, keepdims=True)
    total = before + jnp.sum(kept[1:2], axis=1, keepdims=True)
    place = place - 1.0 + jnp.where(iota(place.shape, 0) == 0, 0.0, before)
    ranks = jnp.where(keep, place, -1.0).astype(I32)
    order[...] = ranks
    cell = jnp.where(iota(table.shape, 1) == 0, before, total)
    table[...] = jnp.where(iota(table.shape, 0) == team_at[0], cell, 0.0)
    at = iota((FIRST, seq_len), 0)
    found = dot32(ones_where(ranks[0:1] == at), tokens[:seq_len])
    found += dot32(ones_where(ranks[1:2] == at), tokens[seq_len:])
    rows[...] = found.astype(BF16)


def deal_kernel(table, team_at, order, tokens, grads, lots_to_me, *hands):
    me, seq_len = team_at[0], order.shape[1]
    most, lots = plan(table)
    lots_to_me[3 * TEAM] = most
    for s in range(TEAM):
        for i, value in enumerate(chosen(lots, [(me == t, (s, t)) for t in range(TEAM)])):
            lots_to_me[3 * s + i] = value
    depth = tokens.shape[1]
    at = iota((CAP, seq_len), 0)
    for k, hand in zip(range(1, TEAM), hands):
        rank, _, number = chosen(lots, [(me == s, (s, s ^ k)) for s in range(TEAM)])
        valid = at < number
        for side in range(2):
            pick = ones_where((order[side : side + 1] - rank == at) & valid)
            span = slice(side * seq_len, (side + 1) * seq_len)
            found, grad = dot32(pick, tokens[span]), dot32_t(pick, grads[:, span])
            if side == 0:
                hand[:, :depth], hand[:, depth:] = found.astype(BF16), grad.astype(BF16)
            else:
                hand[:, :depth] += found.astype(BF16)
                hand[:, depth:] += grad.astype(BF16)


def place_kernel(lots_to_me, team_at, order, tokens, grads, hand1, hand2, hand3, rows, grad1, grad2):
    me, seq_len = team_at[0], order.shape[1]
    depth, rank_size = tokens.shape[1], grad1.shape[1]
    kept = lots_to_me[3 * me + 2]
    step = FIRST
    at = iota((step, seq_len), 0)

    def summed(parts):
        return parts[:, :rank_size] + parts[:, rank_size:]

    first = dot32_t(ones_where(order[0:1] == at), grads[:, :seq_len])
    grad1[...] = summed(first + dot32_t(ones_where(order[1:2] == at), grads[:, seq_len:]))
    for base in range(0, rows.shape[0], step):
        block = slice(base, base + step)
        found, grad = 0.0, 0.0
        for side in range(2):
            pick = ones_where((order[side : side + 1] - (FIRST + base) == at) & (at + base < kept))
            span = slice(side * seq_len, (side + 1) * seq_len)
            found += dot32(pick, tokens[span])
            grad += dot32_t(pick, grads[:, span])
        for k, hand in ((1, hand1), (2, hand2), (3, hand3)):
            row, number = lots_to_me[3 * (me ^ k) + 1], lots_to_me[3 * (me ^ k) + 2]
            source = iota((step, CAP), 1)
            put = ones_where((iota((step, CAP), 0) + base - row == source) & (source < number))
            found += dot32(put, hand[:, :depth])
            grad += dot32(put, hand[:, depth:])
        rows[block] = found.astype(BF16)
        grad2[block] = summed(grad)


def project(units, gate, up, proj, act):
    at = pl.program_id(0)
    hidden = gate / (1.0 + jnp.exp(-gate)) * up
    if units % gate.shape[1]:
        hidden = jnp.where(iota(hidden.shape, 1) + at * gate.shape[1] < units, hidden, 0.0)
    part = dot32(hidden.astype(BF16), proj[...])

    @pl.when(at == 0)
    def _():
        act[...] = part

    @pl.when(at > 0)
    def _():
        act[...] += part


def mlp_kernel(units, x, gate_w, up_w, proj, act):
    project(units, dot32(x[...], gate_w[...]), dot32(x[...], up_w[...]), proj, act)


def early_kernel(ids, x, x1, x3, gate, gate1, gate3, up, up1, up3, gate_sum, up_sum):
    del ids
    gate_sum[...] = dot32(x[...], gate[...]) + dot32(x1[...], gate1[...]) + dot32(x3[...], gate3[...])
    up_sum[...] = dot32(x[...], up[...]) + dot32(x1[...], up1[...]) + dot32(x3[...], up3[...])


def late_kernel(units, ids, at_side, at_middle, gate_w, up_w, gate_sum, up_sum, proj, act):
    middle = (ids[0] == 1) | (ids[0] == 2)
    x = jnp.where(middle, at_middle[...], at_side[...])
    gate, up = gate_sum[...] + dot32(x, gate_w[...]), up_sum[...] + dot32(x, up_w[...])
    project(units, gate, up, proj, act)


def sketch_kernel(table, lots_to_me, team_at, grads, act1, act2, out):
    me = team_at[0]
    lane = iota((1, grads.shape[1]), 1)
    parts = []
    for s in range(TEAM):
        rank, row, number = lots_to_me[3 * s], lots_to_me[3 * s + 1] + FIRST, lots_to_me[3 * s + 2]
        edge = jnp.clip(row + table[2 * s] - rank, row, row + number)
        own = (me == s) & (lane < FIRST)
        cut = table[2 * s]
        for low, high, early in ((row, edge, lane < cut), (edge, row + number, lane >= cut)):
            mine = ((lane >= low) & (lane < high)) | (own & early)
            parts.append(grads[...] * jnp.where(mine, 1.0, 0.0))
    act = jnp.concatenate([act1[...], act2[...]], axis=0)
    out[...] = jnp.dot(
        jnp.concatenate(parts, axis=0), act, precision=lax.Precision.HIGHEST, preferred_element_type=F32
    )


VMEM = pl.BlockSpec(memory_space=pltpu.VMEM)
SMEM = pl.BlockSpec(memory_space=pltpu.SMEM)


def call(kernel, name, specs, out_shape, out_specs, *args):
    return pl.pallas_call(
        kernel, out_shape=out_shape, in_specs=specs, out_specs=out_specs, name=name,
        compiler_params=pltpu.CompilerParams(vmem_limit_bytes=40 * MIB),
    )(*args)


def mlp(x, gate_w, up_w, proj_in):
    rows, depth = x.shape
    units, tile, rank = gate_w.shape[1], 256, proj_in.shape[1]
    weight = pl.BlockSpec((depth, tile), lambda j: (0, j))
    return pl.pallas_call(
        functools.partial(mlp_kernel, units),
        grid=(proj_in.shape[0] // tile,),
        in_specs=[
            pl.BlockSpec((rows, depth), lambda j: (0, 0)), weight, weight,
            pl.BlockSpec((tile, rank), lambda j: (j, 0)),
        ],
        out_specs=pl.BlockSpec((rows, rank), lambda j: (0, 0)),
        out_shape=jax.ShapeDtypeStruct((rows, rank), F32),
        compiler_params=pltpu.CompilerParams(
            dimension_semantics=("arbitrary",), vmem_limit_bytes=48 * MIB
        ),
        cost_estimate=pl.CostEstimate(
            flops=4 * rows * depth * units, bytes_accessed=4 * depth * units, transcendentals=rows * units
        ),
        name="mlp",
    )(x, gate_w, up_w, proj_in)


def grid_params():
    return pltpu.CompilerParams(dimension_semantics=("arbitrary",), vmem_limit_bytes=48 * MIB)


def parted_specs(rows, depth, tile, slots):
    whole = pl.BlockSpec((rows, depth), lambda j, ids: (0, 0))
    weight = [pl.BlockSpec((depth, tile), lambda j, ids, s=s: (ids[s], j)) for s in slots]
    return whole, weight, pl.BlockSpec((rows, tile), lambda j, ids: (0, j))


def early(ids, xs, gate_w, up_w, tile=256):
    (rows, depth), units = xs[0].shape, gate_w.shape[1]
    steps = -(-units // tile)
    whole, weight, sums = parted_specs(rows, depth, tile, (0, 1, 3))
    return pl.pallas_call(
        early_kernel,
        grid_spec=pltpu.PrefetchScalarGridSpec(
            num_scalar_prefetch=1, grid=(steps,), in_specs=[whole] * 3 + weight * 2, out_specs=(sums,) * 2
        ),
        out_shape=(jax.ShapeDtypeStruct((rows, steps * tile), F32),) * 2,
        compiler_params=grid_params(),
        cost_estimate=pl.CostEstimate(
            flops=12 * rows * depth * units, bytes_accessed=12 * depth * units, transcendentals=0
        ),
        name="early",
    )(ids, *xs, *[gate_w] * 3, *[up_w] * 3)


def late(ids, at_side, at_middle, sums, gate_w, up_w, proj_in, tile=256):
    (rows, depth), units, rank = at_side.shape, gate_w.shape[1], proj_in.shape[1]
    whole, weight, sums_spec = parted_specs(rows, depth, tile, (2,))
    return pl.pallas_call(
        functools.partial(late_kernel, units),
        grid_spec=pltpu.PrefetchScalarGridSpec(
            num_scalar_prefetch=1, grid=(proj_in.shape[0] // tile,),
            in_specs=[whole] * 2 + weight * 2 + [sums_spec] * 2 + [pl.BlockSpec((tile, rank), lambda j, ids: (j, 0))],
            out_specs=pl.BlockSpec((rows, rank), lambda j, ids: (0, 0)),
        ),
        out_shape=jax.ShapeDtypeStruct((rows, rank), F32),
        compiler_params=grid_params(),
        cost_estimate=pl.CostEstimate(
            flops=4 * rows * depth * units, bytes_accessed=4 * depth * units, transcendentals=rows * units
        ),
        name="late",
    )(ids, at_side, at_middle, gate_w, up_w, *sums, proj_in)


IN, MIDDLE, OUT = [(0, 1), (3, 2)], [(1, 2), (2, 1)], [(1, 0), (2, 3)]


def gathered(x):
    return lax.all_gather(x, "mp", axis=1, tiled=True)


def hop(x, pairs):
    return lax.ppermute(x, "mp", pairs)


def after(x, *others):
    return lax.optimization_barrier((x, *others))[0]


def rest_case(size, table, lots, team_at, ids, x1, rows, grad1, grad2, gate_w, up_w, proj_in):
    x = rows[:size]
    side, far = swap(x, "mp", 1), swap(x, "mp", 3)
    grads = jnp.concatenate([grad1, grad2[:size]], axis=0).T
    from_end = hop(grads, IN)
    act1 = mlp(x1, gate_w, up_w, proj_in)
    side, far, act1, from_end = lax.optimization_barrier((side, far, act1, from_end))
    at_side, at_middle = hop(far, OUT), hop(side, MIDDLE)
    grads = grads + from_end
    half = hop(grads, MIDDLE)
    sums = early(ids, (x, side, far), gate_w, up_w)
    sums, at_side, at_middle, half = lax.optimization_barrier((sums, at_side, at_middle, half))
    grads = grads + half
    total = hop(grads, OUT)
    act2 = late(ids, at_side, at_middle, sums, gate_w, up_w, proj_in)
    grads = jnp.where((ids[0] == 1) | (ids[0] == 2), grads, total)
    out_shape = jax.ShapeDtypeStruct((2 * TEAM * grad1.shape[1], act1.shape[1]), F32)
    return call(
        sketch_kernel, "sketch", [SMEM] * 3 + [VMEM] * 3, out_shape, VMEM,
        table, lots, team_at, grads, act1, act2,
    )


def swap(x, axis, k, size=4):
    return lax.ppermute(x, axis, [(s, s ^ k) for s in range(size)])


def sketch_of_kept(tokens, grad_out, gate_w, up_w, proj_in, proj_out, lengths, loss_mask, all_queries):
    most, depth = tokens.shape
    rank = proj_in.shape[1]
    team_at = lax.axis_index("dp").astype(I32).reshape(1)
    order, cells, x1 = call(
        first_kernel, "first", [SMEM] * 2 + [VMEM] * 2,
        (
            jax.ShapeDtypeStruct(loss_mask.shape, I32),
            jax.ShapeDtypeStruct((8, 128), F32),
            jax.ShapeDtypeStruct((FIRST, depth), BF16),
        ),
        (VMEM,) * 3, team_at, lengths, loss_mask, tokens,
    )
    x1 = gathered(x1)
    cells = cells + swap(cells, "dp", 1) + swap(cells, "dp", 2) + swap(cells, "dp", 3)
    table = cells[:TEAM, :2].astype(I32).reshape(-1)
    grad_part = lax.dot_general(proj_out, grad_out, (((0,), (1,)), ((), ())), preferred_element_type=F32)
    high = lax.reduce_precision(grad_part, 8, 7)
    grads = jnp.concatenate([high.astype(BF16), (grad_part - high).astype(BF16)], axis=0)
    hand = jax.ShapeDtypeStruct((CAP, depth + 2 * rank), BF16)
    lots, *hands = call(
        deal_kernel, "deal", [SMEM] * 2 + [VMEM] * 3,
        (jax.ShapeDtypeStruct((3 * TEAM + 1,), I32),) + (hand,) * 3,
        (SMEM,) + (VMEM,) * 3, table, team_at, order, tokens, grads,
    )
    hands = [swap(hand, "dp", k) for k, hand in zip((1, 2, 3), hands)]
    rows, grad1, grad2 = call(
        place_kernel, "place", [SMEM] * 2 + [VMEM] * 6,
        (
            jax.ShapeDtypeStruct((most - FIRST, depth), BF16),
            jax.ShapeDtypeStruct((FIRST, rank), F32),
            jax.ShapeDtypeStruct((most - FIRST, rank), F32),
        ),
        (VMEM,) * 3, lots, team_at, order, tokens, grads, *hands,
    )
    rows, all_queries = lax.optimization_barrier((rows, all_queries))
    me = lax.axis_index("mp").astype(I32)
    ids = jnp.stack([me, me ^ 1, me ^ 2, me ^ 3])
    sizes = sorted({s for s in (64, 128, 192, 256, 320, 384, 512) if s < most - FIRST} | {most - FIRST})
    case = sum((lots[3 * TEAM] > s).astype(I32) for s in sizes[:-1])
    padded = jnp.pad(proj_in, ((0, -proj_in.shape[0] % 256), (0, 0)))
    parts = lax.switch(
        case, [functools.partial(rest_case, s) for s in sizes],
        table, lots, team_at, ids, x1, rows, grad1, grad2, gate_w, up_w, padded,
    )
    parts = parts.reshape(TEAM, 2 * rank, rank)
    me = team_at[0]
    part = lax.dynamic_index_in_dim(parts, me, 0, False)
    for k in (1, 2, 3):
        part = part + swap(lax.dynamic_index_in_dim(parts, me ^ k, 0, False), "dp", k)
    return part + swap(part, "mp", 1) + swap(part, "mp", 2) + swap(part, "mp", 3), all_queries


def sketch_in_general(tokens, grad_out, gate_w, up_w, proj_in, proj_out, lengths, loss_mask, all_queries):
    roll_count, seq_len = loss_mask.shape
    rank = proj_in.shape[1]
    keep = (jnp.arange(seq_len, dtype=I32)[None, :] < lengths[:, None]) & (loss_mask == 1)
    pieces = gathered(tokens)
    hidden = (jax.nn.silu(dot32(pieces, gate_w)) * dot32(pieces, up_w)).astype(BF16)
    stacked = jnp.concatenate([dot32(grad_out, proj_out), dot32(hidden, proj_in)], axis=1)
    summed = lax.psum(stacked, "mp").reshape(roll_count, seq_len, 2 * rank)
    weighted = summed[:, :, :rank] * keep.astype(F32)[:, :, None]
    sums = jnp.einsum("rti,rtj->rij", weighted, summed[:, :, rank:], precision=lax.Precision.HIGHEST)
    return sums, all_queries


def team_queries(queries):
    me = lax.axis_index("dp")
    out = jnp.zeros((TEAM,) + queries.shape, queries.dtype)
    out = lax.dynamic_update_index_in_dim(out, queries, me, 0)
    for k in (1, 2, 3):
        out = lax.dynamic_update_index_in_dim(out, swap(queries, "dp", k), me ^ k, 0)
    return out


def local(team, planes, tokens, grad_out, gate_w, up_w, proj_in, proj_out, lengths, loss_mask, queries):
    roll_count, seq_len = loss_mask.shape
    fits = team == TEAM and planes == PLANES and roll_count == 2 and seq_len % 256 == 0
    fits = fits and tokens.shape[1] % 128 == 0 and gate_w.shape[1] % 128 == 0 and proj_in.shape[1] == 64
    form = sketch_of_kept if fits else sketch_in_general
    all_queries = team_queries(queries) if fits else lax.all_gather(queries, "dp", axis=0)
    sketch_sum, all_queries = form(
        tokens, grad_out, gate_w, up_w, proj_in, proj_out, lengths, loss_mask, all_queries
    )
    norm_factor = 1.0 / jnp.sqrt(jnp.float32(seq_len))
    sketch = (sketch_sum.reshape(roll_count, team, -1) * norm_factor).astype(BF16)
    return jnp.einsum("rdk,dqk->rq", sketch, all_queries, preferred_element_type=F32)


def solution(mesh):
    placed = (
        P(("groups", "dp"), "mp"),
        P(("groups", "dp"), "mp"),
        P(None, "mp"),
        P(None, "mp"),
        P("mp", None),
        P("mp", None),
        P(("groups", "dp")),
        P(("groups", "dp"), None),
        P("mp", "dp"),
    )
    return jax.shard_map(
        functools.partial(local, mesh.shape["dp"], mesh.shape["mp"]),
        mesh=mesh, in_specs=placed, out_specs=P(("groups", "dp"), "mp"), check_vma=False,
    )
```

```python
import functools

import jax
import jax.numpy as jnp
from jax import lax
from jax.experimental import pallas as pl
from jax.experimental.pallas import tpu as pltpu
from jax.sharding import PartitionSpec as P

BF16, F32, I32 = jnp.bfloat16, jnp.float32, jnp.int32
FIRST = 256
CAP = 192
TEAM = 4
PLANES = 4
MIB = 2**20


def dot32(a, b):
    return jnp.dot(a, b, preferred_element_type=F32)


def dot32_t(a, b):
    return lax.dot_general(a, b, (((1,), (1,)), ((), ())), preferred_element_type=F32)


def iota(shape, axis):
    return lax.broadcasted_iota(I32, shape, axis)


def ones_where(cond):
    return jnp.where(cond, 1.0, 0.0).astype(BF16)


def dealt(rest, most):
    keep = [jnp.minimum(m, most) for m in rest]
    spare_at, room_at, a, b = [], [], 0, 0
    for m, k in zip(rest, keep):
        spare_at.append(a)
        room_at.append(b)
        a, b = a + (m - k), b + (most - k)
    start, moved = {}, {}
    for s in range(TEAM):
        for t in range(TEAM):
            if s != t:
                low = jnp.maximum(spare_at[s], room_at[t])
                high = jnp.minimum(spare_at[s] + rest[s] - keep[s], room_at[t] + most - keep[t])
                start[s, t], moved[s, t] = low, jnp.maximum(high - low, 0)
    return keep, spare_at, room_at, start, moved


def plan(table):
    rest = [jnp.maximum(table[2 * s + 1] - FIRST, 0) for s in range(TEAM)]
    even = (rest[0] + rest[1] + rest[2] + rest[3] + (TEAM - 1)) // TEAM
    most = functools.reduce(jnp.maximum, rest)
    for tried in ((3 * most + even) // 4, (most + even) // 2, even):
        largest = functools.reduce(jnp.maximum, dealt(rest, tried)[4].values())
        most = jnp.where(largest <= CAP, tried, most)
    keep, spare_at, room_at, start, moved = dealt(rest, most)
    lots = {}
    for s in range(TEAM):
        lots[s, s] = (FIRST, 0, keep[s])
        for t in range(TEAM):
            if s != t:
                rank = FIRST + keep[s] + start[s, t] - spare_at[s]
                lots[s, t] = (rank, keep[t] + start[s, t] - room_at[t], moved[s, t])
    return most, lots


def chosen(lots, pairs):
    out = [0, 0, 0]
    for cond, pair in pairs:
        out = [jnp.where(cond, new, old) for new, old in zip(lots[pair], out)]
    return out


def first_kernel(team_at, lengths, loss_mask, tokens, order, table, rows):
    seq_len = loss_mask.shape[1]
    limit = jnp.where(iota(loss_mask.shape, 0) == 0, lengths[0], lengths[1])
    keep = (iota(loss_mask.shape, 1) < limit) & (loss_mask[...] == 1)
    upto = ones_where(iota((seq_len, seq_len), 0) <= iota((seq_len, seq_len), 1))
    kept = jnp.where(keep, 1.0, 0.0)
    place = dot32(kept.astype(BF16), upto)
    before = jnp.sum(kept[0:1], axis=1, keepdims=True)
    total = before + jnp.sum(kept[1:2], axis=1, keepdims=True)
    place = place - 1.0 + jnp.where(iota(place.shape, 0) == 0, 0.0, before)
    ranks = jnp.where(keep, place, -1.0).astype(I32)
    order[...] = ranks
    cell = jnp.where(iota(table.shape, 1) == 0, before, total)
    table[...] = jnp.where(iota(table.shape, 0) == team_at[0], cell, 0.0)
    at = iota((FIRST, seq_len), 0)
    found = dot32(ones_where(ranks[0:1] == at), tokens[:seq_len])
    found += dot32(ones_where(ranks[1:2] == at), tokens[seq_len:])
    rows[...] = found.astype(BF16)


def deal_kernel(table, team_at, order, tokens, grads, lots_to_me, *hands):
    me, seq_len = team_at[0], order.shape[1]
    most, lots = plan(table)
    lots_to_me[3 * TEAM] = most
    for s in range(TEAM):
        for i, value in enumerate(chosen(lots, [(me == t, (s, t)) for t in range(TEAM)])):
            lots_to_me[3 * s + i] = value
    depth = tokens.shape[1]
    at = iota((CAP, seq_len), 0)
    for k, hand in zip(range(1, TEAM), hands):
        rank, _, number = chosen(lots, [(me == s, (s, s ^ k)) for s in range(TEAM)])
        valid = at < number
        for side in range(2):
            pick = ones_where((order[side : side + 1] - rank == at) & valid)
            span = slice(side * seq_len, (side + 1) * seq_len)
            found, grad = dot32(pick, tokens[span]), dot32_t(pick, grads[:, span])
            if side == 0:
                hand[:, :depth], hand[:, depth:] = found.astype(BF16), grad.astype(BF16)
            else:
                hand[:, :depth] += found.astype(BF16)
                hand[:, depth:] += grad.astype(BF16)


def place_kernel(lots_to_me, team_at, order, tokens, grads, hand1, hand2, hand3, rows, grads_here):
    me, seq_len = team_at[0], order.shape[1]
    depth, rank_size = tokens.shape[1], grads_here.shape[0]
    kept = lots_to_me[3 * me + 2]
    step = FIRST
    at = iota((step, seq_len), 0)
    for base in range(-FIRST, rows.shape[0], step):
        valid = None if base < 0 else at + base < kept
        found, grad = 0.0, 0.0
        for side in range(2):
            hit = order[side : side + 1] - (FIRST + base) == at
            pick = ones_where(hit if valid is None else hit & valid)
            span = slice(side * seq_len, (side + 1) * seq_len)
            if base >= 0:
                found += dot32(pick, tokens[span])
            grad += dot32_t(grads[:, span], pick)
        if base >= 0:
            dealt_grad = 0.0
            for k, hand in ((1, hand1), (2, hand2), (3, hand3)):
                row, number = lots_to_me[3 * (me ^ k) + 1], lots_to_me[3 * (me ^ k) + 2]
                source = iota((step, CAP), 1)
                put = ones_where((iota((step, CAP), 0) + base - row == source) & (source < number))
                found += dot32(put, hand[:, :depth])
                dealt_grad += dot32(put, hand[:, depth:])
            grad += dealt_grad.T
            rows[base : base + step] = found.astype(BF16)
        grads_here[:, FIRST + base : FIRST + base + step] = grad[:rank_size] + grad[rank_size:]


def project(units, gate, up, proj, act):
    at = pl.program_id(0)
    hidden = gate / (1.0 + jnp.exp(-gate)) * up
    if units % gate.shape[1]:
        hidden = jnp.where(iota(hidden.shape, 1) + at * gate.shape[1] < units, hidden, 0.0)
    part = dot32(hidden.astype(BF16), proj[...])

    rows = part.shape[0]

    @pl.when(at == 0)
    def _():
        act[:rows] = part

    @pl.when(at > 0)
    def _():
        act[:rows] += part


def sums_kernel(slots, ids, *refs):
    del ids
    xs, gates, ups = refs[:slots], refs[slots : 2 * slots], refs[2 * slots : 3 * slots]
    gate_sum, up_sum = refs[3 * slots :]
    gate_sum[...] = sum(dot32(x[...], w[...]) for x, w in zip(xs, gates))
    up_sum[...] = sum(dot32(x[...], w[...]) for x, w in zip(xs, ups))


def rest_kernel(units, ids, x1, x2, x3, gate1, gate2, gate3, up1, up2, up3, gate_sum, up_sum, proj, act):
    del ids
    gate = gate_sum[...] + dot32(x1[...], gate1[...]) + dot32(x2[...], gate2[...]) + dot32(x3[...], gate3[...])
    up = up_sum[...] + dot32(x1[...], up1[...]) + dot32(x2[...], up2[...]) + dot32(x3[...], up3[...])
    project(units, gate, up, proj, act)


def late_kernel(units, ids, at_side, at_middle, gate_w, up_w, gate_sum, up_sum, proj, act):
    middle = (ids[0] == 1) | (ids[0] == 2)
    x = jnp.where(middle, at_middle[...], at_side[...])
    gate, up = gate_sum[...] + dot32(x, gate_w[...]), up_sum[...] + dot32(x, up_w[...])
    project(units, gate, up, proj, act)


def sketch_kernel(table, lots_to_me, team_at, grads, act1, act2, out):
    me, size = team_at[0], lots_to_me[3 * TEAM]

    def product(grad, lane, act):
        parts = []
        for s in range(TEAM):
            rank, row, number = lots_to_me[3 * s], lots_to_me[3 * s + 1] + FIRST, lots_to_me[3 * s + 2]
            edge = jnp.clip(row + table[2 * s] - rank, row, row + number)
            own = (me == s) & (lane < FIRST)
            cut = table[2 * s]
            for low, high, early in ((row, edge, lane < cut), (edge, row + number, lane >= cut)):
                mine = ((lane >= low) & (lane < high)) | (own & early)
                parts.append(jnp.where(mine, grad, 0.0))
        return jnp.dot(
            jnp.concatenate(parts, axis=0), act, precision=lax.Precision.HIGHEST, preferred_element_type=F32
        )

    out[...] = product(grads[:, :FIRST], iota((1, FIRST), 1), act1[...])

    def step(chunk, carry):
        base = pl.multiple_of(chunk * FIRST, FIRST)
        act = act2[pl.ds(base, FIRST), :]
        act = jnp.where(iota(act.shape, 0) + base < size, act, 0.0)
        lane = iota((1, FIRST), 1) + base + FIRST
        out[...] += product(grads[:, pl.ds(base + FIRST, FIRST)], lane, act)
        return carry

    lax.fori_loop(0, (size + FIRST - 1) // FIRST, step, 0)


VMEM = pl.BlockSpec(memory_space=pltpu.VMEM)
SMEM = pl.BlockSpec(memory_space=pltpu.SMEM)


def call(kernel, name, specs, out_shape, out_specs, *args):
    return pl.pallas_call(
        kernel, out_shape=out_shape, in_specs=specs, out_specs=out_specs, name=name,
        compiler_params=pltpu.CompilerParams(vmem_limit_bytes=40 * MIB),
    )(*args)


def grid_params():
    return pltpu.CompilerParams(dimension_semantics=("arbitrary",), vmem_limit_bytes=48 * MIB)


def parted_specs(rows, depth, tile, slots):
    whole = pl.BlockSpec((rows, depth), lambda j, ids: (0, 0))
    weight = [pl.BlockSpec((depth, tile), lambda j, ids, s=s: (ids[s], j)) for s in slots]
    return whole, weight, pl.BlockSpec((rows, tile), lambda j, ids: (0, j))


def sums_of(ids, slots, xs, gate_w, up_w, tile=256):
    (rows, depth), units, count = xs[0].shape, gate_w.shape[1], len(xs)
    steps = -(-units // tile)
    whole, weight, sums = parted_specs(rows, depth, tile, slots)
    return pl.pallas_call(
        functools.partial(sums_kernel, count),
        grid_spec=pltpu.PrefetchScalarGridSpec(
            num_scalar_prefetch=1, grid=(steps,), in_specs=[whole] * count + weight * 2, out_specs=(sums,) * 2
        ),
        out_shape=(jax.ShapeDtypeStruct((rows, steps * tile), F32),) * 2,
        compiler_params=grid_params(),
        cost_estimate=pl.CostEstimate(
            flops=4 * count * rows * depth * units, bytes_accessed=4 * count * depth * units, transcendentals=0
        ),
        name="sums",
    )(ids, *xs, *[gate_w] * count, *[up_w] * count)


def projected(kernel, name, ids, slots, xs, x_specs, sums, gate_w, up_w, proj_in, rows, most, tile=256):
    depth, units, rank = gate_w.shape[0] // PLANES, gate_w.shape[1], proj_in.shape[1]
    _, weight, sums_spec = parted_specs(rows, depth, tile, slots)
    return pl.pallas_call(
        functools.partial(kernel, units),
        grid_spec=pltpu.PrefetchScalarGridSpec(
            num_scalar_prefetch=1, grid=(proj_in.shape[0] // tile,),
            in_specs=x_specs + weight * 2 + [sums_spec] * 2 + [pl.BlockSpec((tile, rank), lambda j, ids: (j, 0))],
            out_specs=pl.BlockSpec((most, rank), lambda j, ids: (0, 0)),
        ),
        out_shape=jax.ShapeDtypeStruct((most, rank), F32),
        compiler_params=grid_params(),
        cost_estimate=pl.CostEstimate(
            flops=4 * rows * depth * units * len(slots), bytes_accessed=4 * depth * units * len(slots),
            transcendentals=rows * units,
        ),
        name=name,
    )(ids, *xs, *[gate_w] * len(slots), *[up_w] * len(slots), *sums, proj_in)


IN, MIDDLE, OUT = [(0, 1), (3, 2)], [(1, 2), (2, 1)], [(1, 0), (2, 3)]


def gathered(x):
    return lax.all_gather(x, "mp", axis=1, tiled=True)


def hop(x, pairs):
    return lax.ppermute(x, "mp", pairs)


def rest_case(size, ids, x1, sums1, rows, gate_w, up_w, proj_in):
    x = rows[:size]
    side, far = swap(x, "mp", 1), swap(x, "mp", 3)
    depth = x.shape[1]
    spread = [pl.BlockSpec((FIRST, depth), lambda j, ids, s=s: (0, ids[s])) for s in (1, 2, 3)]
    act1 = projected(
        rest_kernel, "rest", ids, (1, 2, 3), [x1] * 3, spread, sums1, gate_w, up_w, proj_in, FIRST, FIRST
    )
    side, far, act1 = lax.optimization_barrier((side, far, act1))
    at_side, at_middle = hop(far, OUT), hop(side, MIDDLE)
    sums2 = sums_of(ids, (0, 1, 3), (x, side, far), gate_w, up_w)
    whole = [pl.BlockSpec((size, depth), lambda j, ids: (0, 0))] * 2
    act2 = projected(
        late_kernel, "late", ids, (2,), [at_side, at_middle], whole, sums2, gate_w, up_w, proj_in,
        size, rows.shape[0],
    )
    return act1, act2


def over_planes(part):
    me = lax.axis_index("mp")
    part = part + hop(part, IN)
    part = part + hop(part, MIDDLE)
    return jnp.where((me == 1) | (me == 2), part, hop(part, OUT))


def swap(x, axis, k, size=4):
    return lax.ppermute(x, axis, [(s, s ^ k) for s in range(size)])


def sketch_of_kept(tokens, grad_out, gate_w, up_w, proj_in, proj_out, lengths, loss_mask, all_queries):
    most, depth = tokens.shape
    rank = proj_in.shape[1]
    team_at = lax.axis_index("dp").astype(I32).reshape(1)
    order, cells, x1 = call(
        first_kernel, "first", [SMEM] * 2 + [VMEM] * 2,
        (
            jax.ShapeDtypeStruct(loss_mask.shape, I32),
            jax.ShapeDtypeStruct((8, 128), F32),
            jax.ShapeDtypeStruct((FIRST, depth), BF16),
        ),
        (VMEM,) * 3, team_at, lengths, loss_mask, tokens,
    )
    own1, x1 = x1, gathered(x1)
    me = lax.axis_index("mp").astype(I32)
    ids = jnp.stack([me, me ^ 1, me ^ 2, me ^ 3])
    cells = cells + swap(cells, "dp", 1) + swap(cells, "dp", 2) + swap(cells, "dp", 3)
    table = cells[:TEAM, :2].astype(I32).reshape(-1)
    grad_part = lax.dot_general(proj_out, grad_out, (((0,), (1,)), ((), ())), preferred_element_type=F32)
    grad_part = over_planes(grad_part)
    high = lax.reduce_precision(grad_part, 8, 7)
    grads = jnp.concatenate([high.astype(BF16), (grad_part - high).astype(BF16)], axis=0)
    hand = jax.ShapeDtypeStruct((CAP, depth + 2 * rank), BF16)
    lots, *hands = call(
        deal_kernel, "deal", [SMEM] * 2 + [VMEM] * 3,
        (jax.ShapeDtypeStruct((3 * TEAM + 1,), I32),) + (hand,) * 3,
        (SMEM,) + (VMEM,) * 3, table, team_at, order, tokens, grads,
    )
    own1, *hands = lax.optimization_barrier((own1, *hands))
    hands = [swap(hand, "dp", k) for k, hand in zip((1, 2, 3), hands)]
    sums1 = sums_of(ids, (0,), (own1,), gate_w, up_w)
    hands, sums1 = lax.optimization_barrier((hands, sums1))
    rows, grads = call(
        place_kernel, "place", [SMEM] * 2 + [VMEM] * 6,
        (
            jax.ShapeDtypeStruct((most - FIRST, depth), BF16),
            jax.ShapeDtypeStruct((rank, most), F32),
        ),
        (VMEM,) * 2, lots, team_at, order, tokens, grads, *hands,
    )
    rows, all_queries = lax.optimization_barrier((rows, all_queries))
    sizes = sorted({s for s in (144, 192, 224, 256, 304, 432) if s < most - FIRST} | {most - FIRST})
    case = sum((lots[3 * TEAM] > s).astype(I32) for s in sizes[:-1])
    padded = jnp.pad(proj_in, ((0, -proj_in.shape[0] % 256), (0, 0)))
    act1, act2 = lax.switch(
        case, [functools.partial(rest_case, s) for s in sizes], ids, x1, sums1, rows, gate_w, up_w, padded
    )
    parts = call(
        sketch_kernel, "sketch", [SMEM] * 3 + [VMEM] * 3, jax.ShapeDtypeStruct((2 * TEAM * rank, rank), F32),
        VMEM, table, lots, team_at, grads, act1, act2,
    )
    parts = parts.reshape(TEAM, 2 * rank, rank)
    me = team_at[0]
    part = lax.dynamic_index_in_dim(parts, me, 0, False)
    for k in (1, 2, 3):
        part = part + swap(lax.dynamic_index_in_dim(parts, me ^ k, 0, False), "dp", k)
    return part + swap(part, "mp", 1) + swap(part, "mp", 2) + swap(part, "mp", 3), all_queries


def sketch_in_general(tokens, grad_out, gate_w, up_w, proj_in, proj_out, lengths, loss_mask, all_queries):
    roll_count, seq_len = loss_mask.shape
    rank = proj_in.shape[1]
    keep = (jnp.arange(seq_len, dtype=I32)[None, :] < lengths[:, None]) & (loss_mask == 1)
    pieces = gathered(tokens)
    hidden = (jax.nn.silu(dot32(pieces, gate_w)) * dot32(pieces, up_w)).astype(BF16)
    stacked = jnp.concatenate([dot32(grad_out, proj_out), dot32(hidden, proj_in)], axis=1)
    summed = lax.psum(stacked, "mp").reshape(roll_count, seq_len, 2 * rank)
    weighted = summed[:, :, :rank] * keep.astype(F32)[:, :, None]
    sums = jnp.einsum("rti,rtj->rij", weighted, summed[:, :, rank:], precision=lax.Precision.HIGHEST)
    return sums, all_queries


def team_queries(queries):
    me = lax.axis_index("dp")
    out = jnp.zeros((TEAM,) + queries.shape, queries.dtype)
    out = lax.dynamic_update_index_in_dim(out, queries, me, 0)
    for k in (1, 2, 3):
        out = lax.dynamic_update_index_in_dim(out, swap(queries, "dp", k), me ^ k, 0)
    return out


def local(team, planes, tokens, grad_out, gate_w, up_w, proj_in, proj_out, lengths, loss_mask, queries):
    roll_count, seq_len = loss_mask.shape
    fits = team == TEAM and planes == PLANES and roll_count == 2 and seq_len % 256 == 0
    fits = fits and tokens.shape[1] % 128 == 0 and gate_w.shape[1] % 128 == 0 and proj_in.shape[1] == 64
    form = sketch_of_kept if fits else sketch_in_general
    all_queries = team_queries(queries) if fits else lax.all_gather(queries, "dp", axis=0)
    sketch_sum, all_queries = form(
        tokens, grad_out, gate_w, up_w, proj_in, proj_out, lengths, loss_mask, all_queries
    )
    norm_factor = 1.0 / jnp.sqrt(jnp.float32(seq_len))
    sketch = (sketch_sum.reshape(roll_count, team, -1) * norm_factor).astype(BF16)
    return jnp.einsum("rdk,dqk->rq", sketch, all_queries, preferred_element_type=F32)


def solution(mesh):
    placed = (
        P(("groups", "dp"), "mp"),
        P(("groups", "dp"), "mp"),
        P(None, "mp"),
        P(None, "mp"),
        P("mp", None),
        P("mp", None),
        P(("groups", "dp")),
        P(("groups", "dp"), None),
        P("mp", "dp"),
    )
    return jax.shard_map(
        functools.partial(local, mesh.shape["dp"], mesh.shape["mp"]),
        mesh=mesh, in_specs=placed, out_specs=P(("groups", "dp"), "mp"), check_vma=False,
    )
```

```python
import functools

import jax
import jax.numpy as jnp
from jax import lax
from jax.experimental import pallas as pl
from jax.experimental.pallas import tpu as pltpu
from jax.sharding import PartitionSpec as P

BF16, F32, I32 = jnp.bfloat16, jnp.float32, jnp.int32
FIRST = 256
CAP = 192
TEAM = 4
PLANES = 4
MIB = 2**20


def dot32(a, b):
    return jnp.dot(a, b, preferred_element_type=F32)


def dot32_t(a, b):
    return lax.dot_general(a, b, (((1,), (1,)), ((), ())), preferred_element_type=F32)


def iota(shape, axis):
    return lax.broadcasted_iota(I32, shape, axis)


def ones_where(cond):
    return jnp.where(cond, 1.0, 0.0).astype(BF16)


def dealt(rest, most):
    keep = [jnp.minimum(m, most) for m in rest]
    spare_at, room_at, a, b = [], [], 0, 0
    for m, k in zip(rest, keep):
        spare_at.append(a)
        room_at.append(b)
        a, b = a + (m - k), b + (most - k)
    start, moved = {}, {}
    for s in range(TEAM):
        for t in range(TEAM):
            if s != t:
                low = jnp.maximum(spare_at[s], room_at[t])
                high = jnp.minimum(spare_at[s] + rest[s] - keep[s], room_at[t] + most - keep[t])
                start[s, t], moved[s, t] = low, jnp.maximum(high - low, 0)
    return keep, spare_at, room_at, start, moved


def plan(table):
    rest = [jnp.maximum(table[2 * s + 1] - FIRST, 0) for s in range(TEAM)]
    even = (rest[0] + rest[1] + rest[2] + rest[3] + (TEAM - 1)) // TEAM
    most = functools.reduce(jnp.maximum, rest)
    for tried in ((3 * most + even) // 4, (most + even) // 2, even):
        largest = functools.reduce(jnp.maximum, dealt(rest, tried)[4].values())
        most = jnp.where(largest <= CAP, tried, most)
    keep, spare_at, room_at, start, moved = dealt(rest, most)
    lots = {}
    for s in range(TEAM):
        lots[s, s] = (FIRST, 0, keep[s])
        for t in range(TEAM):
            if s != t:
                rank = FIRST + keep[s] + start[s, t] - spare_at[s]
                lots[s, t] = (rank, keep[t] + start[s, t] - room_at[t], moved[s, t])
    return most, lots


def chosen(lots, pairs):
    out = [0, 0, 0]
    for cond, pair in pairs:
        out = [jnp.where(cond, new, old) for new, old in zip(lots[pair], out)]
    return out


def first_kernel(team_at, lengths, loss_mask, tokens, order, table, rows):
    seq_len = loss_mask.shape[1]
    limit = jnp.where(iota(loss_mask.shape, 0) == 0, lengths[0], lengths[1])
    keep = (iota(loss_mask.shape, 1) < limit) & (loss_mask[...] == 1)
    upto = ones_where(iota((seq_len, seq_len), 0) <= iota((seq_len, seq_len), 1))
    kept = jnp.where(keep, 1.0, 0.0)
    place = dot32(kept.astype(BF16), upto)
    before = jnp.sum(kept[0:1], axis=1, keepdims=True)
    total = before + jnp.sum(kept[1:2], axis=1, keepdims=True)
    place = place - 1.0 + jnp.where(iota(place.shape, 0) == 0, 0.0, before)
    ranks = jnp.where(keep, place, -1.0).astype(I32)
    order[...] = ranks
    cell = jnp.where(iota(table.shape, 1) == 0, before, total)
    table[...] = jnp.where(iota(table.shape, 0) == team_at[0], cell, 0.0)
    at = iota((FIRST, seq_len), 0)
    found = dot32(ones_where(ranks[0:1] == at), tokens[:seq_len])
    found += dot32(ones_where(ranks[1:2] == at), tokens[seq_len:])
    rows[...] = found.astype(BF16)


def deal_kernel(table, team_at, order, tokens, grads, lots_to_me, *hands):
    me, seq_len = team_at[0], order.shape[1]
    most, lots = plan(table)
    lots_to_me[3 * TEAM] = most
    for s in range(TEAM):
        for i, value in enumerate(chosen(lots, [(me == t, (s, t)) for t in range(TEAM)])):
            lots_to_me[3 * s + i] = value
    depth = tokens.shape[1]
    at = iota((CAP, seq_len), 0)
    for k, hand in zip(range(1, TEAM), hands):
        rank, _, number = chosen(lots, [(me == s, (s, s ^ k)) for s in range(TEAM)])
        valid = at < number
        for side in range(2):
            pick = ones_where((order[side : side + 1] - rank == at) & valid)
            span = slice(side * seq_len, (side + 1) * seq_len)
            found, grad = dot32(pick, tokens[span]), dot32_t(pick, grads[:, span])
            if side == 0:
                hand[:, :depth], hand[:, depth:] = found.astype(BF16), grad.astype(BF16)
            else:
                hand[:, :depth] += found.astype(BF16)
                hand[:, depth:] += grad.astype(BF16)


def place_kernel(lots_to_me, team_at, order, tokens, grads, hand1, hand2, hand3, rows, grads_here):
    me, seq_len = team_at[0], order.shape[1]
    depth, rank_size = tokens.shape[1], grads_here.shape[0]
    kept = lots_to_me[3 * me + 2]
    step = FIRST
    at = iota((step, seq_len), 0)
    for base in range(-FIRST, rows.shape[0], step):
        valid = None if base < 0 else at + base < kept
        found, grad = 0.0, 0.0
        for side in range(2):
            hit = order[side : side + 1] - (FIRST + base) == at
            pick = ones_where(hit if valid is None else hit & valid)
            span = slice(side * seq_len, (side + 1) * seq_len)
            if base >= 0:
                found += dot32(pick, tokens[span])
            grad += dot32_t(grads[:, span], pick)
        if base >= 0:
            dealt_grad = 0.0
            for k, hand in ((1, hand1), (2, hand2), (3, hand3)):
                row, number = lots_to_me[3 * (me ^ k) + 1], lots_to_me[3 * (me ^ k) + 2]
                source = iota((step, CAP), 1)
                put = ones_where((iota((step, CAP), 0) + base - row == source) & (source < number))
                found += dot32(put, hand[:, :depth])
                dealt_grad += dot32(put, hand[:, depth:])
            grad += dealt_grad.T
            rows[base : base + step] = found.astype(BF16)
        grads_here[:, FIRST + base : FIRST + base + step] = grad[:rank_size] + grad[rank_size:]


def project(units, gate, up, proj, act):
    at = pl.program_id(0)
    hidden = gate / (1.0 + jnp.exp(-gate)) * up
    if units % gate.shape[1]:
        hidden = jnp.where(iota(hidden.shape, 1) + at * gate.shape[1] < units, hidden, 0.0)
    part = dot32(hidden.astype(BF16), proj[...])

    rows = part.shape[0]

    @pl.when(at == 0)
    def _():
        act[:rows] = part

    @pl.when(at > 0)
    def _():
        act[:rows] += part


def sums_kernel(slots, ids, *refs):
    del ids
    xs, gates, ups = refs[:slots], refs[slots : 2 * slots], refs[2 * slots : 3 * slots]
    gate_sum, up_sum = refs[3 * slots :]
    gate_sum[...] = sum(dot32(x[...], w[...]) for x, w in zip(xs, gates))
    up_sum[...] = sum(dot32(x[...], w[...]) for x, w in zip(xs, ups))


def rest_kernel(units, ids, x1, x2, x3, gate1, gate2, gate3, up1, up2, up3, gate_sum, up_sum, proj, act):
    del ids
    gate = gate_sum[...] + dot32(x1[...], gate1[...]) + dot32(x2[...], gate2[...]) + dot32(x3[...], gate3[...])
    up = up_sum[...] + dot32(x1[...], up1[...]) + dot32(x2[...], up2[...]) + dot32(x3[...], up3[...])
    project(units, gate, up, proj, act)


def late_kernel(units, ids, at_side, at_middle, gate_w, up_w, gate_sum, up_sum, proj, act):
    middle = (ids[0] == 1) | (ids[0] == 2)
    x = jnp.where(middle, at_middle[...], at_side[...])
    gate, up = gate_sum[...] + dot32(x, gate_w[...]), up_sum[...] + dot32(x, up_w[...])
    project(units, gate, up, proj, act)


def sketch_kernel(table, lots_to_me, team_at, grads, act1, act2, out):
    me, size = team_at[0], lots_to_me[3 * TEAM]

    def product(grad, lane, act):
        parts = []
        for s in range(TEAM):
            rank, row, number = lots_to_me[3 * s], lots_to_me[3 * s + 1] + FIRST, lots_to_me[3 * s + 2]
            edge = jnp.clip(row + table[2 * s] - rank, row, row + number)
            own = (me == s) & (lane < FIRST)
            cut = table[2 * s]
            for low, high, early in ((row, edge, lane < cut), (edge, row + number, lane >= cut)):
                mine = ((lane >= low) & (lane < high)) | (own & early)
                parts.append(jnp.where(mine, grad, 0.0))
        return jnp.dot(
            jnp.concatenate(parts, axis=0), act, precision=lax.Precision.HIGHEST, preferred_element_type=F32
        )

    out[...] = product(grads[:, :FIRST], iota((1, FIRST), 1), act1[...])

    def step(chunk, carry):
        base = pl.multiple_of(chunk * FIRST, FIRST)
        act = act2[pl.ds(base, FIRST), :]
        act = jnp.where(iota(act.shape, 0) + base < size, act, 0.0)
        lane = iota((1, FIRST), 1) + base + FIRST
        out[...] += product(grads[:, pl.ds(base + FIRST, FIRST)], lane, act)
        return carry

    lax.fori_loop(0, (size + FIRST - 1) // FIRST, step, 0)


VMEM = pl.BlockSpec(memory_space=pltpu.VMEM)
SMEM = pl.BlockSpec(memory_space=pltpu.SMEM)


def call(kernel, name, specs, out_shape, out_specs, *args):
    return pl.pallas_call(
        kernel, out_shape=out_shape, in_specs=specs, out_specs=out_specs, name=name,
        compiler_params=pltpu.CompilerParams(vmem_limit_bytes=40 * MIB),
    )(*args)


def grid_params():
    return pltpu.CompilerParams(dimension_semantics=("arbitrary",), vmem_limit_bytes=48 * MIB)


def streamed(body, name, ids, slots, xs, x_specs, gate_w, up_w, rest, rest_specs, outs, out_specs, flops, tile=256):
    depth, units = gate_w.shape[0] // PLANES, gate_w.shape[1]
    count, given, made = len(xs), len(rest), len(outs)

    def kernel(ids, *refs):
        x_refs, refs = refs[:count], refs[count:]
        gate_ref, up_ref = refs[:2]
        streams = refs[2 : 2 + given + made]
        weight = [
            pl.BlockSpec((depth, tile), lambda j, s=s: (ids[s], j), pipeline_mode=pl.Buffered(3)) for s in slots
        ]
        kept = [i for i, spec in enumerate(rest_specs + out_specs) if spec is None]
        flow = [i for i in range(given) if rest_specs[i] is not None]
        flow_out = [i for i in range(made) if out_specs[i] is not None]

        def step(*tiles):
            tiles = list(tiles)
            weights, tiles = tiles[: 2 * len(slots)], tiles[2 * len(slots) :]
            args = [streams[i] if i in kept else tiles.pop(0) for i in range(given + made)]
            body(ids, *x_refs, *weights, *args)

        pltpu.emit_pipeline(
            step, grid=(-(-units // tile),),
            in_specs=weight * 2 + [rest_specs[i] for i in flow], out_specs=[out_specs[i] for i in flow_out],
        )(
            *[gate_ref] * len(slots), *[up_ref] * len(slots),
            *[streams[i] for i in flow], *[streams[given + i] for i in flow_out],
        )

    anywhere = pl.BlockSpec(memory_space=pl.ANY)
    return pl.pallas_call(
        kernel,
        grid_spec=pltpu.PrefetchScalarGridSpec(
            num_scalar_prefetch=1, grid=(1,),
            in_specs=x_specs + [anywhere] * 2 + [VMEM if spec is None else anywhere for spec in rest_specs],
            out_specs=[VMEM if spec is None else anywhere for spec in out_specs],
        ),
        out_shape=outs,
        compiler_params=grid_params(),
        cost_estimate=pl.CostEstimate(
            flops=flops, bytes_accessed=4 * depth * units * len(slots), transcendentals=0
        ),
        name=name,
    )(ids, *xs, gate_w, up_w, *rest)


def tiled(rows, tile=256):
    return pl.BlockSpec((rows, tile), lambda j: (0, j))


def sums_of(ids, slots, xs, gate_w, up_w, tile=256):
    (rows, depth), units, count = xs[0].shape, gate_w.shape[1], len(xs)
    out = jax.ShapeDtypeStruct((rows, -(-units // tile) * tile), F32)
    return streamed(
        functools.partial(sums_kernel, count), "sums", ids, slots, xs, [VMEM] * count, gate_w, up_w, [], [],
        [out, out], [tiled(rows)] * 2, 4 * count * rows * depth * units,
    )


def projected(body, name, ids, slots, xs, x_specs, sums, gate_w, up_w, proj_in, rows, most, tile=256):
    depth, units, rank = gate_w.shape[0] // PLANES, gate_w.shape[1], proj_in.shape[1]
    return streamed(
        functools.partial(body, units), name, ids, slots, xs, x_specs, gate_w, up_w,
        [*sums, proj_in], [tiled(rows)] * 2 + [pl.BlockSpec((tile, rank), lambda j: (j, 0))],
        [jax.ShapeDtypeStruct((most, rank), F32)], [None], 4 * rows * depth * units * len(slots),
    )[0]


MIDDLE, OUT = [(1, 2), (2, 1)], [(1, 0), (2, 3)]


def gathered(x):
    return lax.all_gather(x, "mp", axis=1, tiled=True)


def hop(x, pairs):
    return lax.ppermute(x, "mp", pairs)


def rest_case(size, ids, x1, sums1, rows, gate_w, up_w, proj_in):
    x = rows[:size]
    side, far = swap(x, "mp", 1), swap(x, "mp", 3)
    depth = x.shape[1]
    spread = [pl.BlockSpec((FIRST, depth), lambda j, ids, s=s: (0, ids[s])) for s in (1, 2, 3)]
    act1 = projected(
        rest_kernel, "rest", ids, (1, 2, 3), [x1] * 3, spread, sums1, gate_w, up_w, proj_in, FIRST, FIRST
    )
    side, far, act1 = lax.optimization_barrier((side, far, act1))
    at_side, at_middle = hop(far, OUT), hop(side, MIDDLE)
    sums2 = sums_of(ids, (0, 1, 3), (x, side, far), gate_w, up_w)
    whole = [VMEM] * 2
    act2 = projected(
        late_kernel, "late", ids, (2,), [at_side, at_middle], whole, sums2, gate_w, up_w, proj_in,
        size, rows.shape[0],
    )
    return act1, act2


def swap(x, axis, k, size=4):
    return lax.ppermute(x, axis, [(s, s ^ k) for s in range(size)])


def sketch_of_kept(tokens, grad_out, gate_w, up_w, proj_in, proj_out, lengths, loss_mask, all_queries):
    most, depth = tokens.shape
    rank = proj_in.shape[1]
    team_at = lax.axis_index("dp").astype(I32).reshape(1)
    order, cells, x1 = call(
        first_kernel, "first", [SMEM] * 2 + [VMEM] * 2,
        (
            jax.ShapeDtypeStruct(loss_mask.shape, I32),
            jax.ShapeDtypeStruct((8, 128), F32),
            jax.ShapeDtypeStruct((FIRST, depth), BF16),
        ),
        (VMEM,) * 3, team_at, lengths, loss_mask, tokens,
    )
    own1, x1 = x1, gathered(x1)
    me = lax.axis_index("mp").astype(I32)
    ids = jnp.stack([me, me ^ 1, me ^ 2, me ^ 3])
    cells = cells + swap(cells, "dp", 1) + swap(cells, "dp", 2) + swap(cells, "dp", 3)
    table = cells[:TEAM, :2].astype(I32).reshape(-1)
    grad_part = lax.dot_general(proj_out, grad_out, (((0,), (1,)), ((), ())), preferred_element_type=F32)
    high = lax.reduce_precision(grad_part, 8, 7)
    grads = jnp.concatenate([high.astype(BF16), (grad_part - high).astype(BF16)], axis=0)
    hand = jax.ShapeDtypeStruct((CAP, depth + 2 * rank), BF16)
    lots, *hands = call(
        deal_kernel, "deal", [SMEM] * 2 + [VMEM] * 3,
        (jax.ShapeDtypeStruct((3 * TEAM + 1,), I32),) + (hand,) * 3,
        (SMEM,) + (VMEM,) * 3, table, team_at, order, tokens, grads,
    )
    own1, *hands = lax.optimization_barrier((own1, *hands))
    hands = [swap(hand, "dp", k) for k, hand in zip((1, 2, 3), hands)]
    sums1 = sums_of(ids, (0,), (own1,), gate_w, up_w)
    hands, sums1 = lax.optimization_barrier((hands, sums1))
    rows, grads = call(
        place_kernel, "place", [SMEM] * 2 + [VMEM] * 6,
        (
            jax.ShapeDtypeStruct((most - FIRST, depth), BF16),
            jax.ShapeDtypeStruct((rank, most), F32),
        ),
        (VMEM,) * 2, lots, team_at, order, tokens, grads, *hands,
    )
    rows, all_queries = lax.optimization_barrier((rows, all_queries))
    grads = lax.psum(grads, "mp")
    sizes = sorted({s for s in (144, 192, 224, 256, 304, 432) if s < most - FIRST} | {most - FIRST})
    case = sum((lots[3 * TEAM] > s).astype(I32) for s in sizes[:-1])
    padded = jnp.pad(proj_in, ((0, -proj_in.shape[0] % 256), (0, 0)))
    act1, act2 = lax.switch(
        case, [functools.partial(rest_case, s) for s in sizes], ids, x1, sums1, rows, gate_w, up_w, padded
    )
    parts = call(
        sketch_kernel, "sketch", [SMEM] * 3 + [VMEM] * 3, jax.ShapeDtypeStruct((2 * TEAM * rank, rank), F32),
        VMEM, table, lots, team_at, grads, act1, act2,
    )
    parts = parts.reshape(TEAM, 2 * rank, rank)
    me = team_at[0]
    part = lax.dynamic_index_in_dim(parts, me, 0, False)
    for k in (1, 2, 3):
        part = part + swap(lax.dynamic_index_in_dim(parts, me ^ k, 0, False), "dp", k)
    return part + swap(part, "mp", 1) + swap(part, "mp", 2) + swap(part, "mp", 3), all_queries


def sketch_in_general(tokens, grad_out, gate_w, up_w, proj_in, proj_out, lengths, loss_mask, all_queries):
    roll_count, seq_len = loss_mask.shape
    rank = proj_in.shape[1]
    keep = (jnp.arange(seq_len, dtype=I32)[None, :] < lengths[:, None]) & (loss_mask == 1)
    pieces = gathered(tokens)
    hidden = (jax.nn.silu(dot32(pieces, gate_w)) * dot32(pieces, up_w)).astype(BF16)
    stacked = jnp.concatenate([dot32(grad_out, proj_out), dot32(hidden, proj_in)], axis=1)
    summed = lax.psum(stacked, "mp").reshape(roll_count, seq_len, 2 * rank)
    weighted = summed[:, :, :rank] * keep.astype(F32)[:, :, None]
    sums = jnp.einsum("rti,rtj->rij", weighted, summed[:, :, rank:], precision=lax.Precision.HIGHEST)
    return sums, all_queries


def team_queries(queries):
    me = lax.axis_index("dp")
    out = jnp.zeros((TEAM,) + queries.shape, queries.dtype)
    out = lax.dynamic_update_index_in_dim(out, queries, me, 0)
    for k in (1, 2, 3):
        out = lax.dynamic_update_index_in_dim(out, swap(queries, "dp", k), me ^ k, 0)
    return out


def local(team, planes, tokens, grad_out, gate_w, up_w, proj_in, proj_out, lengths, loss_mask, queries):
    roll_count, seq_len = loss_mask.shape
    fits = team == TEAM and planes == PLANES and roll_count == 2 and seq_len % 256 == 0
    fits = fits and tokens.shape[1] % 128 == 0 and gate_w.shape[1] % 128 == 0 and proj_in.shape[1] == 64
    form = sketch_of_kept if fits else sketch_in_general
    all_queries = team_queries(queries) if fits else lax.all_gather(queries, "dp", axis=0)
    sketch_sum, all_queries = form(
        tokens, grad_out, gate_w, up_w, proj_in, proj_out, lengths, loss_mask, all_queries
    )
    norm_factor = 1.0 / jnp.sqrt(jnp.float32(seq_len))
    sketch = (sketch_sum.reshape(roll_count, team, -1) * norm_factor).astype(BF16)
    return jnp.einsum("rdk,dqk->rq", sketch, all_queries, preferred_element_type=F32)


def solution(mesh):
    placed = (
        P(("groups", "dp"), "mp"),
        P(("groups", "dp"), "mp"),
        P(None, "mp"),
        P(None, "mp"),
        P("mp", None),
        P("mp", None),
        P(("groups", "dp")),
        P(("groups", "dp"), None),
        P("mp", "dp"),
    )
    return jax.shard_map(
        functools.partial(local, mesh.shape["dp"], mesh.shape["mp"]),
        mesh=mesh, in_specs=placed, out_specs=P(("groups", "dp"), "mp"), check_vma=False,
    )
```

```python
import functools

import jax
import jax.numpy as jnp
from jax import lax
from jax.experimental import pallas as pl
from jax.experimental.pallas import tpu as pltpu
from jax.sharding import PartitionSpec as P

BF16, F32, I32 = jnp.bfloat16, jnp.float32, jnp.int32
FIRST = 256
CAP = 192
TEAM = 4
PLANES = 4
MIB = 2**20


def dot32(a, b):
    return jnp.dot(a, b, preferred_element_type=F32)


def dot32_t(a, b):
    return lax.dot_general(a, b, (((1,), (1,)), ((), ())), preferred_element_type=F32)


def iota(shape, axis):
    return lax.broadcasted_iota(I32, shape, axis)


def ones_where(cond):
    return jnp.where(cond, 1.0, 0.0).astype(BF16)


def dealt(rest, most):
    keep = [jnp.minimum(m, most) for m in rest]
    spare_at, room_at, a, b = [], [], 0, 0
    for m, k in zip(rest, keep):
        spare_at.append(a)
        room_at.append(b)
        a, b = a + (m - k), b + (most - k)
    start, moved = {}, {}
    for s in range(TEAM):
        for t in range(TEAM):
            if s != t:
                low = jnp.maximum(spare_at[s], room_at[t])
                high = jnp.minimum(spare_at[s] + rest[s] - keep[s], room_at[t] + most - keep[t])
                start[s, t], moved[s, t] = low, jnp.maximum(high - low, 0)
    return keep, spare_at, room_at, start, moved


def plan(table):
    rest = [jnp.maximum(table[2 * s + 1] - FIRST, 0) for s in range(TEAM)]
    even = (rest[0] + rest[1] + rest[2] + rest[3] + (TEAM - 1)) // TEAM
    most = functools.reduce(jnp.maximum, rest)
    for tried in ((3 * most + even) // 4, (most + even) // 2, even):
        largest = functools.reduce(jnp.maximum, dealt(rest, tried)[4].values())
        most = jnp.where(largest <= CAP, tried, most)
    keep, spare_at, room_at, start, moved = dealt(rest, most)
    lots = {}
    for s in range(TEAM):
        lots[s, s] = (FIRST, 0, keep[s])
        for t in range(TEAM):
            if s != t:
                rank = FIRST + keep[s] + start[s, t] - spare_at[s]
                lots[s, t] = (rank, keep[t] + start[s, t] - room_at[t], moved[s, t])
    return most, lots


def chosen(lots, pairs):
    out = [0, 0, 0]
    for cond, pair in pairs:
        out = [jnp.where(cond, new, old) for new, old in zip(lots[pair], out)]
    return out


def first_kernel(team_at, lengths, loss_mask_hbm, tokens_hbm, order, table, rows, loss_mask, tokens, sems):
    mask_copy = pltpu.make_async_copy(loss_mask_hbm, loss_mask, sems.at[0])
    token_copy = pltpu.make_async_copy(tokens_hbm, tokens, sems.at[1])
    mask_copy.start()
    token_copy.start()
    seq_len = loss_mask.shape[1]
    upto = ones_where(iota((seq_len, seq_len), 0) <= iota((seq_len, seq_len), 1))
    limit = jnp.where(iota(loss_mask.shape, 0) == 0, lengths[0], lengths[1])
    mask_copy.wait()
    keep = (iota(loss_mask.shape, 1) < limit) & (loss_mask[...] == 1)
    kept = jnp.where(keep, 1.0, 0.0)
    place = dot32(kept.astype(BF16), upto)
    before = jnp.sum(kept[0:1], axis=1, keepdims=True)
    total = before + jnp.sum(kept[1:2], axis=1, keepdims=True)
    place = place - 1.0 + jnp.where(iota(place.shape, 0) == 0, 0.0, before)
    ranks = jnp.where(keep, place, -1.0).astype(I32)
    order[...] = ranks
    cell = jnp.where(iota(table.shape, 1) == 0, before, total)
    table[...] = jnp.where(iota(table.shape, 0) == team_at[0], cell, 0.0)
    at = iota((FIRST, seq_len), 0)
    token_copy.wait()
    found = dot32(ones_where(ranks[0:1] == at), tokens[:seq_len])
    found += dot32(ones_where(ranks[1:2] == at), tokens[seq_len:])
    rows[...] = found.astype(BF16)


def deal_kernel(table, team_at, order, tokens, grads, lots_to_me, *hands):
    me, seq_len = team_at[0], order.shape[1]
    most, lots = plan(table)
    lots_to_me[3 * TEAM] = most
    for s in range(TEAM):
        for i, value in enumerate(chosen(lots, [(me == t, (s, t)) for t in range(TEAM)])):
            lots_to_me[3 * s + i] = value
    depth = tokens.shape[1]
    at = iota((CAP, seq_len), 0)
    for k, hand in zip(range(1, TEAM), hands):
        rank, _, number = chosen(lots, [(me == s, (s, s ^ k)) for s in range(TEAM)])
        valid = at < number
        for side in range(2):
            pick = ones_where((order[side : side + 1] - rank == at) & valid)
            span = slice(side * seq_len, (side + 1) * seq_len)
            found, grad = dot32(pick, tokens[span]), dot32_t(pick, grads[:, span])
            if side == 0:
                hand[:, :depth], hand[:, depth:] = found.astype(BF16), grad.astype(BF16)
            else:
                hand[:, :depth] += found.astype(BF16)
                hand[:, depth:] += grad.astype(BF16)


def place_kernel(lots_to_me, team_at, order, tokens, grads, hand1, hand2, hand3, rows, grads_here):
    me, seq_len = team_at[0], order.shape[1]
    depth, rank_size = tokens.shape[1], grads_here.shape[0]
    kept = lots_to_me[3 * me + 2]
    step = FIRST
    at = iota((step, seq_len), 0)
    for base in range(-FIRST, rows.shape[0], step):
        valid = None if base < 0 else at + base < kept
        found, grad = 0.0, 0.0
        for side in range(2):
            hit = order[side : side + 1] - (FIRST + base) == at
            pick = ones_where(hit if valid is None else hit & valid)
            span = slice(side * seq_len, (side + 1) * seq_len)
            if base >= 0:
                found += dot32(pick, tokens[span])
            grad += dot32_t(grads[:, span], pick)
        if base >= 0:
            dealt_grad = 0.0
            for k, hand in ((1, hand1), (2, hand2), (3, hand3)):
                row, number = lots_to_me[3 * (me ^ k) + 1], lots_to_me[3 * (me ^ k) + 2]
                source = iota((step, CAP), 1)
                put = ones_where((iota((step, CAP), 0) + base - row == source) & (source < number))
                found += dot32(put, hand[:, :depth])
                dealt_grad += dot32(put, hand[:, depth:])
            grad += dealt_grad.T
            rows[base : base + step] = found.astype(BF16)
        grads_here[:, FIRST + base : FIRST + base + step] = grad[:rank_size] + grad[rank_size:]


def sums_kernel(slots, ids, *refs):
    del ids
    xs, gates, ups = refs[:slots], refs[slots : 2 * slots], refs[2 * slots : 3 * slots]
    gate_sum, up_sum = refs[3 * slots :]
    gate_sum[...] = sum(dot32(x[...], w[...]) for x, w in zip(xs, gates))
    up_sum[...] = sum(dot32(x[...], w[...]) for x, w in zip(xs, ups))


def sketch_kernel(table, lots_to_me, team_at, grads, act1, act2, out):
    me, size = team_at[0], lots_to_me[3 * TEAM]

    def product(grad, lane, act):
        parts = []
        for s in range(TEAM):
            rank, row, number = lots_to_me[3 * s], lots_to_me[3 * s + 1] + FIRST, lots_to_me[3 * s + 2]
            edge = jnp.clip(row + table[2 * s] - rank, row, row + number)
            own = (me == s) & (lane < FIRST)
            cut = table[2 * s]
            for low, high, early in ((row, edge, lane < cut), (edge, row + number, lane >= cut)):
                mine = ((lane >= low) & (lane < high)) | (own & early)
                parts.append(jnp.where(mine, grad, 0.0))
        return jnp.dot(
            jnp.concatenate(parts, axis=0), act, precision=lax.Precision.HIGHEST, preferred_element_type=F32
        )

    out[...] = product(grads[:, :FIRST], iota((1, FIRST), 1), act1[...])

    def step(chunk, carry):
        base = pl.multiple_of(chunk * FIRST, FIRST)
        act = act2[pl.ds(base, FIRST), :]
        act = jnp.where(iota(act.shape, 0) + base < size, act, 0.0)
        lane = iota((1, FIRST), 1) + base + FIRST
        out[...] += product(grads[:, pl.ds(base + FIRST, FIRST)], lane, act)
        return carry

    lax.fori_loop(0, (size + FIRST - 1) // FIRST, step, 0)


ANY = pl.BlockSpec(memory_space=pl.ANY)
HBM = pl.BlockSpec(memory_space=pltpu.HBM)
VMEM = pl.BlockSpec(memory_space=pltpu.VMEM)
SMEM = pl.BlockSpec(memory_space=pltpu.SMEM)


def call(kernel, name, specs, out_shape, out_specs, *args, scratch=()):
    return pl.pallas_call(
        kernel, out_shape=out_shape, in_specs=specs, out_specs=out_specs, name=name, scratch_shapes=scratch,
        compiler_params=pltpu.CompilerParams(vmem_limit_bytes=32 * MIB),
    )(*args)


def weight_specs(ids, slots, depth, tile):
    deep = pl.Buffered(3)
    return [pl.BlockSpec((depth, tile), lambda j, s=s: (ids[s], j), pipeline_mode=deep) for s in slots] * 2


def tiled(rows, tile):
    return pl.BlockSpec((rows, tile), lambda j: (0, j))


def kernel_call(kernel, name, ids, operands, specs, out_shape, out_specs, scratch, flops, moved):
    return pl.pallas_call(
        kernel,
        in_specs=[SMEM] + specs, out_specs=out_specs, out_shape=out_shape, scratch_shapes=scratch, name=name,
        compiler_params=pltpu.CompilerParams(vmem_limit_bytes=32 * MIB),
        cost_estimate=pl.CostEstimate(flops=flops, bytes_accessed=moved, transcendentals=0),
    )(ids, *operands)


def sums_of(ids, slots, xs, gate_w, up_w, tile=256):
    (rows, depth), units, count = xs[0].shape, gate_w.shape[1], len(xs)
    steps = -(-units // tile)

    def kernel(ids, *refs):
        x_refs, (gate_w, up_w, gate_sum, up_sum) = refs[:count], refs[count:]

        def step(*tiles):
            gates, ups, (gate, up) = tiles[:count], tiles[count : 2 * count], tiles[2 * count :]
            gate[...] = sum(dot32(x[...], w[...]) for x, w in zip(x_refs, gates))
            up[...] = sum(dot32(x[...], w[...]) for x, w in zip(x_refs, ups))

        pltpu.emit_pipeline(
            step, grid=(steps,), in_specs=weight_specs(ids, slots, depth, tile), out_specs=[tiled(rows, tile)] * 2
        )(*[gate_w] * count, *[up_w] * count, gate_sum, up_sum)

    out = jax.ShapeDtypeStruct((rows, steps * tile), F32)
    return kernel_call(
        kernel, "sums", ids, [*xs, gate_w, up_w], [VMEM] * count + [ANY] * 2, (out, out), (ANY, ANY), (),
        4 * count * rows * depth * units, 4 * count * depth * units,
    )


def late(ids, at_side, at_middle, sums, gate_w, up_w, proj_in, most, tile=256):
    (rows, depth), units, rank, pairs = at_side.shape, gate_w.shape[1], proj_in.shape[1], len(sums)
    steps = proj_in.shape[0] // tile

    def kernel(ids, at_side, at_middle, gate_w, up_w, proj, *refs):
        sum_refs, (act, x, gate, up) = refs[: 2 * pairs], refs[2 * pairs :]
        middle = (ids[0] == 1) | (ids[0] == 2)
        x[...] = jnp.where(middle, at_middle[...], at_side[...])
        act[:rows] = jnp.zeros((rows, rank), F32)

        def project(j):
            g = gate[...]
            hidden = g / (1.0 + jnp.exp(-g)) * up[...]
            column = iota(hidden.shape, 1) + j * tile
            hidden = jnp.where((column >= 0) & (column < units), hidden, 0.0).astype(BF16)
            at = pl.multiple_of(jnp.maximum(j, 0) * tile, tile)
            return dot32(hidden, proj[pl.ds(at, tile), :])

        def step(gate_tile, up_tile, *tiles):
            before = project(pl.program_id(0) - 1)
            gate[...] = sum((t[...] for t in tiles[0::2]), dot32(x[...], gate_tile[...]))
            up[...] = sum((t[...] for t in tiles[1::2]), dot32(x[...], up_tile[...]))
            act[:rows] += before

        pltpu.emit_pipeline(
            step, grid=(steps,),
            in_specs=weight_specs(ids, (2,), depth, tile) + [tiled(rows, tile)] * (2 * pairs), out_specs=[],
        )(gate_w, up_w, *sum_refs)
        act[:rows] += project(steps - 1)

    flat = [t for pair in sums for t in pair]
    return kernel_call(
        kernel, "late", ids, [at_side, at_middle, gate_w, up_w, proj_in, *flat],
        [VMEM] * 2 + [ANY] * 2 + [VMEM] + [ANY] * len(flat), jax.ShapeDtypeStruct((most, rank), F32), VMEM,
        [pltpu.VMEM((rows, depth), BF16)] + [pltpu.VMEM((rows, tile), F32)] * 2,
        4 * rows * depth * units, 4 * depth * units,
    )


MIDDLE, OUT = [(1, 2), (2, 1)], [(1, 0), (2, 3)]


def gathered(x):
    return lax.all_gather(x, "mp", axis=1, tiled=True)


def hop(x, pairs):
    return lax.ppermute(x, "mp", pairs)


def rest_case(size, ids, at_side1, at_middle1, sums_own, sums_near, rows, gate_w, up_w, proj_in):
    x = rows[:size]
    side, far = swap(x, "mp", 1), swap(x, "mp", 3)
    act1 = late(ids, at_side1, at_middle1, [sums_own, sums_near], gate_w, up_w, proj_in, FIRST)
    side, far, act1 = lax.optimization_barrier((side, far, act1))
    at_side, at_middle = hop(far, OUT), hop(side, MIDDLE)
    sums = sums_of(ids, (0, 1, 3), (x, side, far), gate_w, up_w)
    act2 = late(ids, at_side, at_middle, [sums], gate_w, up_w, proj_in, rows.shape[0])
    return act1, act2


def swap(x, axis, k, size=4):
    return lax.ppermute(x, axis, [(s, s ^ k) for s in range(size)])


def sketch_of_kept(tokens, grad_out, gate_w, up_w, proj_in, proj_out, lengths, loss_mask, all_queries):
    most, depth = tokens.shape
    rank = proj_in.shape[1]
    team_at = lax.axis_index("dp").astype(I32).reshape(1)
    order, cells, own1 = call(
        first_kernel, "first", [SMEM] * 2 + [HBM] * 2,
        (
            jax.ShapeDtypeStruct(loss_mask.shape, I32),
            jax.ShapeDtypeStruct((8, 128), F32),
            jax.ShapeDtypeStruct((FIRST, depth), BF16),
        ),
        (VMEM,) * 3, team_at, lengths, loss_mask, tokens,
        scratch=[
            pltpu.VMEM(loss_mask.shape, I32), pltpu.VMEM(tokens.shape, BF16), pltpu.SemaphoreType.DMA((2,))
        ],
    )
    side1, far1 = swap(own1, "mp", 1), swap(own1, "mp", 3)
    me = lax.axis_index("mp").astype(I32)
    ids = jnp.stack([me, me ^ 1, me ^ 2, me ^ 3])
    cells = cells + swap(cells, "dp", 1) + swap(cells, "dp", 2) + swap(cells, "dp", 3)
    table = cells[:TEAM, :2].astype(I32).reshape(-1)
    grad_part = lax.dot_general(proj_out, grad_out, (((0,), (1,)), ((), ())), preferred_element_type=F32)
    high = lax.reduce_precision(grad_part, 8, 7)
    grads = jnp.concatenate([high.astype(BF16), (grad_part - high).astype(BF16)], axis=0)
    hand = jax.ShapeDtypeStruct((CAP, depth + 2 * rank), BF16)
    lots, *hands = call(
        deal_kernel, "deal", [SMEM] * 2 + [VMEM] * 3,
        (jax.ShapeDtypeStruct((3 * TEAM + 1,), I32),) + (hand,) * 3,
        (SMEM,) + (VMEM,) * 3, table, team_at, order, tokens, grads,
    )
    own1, *hands = lax.optimization_barrier((own1, *hands))
    hands = [swap(hand, "dp", k) for k, hand in zip((1, 2, 3), hands)]
    sums_own = sums_of(ids, (0,), (own1,), gate_w, up_w)
    side1, far1, sums_own = lax.optimization_barrier((side1, far1, sums_own))
    at_side1, at_middle1 = hop(far1, OUT), hop(side1, MIDDLE)
    sums_near = sums_of(ids, (1, 3), (side1, far1), gate_w, up_w)
    hands, sums_near = lax.optimization_barrier((hands, sums_near))
    rows, grads = call(
        place_kernel, "place", [SMEM] * 2 + [VMEM] * 6,
        (
            jax.ShapeDtypeStruct((most - FIRST, depth), BF16),
            jax.ShapeDtypeStruct((rank, most), F32),
        ),
        (VMEM,) * 2, lots, team_at, order, tokens, grads, *hands,
    )
    rows, all_queries = lax.optimization_barrier((rows, all_queries))
    grads = lax.psum(grads, "mp")
    sizes = sorted({s for s in (128, 160, 192, 224, 256, 288, 320, 384) if s < most - FIRST} | {most - FIRST})
    case = sum((lots[3 * TEAM] > s).astype(I32) for s in sizes[:-1])
    padded = jnp.pad(proj_in, ((0, -proj_in.shape[0] % 256), (0, 0)))
    act1, act2 = lax.switch(
        case, [functools.partial(rest_case, s) for s in sizes],
        ids, at_side1, at_middle1, sums_own, sums_near,
        rows, gate_w, up_w, padded,
    )
    parts = call(
        sketch_kernel, "sketch", [SMEM] * 3 + [VMEM] * 3, jax.ShapeDtypeStruct((2 * TEAM * rank, rank), F32),
        VMEM, table, lots, team_at, grads, act1, act2,
    )
    parts = parts.reshape(TEAM, 2 * rank, rank)
    me = team_at[0]
    part = lax.dynamic_index_in_dim(parts, me, 0, False)
    for k in (1, 2, 3):
        part = part + swap(lax.dynamic_index_in_dim(parts, me ^ k, 0, False), "dp", k)
    return part + swap(part, "mp", 1) + swap(part, "mp", 2) + swap(part, "mp", 3), all_queries


def sketch_in_general(tokens, grad_out, gate_w, up_w, proj_in, proj_out, lengths, loss_mask, all_queries):
    roll_count, seq_len = loss_mask.shape
    rank = proj_in.shape[1]
    keep = (jnp.arange(seq_len, dtype=I32)[None, :] < lengths[:, None]) & (loss_mask == 1)
    pieces = gathered(tokens)
    hidden = (jax.nn.silu(dot32(pieces, gate_w)) * dot32(pieces, up_w)).astype(BF16)
    stacked = jnp.concatenate([dot32(grad_out, proj_out), dot32(hidden, proj_in)], axis=1)
    summed = lax.psum(stacked, "mp").reshape(roll_count, seq_len, 2 * rank)
    weighted = summed[:, :, :rank] * keep.astype(F32)[:, :, None]
    sums = jnp.einsum("rti,rtj->rij", weighted, summed[:, :, rank:], precision=lax.Precision.HIGHEST)
    return sums, all_queries


def local(team, planes, tokens, grad_out, gate_w, up_w, proj_in, proj_out, lengths, loss_mask, queries):
    roll_count, seq_len = loss_mask.shape
    fits = team == TEAM and planes == PLANES and roll_count == 2 and seq_len % 256 == 0
    fits = fits and tokens.shape[1] % 128 == 0 and gate_w.shape[1] % 128 == 0 and proj_in.shape[1] == 64
    form = sketch_of_kept if fits else sketch_in_general
    all_queries = lax.all_gather(queries, "dp", axis=0)
    sketch_sum, all_queries = form(
        tokens, grad_out, gate_w, up_w, proj_in, proj_out, lengths, loss_mask, all_queries
    )
    norm_factor = 1.0 / jnp.sqrt(jnp.float32(seq_len))
    sketch = (sketch_sum.reshape(roll_count, team, -1) * norm_factor).astype(BF16)
    return jnp.einsum("rdk,dqk->rq", sketch, all_queries, preferred_element_type=F32)


def solution(mesh):
    placed = (
        P(("groups", "dp"), "mp"),
        P(("groups", "dp"), "mp"),
        P(None, "mp"),
        P(None, "mp"),
        P("mp", None),
        P("mp", None),
        P(("groups", "dp")),
        P(("groups", "dp"), None),
        P("mp", "dp"),
    )
    return jax.shard_map(
        functools.partial(local, mesh.shape["dp"], mesh.shape["mp"]),
        mesh=mesh, in_specs=placed, out_specs=P(("groups", "dp"), "mp"), check_vma=False,
    )
```

```python
import functools

import jax
import jax.numpy as jnp
from jax import lax
from jax.experimental import pallas as pl
from jax.experimental.pallas import tpu as pltpu
from jax.sharding import PartitionSpec as P

BF16, F32, I32 = jnp.bfloat16, jnp.float32, jnp.int32
FIRST = 256
SIZES = (160, 208, 256, 304, 400)
CAP = 192
TEAM = 4
PLANES = 4
MIB = 2**20


def dot32(a, b):
    return jnp.dot(a, b, preferred_element_type=F32)


def dot32_t(a, b):
    return lax.dot_general(a, b, (((1,), (1,)), ((), ())), preferred_element_type=F32)


def iota(shape, axis):
    return lax.broadcasted_iota(I32, shape, axis)


def ones_where(cond):
    return jnp.where(cond, 1.0, 0.0).astype(BF16)


def dealt(rest, most):
    keep = [jnp.minimum(m, most) for m in rest]
    spare_at, room_at, a, b = [], [], 0, 0
    for m, k in zip(rest, keep):
        spare_at.append(a)
        room_at.append(b)
        a, b = a + (m - k), b + (most - k)
    start, moved = {}, {}
    for s in range(TEAM):
        for t in range(TEAM):
            if s != t:
                low = jnp.maximum(spare_at[s], room_at[t])
                high = jnp.minimum(spare_at[s] + rest[s] - keep[s], room_at[t] + most - keep[t])
                start[s, t], moved[s, t] = low, jnp.maximum(high - low, 0)
    return keep, spare_at, room_at, start, moved


def plan(table):
    rest = [jnp.maximum(table[2 * s + 1] - FIRST, 0) for s in range(TEAM)]
    even = (rest[0] + rest[1] + rest[2] + rest[3] + (TEAM - 1)) // TEAM
    most = functools.reduce(jnp.maximum, rest)
    for tried in ((3 * most + even) // 4, (most + even) // 2, even):
        largest = functools.reduce(jnp.maximum, dealt(rest, tried)[4].values())
        most = jnp.where(largest <= CAP, tried, most)
    keep, spare_at, room_at, start, moved = dealt(rest, most)
    lots = {}
    for s in range(TEAM):
        lots[s, s] = (FIRST, 0, keep[s])
        for t in range(TEAM):
            if s != t:
                rank = FIRST + keep[s] + start[s, t] - spare_at[s]
                lots[s, t] = (rank, keep[t] + start[s, t] - room_at[t], moved[s, t])
    return most, lots


def chosen(lots, pairs):
    out = [0, 0, 0]
    for cond, pair in pairs:
        out = [jnp.where(cond, new, old) for new, old in zip(lots[pair], out)]
    return out


def first_kernel(team_at, lengths, loss_mask, tokens, order, table, rows):
    seq_len = loss_mask.shape[1]
    limit = jnp.where(iota(loss_mask.shape, 0) == 0, lengths[0], lengths[1])
    keep = (iota(loss_mask.shape, 1) < limit) & (loss_mask[...] == 1)
    upto = ones_where(iota((seq_len, seq_len), 0) <= iota((seq_len, seq_len), 1))
    kept = jnp.where(keep, 1.0, 0.0)
    place = dot32(kept.astype(BF16), upto)
    before = jnp.sum(kept[0:1], axis=1, keepdims=True)
    total = before + jnp.sum(kept[1:2], axis=1, keepdims=True)
    place = place - 1.0 + jnp.where(iota(place.shape, 0) == 0, 0.0, before)
    ranks = jnp.where(keep, place, -1.0).astype(I32)
    order[...] = ranks
    cell = jnp.where(iota(table.shape, 1) == 0, before, total)
    table[...] = jnp.where(iota(table.shape, 0) == team_at[0], cell, 0.0)
    at = iota((FIRST, seq_len), 0)
    found = dot32(ones_where(ranks[0:1] == at), tokens[:seq_len])
    found += dot32(ones_where(ranks[1:2] == at), tokens[seq_len:])
    rows[...] = found.astype(BF16)


def deal_kernel(sizes, table, team_at, order, tokens, grads, lots_to_me, *hands):
    me, seq_len = team_at[0], order.shape[1]
    most, lots = plan(table)
    lots_to_me[3 * TEAM] = most
    lots_to_me[3 * TEAM + 1] = sum((most > size).astype(I32) for size in sizes[:-1])
    for s in range(TEAM):
        for i, value in enumerate(chosen(lots, [(me == t, (s, t)) for t in range(TEAM)])):
            lots_to_me[3 * s + i] = value
    depth = tokens.shape[1]
    at = iota((CAP, seq_len), 0)
    for k, hand in zip(range(1, TEAM), hands):
        rank, _, number = chosen(lots, [(me == s, (s, s ^ k)) for s in range(TEAM)])
        valid = at < number
        for side in range(2):
            pick = ones_where((order[side : side + 1] - rank == at) & valid)
            span = slice(side * seq_len, (side + 1) * seq_len)
            found, grad = dot32(pick, tokens[span]), dot32_t(pick, grads[:, span])
            if side == 0:
                hand[:, :depth], hand[:, depth:] = found.astype(BF16), grad.astype(BF16)
            else:
                hand[:, :depth] += found.astype(BF16)
                hand[:, depth:] += grad.astype(BF16)


def place_kernel(lots_to_me, team_at, order, tokens, grads, hand1, hand2, hand3, rows, grads_here):
    me, seq_len = team_at[0], order.shape[1]
    depth, rank_size = tokens.shape[1], grads_here.shape[0]
    kept = lots_to_me[3 * me + 2]
    step = FIRST
    at = iota((step, seq_len), 0)
    for base in range(-FIRST, rows.shape[0], step):
        valid = None if base < 0 else at + base < kept
        found, grad = 0.0, 0.0
        for side in range(2):
            hit = order[side : side + 1] - (FIRST + base) == at
            pick = ones_where(hit if valid is None else hit & valid)
            span = slice(side * seq_len, (side + 1) * seq_len)
            if base >= 0:
                found += dot32(pick, tokens[span])
            grad += dot32_t(grads[:, span], pick)
        if base >= 0:
            dealt_grad = 0.0
            for k, hand in ((1, hand1), (2, hand2), (3, hand3)):
                row, number = lots_to_me[3 * (me ^ k) + 1], lots_to_me[3 * (me ^ k) + 2]
                source = iota((step, CAP), 1)
                put = ones_where((iota((step, CAP), 0) + base - row == source) & (source < number))
                found += dot32(put, hand[:, :depth])
                dealt_grad += dot32(put, hand[:, depth:])
            grad += dealt_grad.T
            rows[base : base + step] = found.astype(BF16)
        grads_here[:, FIRST + base : FIRST + base + step] = grad[:rank_size] + grad[rank_size:]


def sums_kernel(slots, ids, *refs):
    del ids
    xs, gates, ups = refs[:slots], refs[slots : 2 * slots], refs[2 * slots : 3 * slots]
    gate_sum, up_sum = refs[3 * slots :]
    gate_sum[...] = sum(dot32(x[...], w[...]) for x, w in zip(xs, gates))
    up_sum[...] = sum(dot32(x[...], w[...]) for x, w in zip(xs, ups))


def sketch_kernel(table, lots_to_me, team_at, grads, act1, act2, out):
    me, size = team_at[0], lots_to_me[3 * TEAM]

    def product(grad, lane, act):
        parts = []
        for s in range(TEAM):
            rank, row, number = lots_to_me[3 * s], lots_to_me[3 * s + 1] + FIRST, lots_to_me[3 * s + 2]
            edge = jnp.clip(row + table[2 * s] - rank, row, row + number)
            own = (me == s) & (lane < FIRST)
            cut = table[2 * s]
            for low, high, early in ((row, edge, lane < cut), (edge, row + number, lane >= cut)):
                mine = ((lane >= low) & (lane < high)) | (own & early)
                parts.append(jnp.where(mine, grad, 0.0))
        return jnp.dot(
            jnp.concatenate(parts, axis=0), act, precision=lax.Precision.HIGHEST, preferred_element_type=F32
        )

    out[...] = product(grads[:, :FIRST], iota((1, FIRST), 1), act1[...])

    def step(chunk, carry):
        base = pl.multiple_of(chunk * FIRST, FIRST)
        act = act2[pl.ds(base, FIRST), :]
        act = jnp.where(iota(act.shape, 0) + base < size, act, 0.0)
        lane = iota((1, FIRST), 1) + base + FIRST
        out[...] += product(grads[:, pl.ds(base + FIRST, FIRST)], lane, act)
        return carry

    lax.fori_loop(0, (size + FIRST - 1) // FIRST, step, 0)


ANY = pl.BlockSpec(memory_space=pl.ANY)
VMEM = pl.BlockSpec(memory_space=pltpu.VMEM)
SMEM = pl.BlockSpec(memory_space=pltpu.SMEM)


def call(kernel, name, specs, out_shape, out_specs, *args):
    return pl.pallas_call(
        kernel, out_shape=out_shape, in_specs=specs, out_specs=out_specs, name=name,
        compiler_params=pltpu.CompilerParams(vmem_limit_bytes=32 * MIB),
    )(*args)


def weight_specs(ids, slots, depth, tile):
    deep = pl.Buffered(3)
    return [pl.BlockSpec((depth, tile), lambda j, s=s: (ids[s], j), pipeline_mode=deep) for s in slots] * 2


def tiled(rows, tile):
    return pl.BlockSpec((rows, tile), lambda j: (0, j))


def kernel_call(kernel, name, ids, operands, specs, out_shape, out_specs, scratch, flops, moved):
    return pl.pallas_call(
        kernel,
        in_specs=[SMEM] + specs, out_specs=out_specs, out_shape=out_shape, scratch_shapes=scratch, name=name,
        compiler_params=pltpu.CompilerParams(vmem_limit_bytes=32 * MIB),
        cost_estimate=pl.CostEstimate(flops=flops, bytes_accessed=moved, transcendentals=0),
    )(ids, *operands)


def sums_of(ids, slots, xs, gate_w, up_w, tile=256):
    (rows, depth), units, count = xs[0].shape, gate_w.shape[1], len(xs)
    steps = -(-units // tile)

    def kernel(ids, *refs):
        x_refs, (gate_w, up_w, gate_sum, up_sum) = refs[:count], refs[count:]

        def step(*tiles):
            gates, ups, (gate, up) = tiles[:count], tiles[count : 2 * count], tiles[2 * count :]
            gate[...] = sum(dot32(x[...], w[...]) for x, w in zip(x_refs, gates))
            up[...] = sum(dot32(x[...], w[...]) for x, w in zip(x_refs, ups))

        pltpu.emit_pipeline(
            step, grid=(steps,), in_specs=weight_specs(ids, slots, depth, tile), out_specs=[tiled(rows, tile)] * 2
        )(*[gate_w] * count, *[up_w] * count, gate_sum, up_sum)

    out = jax.ShapeDtypeStruct((rows, steps * tile), F32)
    return kernel_call(
        kernel, "sums", ids, [*xs, gate_w, up_w], [VMEM] * count + [ANY] * 2, (out, out), (ANY, ANY), (),
        4 * count * rows * depth * units, 4 * count * depth * units,
    )


def projected(ids, slots, xs, at_side, at_middle, sums, gate_w, up_w, proj_in, most, tile=256):
    (rows, depth), units, rank, count = at_side.shape, gate_w.shape[1], proj_in.shape[1], len(slots)
    steps = proj_in.shape[0] // tile

    def kernel(ids, at_side, at_middle, gate_w, up_w, proj, gate_sum, up_sum, *refs):
        x_refs, (act, x, gate, up) = refs[: count - 1], refs[count - 1 :]
        middle = (ids[0] == 1) | (ids[0] == 2)
        x[...] = jnp.where(middle, at_middle[...], at_side[...])
        act[:rows] = jnp.zeros((rows, rank), F32)

        def project(j):
            g = gate[...]
            hidden = g / (1.0 + jnp.exp(-g)) * up[...]
            column = iota(hidden.shape, 1) + j * tile
            hidden = jnp.where((column >= 0) & (column < units), hidden, 0.0).astype(BF16)
            at = pl.multiple_of(jnp.maximum(j, 0) * tile, tile)
            return dot32(hidden, proj[pl.ds(at, tile), :])

        def step(*tiles):
            gates, ups, (gate_tile, up_tile) = tiles[:count], tiles[count : 2 * count], tiles[2 * count :]
            before = project(pl.program_id(0) - 1)
            blocks = [*x_refs, x]
            gate[...] = sum((dot32(b[...], w[...]) for b, w in zip(blocks, gates)), gate_tile[...])
            up[...] = sum((dot32(b[...], w[...]) for b, w in zip(blocks, ups)), up_tile[...])
            act[:rows] += before

        pltpu.emit_pipeline(
            step, grid=(steps,),
            in_specs=weight_specs(ids, slots, depth, tile) + [tiled(rows, tile)] * 2, out_specs=[],
        )(*[gate_w] * count, *[up_w] * count, gate_sum, up_sum)
        act[:rows] += project(steps - 1)

    return kernel_call(
        kernel, "late", ids, [at_side, at_middle, gate_w, up_w, proj_in, *sums, *xs],
        [VMEM] * 2 + [ANY] * 2 + [VMEM] + [ANY] * 2 + [VMEM] * len(xs),
        jax.ShapeDtypeStruct((most, rank), F32), VMEM,
        [pltpu.VMEM((rows, depth), BF16)] + [pltpu.VMEM((rows, tile), F32)] * 2,
        4 * count * rows * depth * units, 4 * count * depth * units,
    )


MIDDLE, OUT = [(1, 2), (2, 1)], [(1, 0), (2, 3)]


def gathered(x):
    return lax.all_gather(x, "mp", axis=1, tiled=True)


def hop(x, pairs):
    return lax.ppermute(x, "mp", pairs)


def rest_case(size, ids, xs1, ends1, sums_own, rows, gate_w, up_w, proj_in):
    x = rows[:size]
    side, far = swap(x, "mp", 1), swap(x, "mp", 3)
    act1 = projected(ids, (1, 3, 2), xs1, *ends1, sums_own, gate_w, up_w, proj_in, FIRST)
    side, far, act1 = lax.optimization_barrier((side, far, act1))
    at_side, at_middle = hop(far, OUT), hop(side, MIDDLE)
    sums = sums_of(ids, (0, 1, 3), (x, side, far), gate_w, up_w)
    act2 = projected(ids, (2,), (), at_side, at_middle, sums, gate_w, up_w, proj_in, rows.shape[0])
    return act1, act2


def swap(x, axis, k, size=4):
    return lax.ppermute(x, axis, [(s, s ^ k) for s in range(size)])


def sketch_of_kept(tokens, grad_out, gate_w, up_w, proj_in, proj_out, lengths, loss_mask, queries):
    most, depth = tokens.shape
    rank = proj_in.shape[1]
    team_at = lax.axis_index("dp").astype(I32).reshape(1)
    order, cells, own1 = call(
        first_kernel, "first", [SMEM] * 2 + [VMEM] * 2,
        (
            jax.ShapeDtypeStruct(loss_mask.shape, I32),
            jax.ShapeDtypeStruct((8, 128), F32),
            jax.ShapeDtypeStruct((FIRST, depth), BF16),
        ),
        (VMEM,) * 3, team_at, lengths, loss_mask, tokens,
    )
    queries = lax.optimization_barrier((queries, own1))[0]
    all_queries = lax.all_gather(queries, "dp", axis=0)
    side1, far1 = swap(own1, "mp", 1), swap(own1, "mp", 3)
    me = lax.axis_index("mp").astype(I32)
    ids = jnp.stack([me, me ^ 1, me ^ 2, me ^ 3])
    cells = cells + swap(cells, "dp", 1) + swap(cells, "dp", 2) + swap(cells, "dp", 3)
    table = cells[:TEAM, :2].astype(I32).reshape(-1)
    grad_part = lax.dot_general(proj_out, grad_out, (((0,), (1,)), ((), ())), preferred_element_type=F32)
    high = lax.reduce_precision(grad_part, 8, 7)
    grads = jnp.concatenate([high.astype(BF16), (grad_part - high).astype(BF16)], axis=0)
    sizes = sorted({s for s in SIZES if s < most - FIRST} | {most - FIRST})
    hand = jax.ShapeDtypeStruct((CAP, depth + 2 * rank), BF16)
    lots, *hands = call(
        functools.partial(deal_kernel, sizes), "deal", [SMEM] * 2 + [VMEM] * 3,
        (jax.ShapeDtypeStruct((3 * TEAM + 2,), I32),) + (hand,) * 3,
        (SMEM,) + (VMEM,) * 3, table, team_at, order, tokens, grads,
    )
    own1, *hands = lax.optimization_barrier((own1, *hands))
    hands = [swap(hand, "dp", k) for k, hand in zip((1, 2, 3), hands)]
    sums_own = sums_of(ids, (0,), (own1,), gate_w, up_w)
    side1, far1, sums_own = lax.optimization_barrier((side1, far1, sums_own))
    ends1 = hop(far1, OUT), hop(side1, MIDDLE)
    hands, side1, far1 = lax.optimization_barrier((hands, side1, far1))
    rows, grads = call(
        place_kernel, "place", [SMEM] * 2 + [VMEM] * 6,
        (
            jax.ShapeDtypeStruct((most - FIRST, depth), BF16),
            jax.ShapeDtypeStruct((rank, most), F32),
        ),
        (VMEM,) * 2, lots, team_at, order, tokens, grads, *hands,
    )
    rows, all_queries = lax.optimization_barrier((rows, all_queries))
    grads = lax.psum(grads, "mp")
    padded = jnp.pad(proj_in, ((0, -proj_in.shape[0] % 256), (0, 0)))
    act1, act2 = lax.switch(
        lots[3 * TEAM + 1], [functools.partial(rest_case, s) for s in sizes],
        ids, (side1, far1), ends1, sums_own, rows, gate_w, up_w, padded,
    )
    parts = call(
        sketch_kernel, "sketch", [SMEM] * 3 + [VMEM] * 3, jax.ShapeDtypeStruct((2 * TEAM * rank, rank), F32),
        VMEM, table, lots, team_at, grads, act1, act2,
    )
    parts = parts.reshape(TEAM, 2 * rank, rank)
    me = team_at[0]
    part = lax.dynamic_index_in_dim(parts, me, 0, False)
    for k in (1, 2, 3):
        part = part + swap(lax.dynamic_index_in_dim(parts, me ^ k, 0, False), "dp", k)
    return part + swap(part, "mp", 1) + swap(part, "mp", 2) + swap(part, "mp", 3), all_queries


def sketch_in_general(tokens, grad_out, gate_w, up_w, proj_in, proj_out, lengths, loss_mask, queries):
    roll_count, seq_len = loss_mask.shape
    rank = proj_in.shape[1]
    keep = (jnp.arange(seq_len, dtype=I32)[None, :] < lengths[:, None]) & (loss_mask == 1)
    pieces = gathered(tokens)
    hidden = (jax.nn.silu(dot32(pieces, gate_w)) * dot32(pieces, up_w)).astype(BF16)
    stacked = jnp.concatenate([dot32(grad_out, proj_out), dot32(hidden, proj_in)], axis=1)
    summed = lax.psum(stacked, "mp").reshape(roll_count, seq_len, 2 * rank)
    weighted = summed[:, :, :rank] * keep.astype(F32)[:, :, None]
    sums = jnp.einsum("rti,rtj->rij", weighted, summed[:, :, rank:], precision=lax.Precision.HIGHEST)
    return sums, lax.all_gather(queries, "dp", axis=0)


def local(team, planes, tokens, grad_out, gate_w, up_w, proj_in, proj_out, lengths, loss_mask, queries):
    roll_count, seq_len = loss_mask.shape
    fits = team == TEAM and planes == PLANES and roll_count == 2 and seq_len % 256 == 0
    fits = fits and tokens.shape[1] % 128 == 0 and gate_w.shape[1] % 128 == 0 and proj_in.shape[1] == 64
    form = sketch_of_kept if fits else sketch_in_general
    sketch_sum, all_queries = form(
        tokens, grad_out, gate_w, up_w, proj_in, proj_out, lengths, loss_mask, queries
    )
    norm_factor = 1.0 / jnp.sqrt(jnp.float32(seq_len))
    sketch = (sketch_sum.reshape(roll_count, team, -1) * norm_factor).astype(BF16)
    return jnp.einsum("rdk,dqk->rq", sketch, all_queries, preferred_element_type=F32)


def solution(mesh):
    placed = (
        P(("groups", "dp"), "mp"),
        P(("groups", "dp"), "mp"),
        P(None, "mp"),
        P(None, "mp"),
        P("mp", None),
        P("mp", None),
        P(("groups", "dp")),
        P(("groups", "dp"), None),
        P("mp", "dp"),
    )
    return jax.shard_map(
        functools.partial(local, mesh.shape["dp"], mesh.shape["mp"]),
        mesh=mesh, in_specs=placed, out_specs=P(("groups", "dp"), "mp"), check_vma=False,
    )
```

```python
import functools

import jax
import jax.numpy as jnp
from jax import lax
from jax.experimental import pallas as pl
from jax.experimental.pallas import tpu as pltpu
from jax.sharding import PartitionSpec as P

BF16, F32, I32 = jnp.bfloat16, jnp.float32, jnp.int32
FIRST = 256
SIZES = (160, 208, 256, 304, 400)
CAP = 192
TEAM = 4
PLANES = 4
MIB = 2**20


def dot32(a, b):
    return jnp.dot(a, b, preferred_element_type=F32)


def dot32_t(a, b):
    return lax.dot_general(a, b, (((1,), (1,)), ((), ())), preferred_element_type=F32)


def iota(shape, axis):
    return lax.broadcasted_iota(I32, shape, axis)


def ones_where(cond):
    return jnp.where(cond, 1.0, 0.0).astype(BF16)


def dealt(rest, most):
    keep = [jnp.minimum(m, most) for m in rest]
    spare_at, room_at, a, b = [], [], 0, 0
    for m, k in zip(rest, keep):
        spare_at.append(a)
        room_at.append(b)
        a, b = a + (m - k), b + (most - k)
    start, moved = {}, {}
    for s in range(TEAM):
        for t in range(TEAM):
            if s != t:
                low = jnp.maximum(spare_at[s], room_at[t])
                high = jnp.minimum(spare_at[s] + rest[s] - keep[s], room_at[t] + most - keep[t])
                start[s, t], moved[s, t] = low, jnp.maximum(high - low, 0)
    return keep, spare_at, room_at, start, moved


def plan(table):
    rest = [jnp.maximum(table[2 * s + 1] - FIRST, 0) for s in range(TEAM)]
    even = (rest[0] + rest[1] + rest[2] + rest[3] + (TEAM - 1)) // TEAM
    most = functools.reduce(jnp.maximum, rest)
    for tried in ((3 * most + even) // 4, (most + even) // 2, even):
        largest = functools.reduce(jnp.maximum, dealt(rest, tried)[4].values())
        most = jnp.where(largest <= CAP, tried, most)
    keep, spare_at, room_at, start, moved = dealt(rest, most)
    lots = {}
    for s in range(TEAM):
        lots[s, s] = (FIRST, 0, keep[s])
        for t in range(TEAM):
            if s != t:
                rank = FIRST + keep[s] + start[s, t] - spare_at[s]
                lots[s, t] = (rank, keep[t] + start[s, t] - room_at[t], moved[s, t])
    return most, lots


def chosen(lots, pairs):
    out = [0, 0, 0]
    for cond, pair in pairs:
        out = [jnp.where(cond, new, old) for new, old in zip(lots[pair], out)]
    return out


def first_kernel(team_at, lengths, loss_mask, tokens, order, table, rows):
    seq_len = loss_mask.shape[1]
    limit = jnp.where(iota(loss_mask.shape, 0) == 0, lengths[0], lengths[1])
    keep = (iota(loss_mask.shape, 1) < limit) & (loss_mask[...] == 1)
    upto = ones_where(iota((seq_len, seq_len), 0) <= iota((seq_len, seq_len), 1))
    kept = jnp.where(keep, 1.0, 0.0)
    place = dot32(kept.astype(BF16), upto)
    before = jnp.sum(kept[0:1], axis=1, keepdims=True)
    total = before + jnp.sum(kept[1:2], axis=1, keepdims=True)
    place = place - 1.0 + jnp.where(iota(place.shape, 0) == 0, 0.0, before)
    ranks = jnp.where(keep, place, -1.0).astype(I32)
    order[...] = ranks
    cell = jnp.where(iota(table.shape, 1) == 0, before, total)
    table[...] = jnp.where(iota(table.shape, 0) == team_at[0], cell, 0.0)
    at = iota((FIRST, seq_len), 0)
    found = dot32(ones_where(ranks[0:1] == at), tokens[:seq_len])
    found += dot32(ones_where(ranks[1:2] == at), tokens[seq_len:])
    rows[...] = found.astype(BF16)


def deal_kernel(sizes, table, team_at, order, tokens, grads, lots_to_me, *hands):
    me, seq_len = team_at[0], order.shape[1]
    most, lots = plan(table)
    lots_to_me[3 * TEAM] = most
    lots_to_me[3 * TEAM + 1] = sum((most > size).astype(I32) for size in sizes[:-1])
    for s in range(TEAM):
        for i, value in enumerate(chosen(lots, [(me == t, (s, t)) for t in range(TEAM)])):
            lots_to_me[3 * s + i] = value
    depth = tokens.shape[1]
    at = iota((CAP, seq_len), 0)
    for k, hand in zip(range(1, TEAM), hands):
        rank, _, number = chosen(lots, [(me == s, (s, s ^ k)) for s in range(TEAM)])
        valid = at < number
        for side in range(2):
            pick = ones_where((order[side : side + 1] - rank == at) & valid)
            span = slice(side * seq_len, (side + 1) * seq_len)
            found, grad = dot32(pick, tokens[span]), dot32_t(pick, grads[:, span])
            if side == 0:
                hand[:, :depth], hand[:, depth:] = found.astype(BF16), grad.astype(BF16)
            else:
                hand[:, :depth] += found.astype(BF16)
                hand[:, depth:] += grad.astype(BF16)


def place_kernel(lots_to_me, team_at, order, tokens, grads, hand1, hand2, hand3, rows, grads_here):
    me, seq_len = team_at[0], order.shape[1]
    depth, rank_size = tokens.shape[1], grads_here.shape[0]
    kept = lots_to_me[3 * me + 2]
    step = FIRST
    at = iota((step, seq_len), 0)
    for base in range(-FIRST, rows.shape[0], step):
        valid = None if base < 0 else at + base < kept
        found, grad = 0.0, 0.0
        for side in range(2):
            hit = order[side : side + 1] - (FIRST + base) == at
            pick = ones_where(hit if valid is None else hit & valid)
            span = slice(side * seq_len, (side + 1) * seq_len)
            if base >= 0:
                found += dot32(pick, tokens[span])
            grad += dot32_t(grads[:, span], pick)
        if base >= 0:
            dealt_grad = 0.0
            for k, hand in ((1, hand1), (2, hand2), (3, hand3)):
                row, number = lots_to_me[3 * (me ^ k) + 1], lots_to_me[3 * (me ^ k) + 2]
                source = iota((step, CAP), 1)
                put = ones_where((iota((step, CAP), 0) + base - row == source) & (source < number))
                found += dot32(put, hand[:, :depth])
                dealt_grad += dot32(put, hand[:, depth:])
            grad += dealt_grad.T
            rows[base : base + step] = found.astype(BF16)
        grads_here[:, FIRST + base : FIRST + base + step] = grad[:rank_size] + grad[rank_size:]


def sums_kernel(slots, ids, *refs):
    del ids
    xs, gates, ups = refs[:slots], refs[slots : 2 * slots], refs[2 * slots : 3 * slots]
    gate_sum, up_sum = refs[3 * slots :]
    gate_sum[...] = sum(dot32(x[...], w[...]) for x, w in zip(xs, gates))
    up_sum[...] = sum(dot32(x[...], w[...]) for x, w in zip(xs, ups))


def sketch_kernel(table, lots_to_me, team_at, grads, act1, act2, out):
    me, size = team_at[0], lots_to_me[3 * TEAM]

    def product(grad, lane, act):
        parts = []
        for s in range(TEAM):
            rank, row, number = lots_to_me[3 * s], lots_to_me[3 * s + 1] + FIRST, lots_to_me[3 * s + 2]
            edge = jnp.clip(row + table[2 * s] - rank, row, row + number)
            own = (me == s) & (lane < FIRST)
            cut = table[2 * s]
            for low, high, early in ((row, edge, lane < cut), (edge, row + number, lane >= cut)):
                mine = ((lane >= low) & (lane < high)) | (own & early)
                parts.append(jnp.where(mine, grad, 0.0))
        return jnp.dot(
            jnp.concatenate(parts, axis=0), act, precision=lax.Precision.HIGHEST, preferred_element_type=F32
        )

    out[...] = product(grads[:, :FIRST], iota((1, FIRST), 1), act1[...])

    def step(chunk, carry):
        base = pl.multiple_of(chunk * FIRST, FIRST)
        act = act2[pl.ds(base, FIRST), :]
        act = jnp.where(iota(act.shape, 0) + base < size, act, 0.0)
        lane = iota((1, FIRST), 1) + base + FIRST
        out[...] += product(grads[:, pl.ds(base + FIRST, FIRST)], lane, act)
        return carry

    lax.fori_loop(0, (size + FIRST - 1) // FIRST, step, 0)


ANY = pl.BlockSpec(memory_space=pl.ANY)
VMEM = pl.BlockSpec(memory_space=pltpu.VMEM)
SMEM = pl.BlockSpec(memory_space=pltpu.SMEM)


def call(kernel, name, specs, out_shape, out_specs, *args):
    return pl.pallas_call(
        kernel, out_shape=out_shape, in_specs=specs, out_specs=out_specs, name=name,
        compiler_params=pltpu.CompilerParams(vmem_limit_bytes=32 * MIB),
    )(*args)


def weight_specs(ids, slots, depth, tile):
    deep = pl.Buffered(3)
    return [pl.BlockSpec((depth, tile), lambda j, s=s: (ids[s], j), pipeline_mode=deep) for s in slots] * 2


def tiled(rows, tile):
    return pl.BlockSpec((rows, tile), lambda j: (0, j))


def kernel_call(kernel, name, ids, operands, specs, out_shape, out_specs, scratch, flops, moved):
    return pl.pallas_call(
        kernel,
        in_specs=[SMEM] + specs, out_specs=out_specs, out_shape=out_shape, scratch_shapes=scratch, name=name,
        compiler_params=pltpu.CompilerParams(vmem_limit_bytes=32 * MIB),
        cost_estimate=pl.CostEstimate(flops=flops, bytes_accessed=moved, transcendentals=0),
    )(ids, *operands)


def sums_of(ids, slots, xs, gate_w, up_w, tile=256):
    (rows, depth), units, count = xs[0].shape, gate_w.shape[1], len(xs)
    steps = -(-units // tile)

    def kernel(ids, *refs):
        x_refs, (gate_w, up_w, gate_sum, up_sum) = refs[:count], refs[count:]

        def step(*tiles):
            gates, ups, (gate, up) = tiles[:count], tiles[count : 2 * count], tiles[2 * count :]
            gate[...] = sum(dot32(x[...], w[...]) for x, w in zip(x_refs, gates))
            up[...] = sum(dot32(x[...], w[...]) for x, w in zip(x_refs, ups))

        pltpu.emit_pipeline(
            step, grid=(steps,), in_specs=weight_specs(ids, slots, depth, tile), out_specs=[tiled(rows, tile)] * 2
        )(*[gate_w] * count, *[up_w] * count, gate_sum, up_sum)

    out = jax.ShapeDtypeStruct((rows, steps * tile), F32)
    return kernel_call(
        kernel, "sums", ids, [*xs, gate_w, up_w], [VMEM] * count + [ANY] * 2, (out, out), (ANY, ANY), (),
        4 * count * rows * depth * units, 4 * count * depth * units,
    )


def projected(ids, slots, xs, at_side, at_middle, sums, gate_w, up_w, proj_in, most, tile=256):
    (rows, depth), units, rank, count = at_side.shape, gate_w.shape[1], proj_in.shape[1], len(slots)
    steps = proj_in.shape[0] // tile

    def kernel(ids, at_side, at_middle, gate_w, up_w, proj, gate_sum, up_sum, *refs):
        x_refs, (act, x, gate, up) = refs[: count - 1], refs[count - 1 :]
        middle = (ids[0] == 1) | (ids[0] == 2)
        x[...] = jnp.where(middle, at_middle[...], at_side[...])
        act[:rows] = jnp.zeros((rows, rank), F32)

        half = -(-rows // 32) * 16
        chunks = [(at, min(half, rows - at)) for at in range(0, rows, half)]

        def hidden_of(j, chunk):
            span = pl.ds(*chunk)
            v = 0.5 * gate[span, :]
            hidden = (v + v * jnp.tanh(v)) * up[span, :]
            column = iota(hidden.shape, 1) + j * tile
            return jnp.where((column >= 0) & (column < units), hidden, 0.0).astype(BF16)

        def project(j, parts):
            at = pl.multiple_of(jnp.maximum(j, 0) * tile, tile)
            act[:rows] += dot32(jnp.concatenate(parts, axis=0), proj[pl.ds(at, tile), :])

        def step(*tiles):
            gates, ups, (gate_tile, up_tile) = tiles[:count], tiles[count : 2 * count], tiles[2 * count :]
            j = pl.program_id(0) - 1
            blocks = [*x_refs, x]
            new_gate, new_up, parts = gate_tile[...], up_tile[...], []
            for i, (block, weight, more) in enumerate(zip(blocks, gates, ups)):
                new_gate += dot32(block[...], weight[...])
                if i == 0:
                    parts.append(hidden_of(j, chunks[0]))
                new_up += dot32(block[...], more[...])
                if i == 0:
                    parts += [hidden_of(j, chunk) for chunk in chunks[1:]]
            project(j, parts)
            gate[...], up[...] = new_gate, new_up

        pltpu.emit_pipeline(
            step, grid=(steps,),
            in_specs=weight_specs(ids, slots, depth, tile) + [tiled(rows, tile)] * 2, out_specs=[],
        )(*[gate_w] * count, *[up_w] * count, gate_sum, up_sum)
        project(steps - 1, [hidden_of(steps - 1, chunk) for chunk in chunks])

    return kernel_call(
        kernel, "late", ids, [at_side, at_middle, gate_w, up_w, proj_in, *sums, *xs],
        [VMEM] * 2 + [ANY] * 2 + [VMEM] + [ANY] * 2 + [VMEM] * len(xs),
        jax.ShapeDtypeStruct((most, rank), F32), VMEM,
        [pltpu.VMEM((rows, depth), BF16)] + [pltpu.VMEM((rows, tile), F32)] * 2,
        4 * count * rows * depth * units, 4 * count * depth * units,
    )


MIDDLE, OUT = [(1, 2), (2, 1)], [(1, 0), (2, 3)]


def gathered(x):
    return lax.all_gather(x, "mp", axis=1, tiled=True)


def hop(x, pairs):
    return lax.ppermute(x, "mp", pairs)


def rest_case(size, ids, xs1, ends1, sums_own, rows, gate_w, up_w, proj_in):
    x = rows[:size]
    side, far = swap(x, "mp", 1), swap(x, "mp", 3)
    act1 = projected(ids, (1, 3, 2), xs1, *ends1, sums_own, gate_w, up_w, proj_in, FIRST)
    side, far, act1 = lax.optimization_barrier((side, far, act1))
    at_side, at_middle = hop(far, OUT), hop(side, MIDDLE)
    sums = sums_of(ids, (0, 1, 3), (x, side, far), gate_w, up_w)
    act2 = projected(ids, (2,), (), at_side, at_middle, sums, gate_w, up_w, proj_in, rows.shape[0])
    return act1, act2


def swap(x, axis, k, size=4):
    return lax.ppermute(x, axis, [(s, s ^ k) for s in range(size)])


def sketch_of_kept(tokens, grad_out, gate_w, up_w, proj_in, proj_out, lengths, loss_mask, queries):
    most, depth = tokens.shape
    rank = proj_in.shape[1]
    team_at = lax.axis_index("dp").astype(I32).reshape(1)
    order, cells, own1 = call(
        first_kernel, "first", [SMEM] * 2 + [VMEM] * 2,
        (
            jax.ShapeDtypeStruct(loss_mask.shape, I32),
            jax.ShapeDtypeStruct((8, 128), F32),
            jax.ShapeDtypeStruct((FIRST, depth), BF16),
        ),
        (VMEM,) * 3, team_at, lengths, loss_mask, tokens,
    )
    side1, far1 = swap(own1, "mp", 1), swap(own1, "mp", 3)
    me = lax.axis_index("mp").astype(I32)
    ids = jnp.stack([me, me ^ 1, me ^ 2, me ^ 3])
    grad_part = lax.dot_general(proj_out, grad_out, (((0,), (1,)), ((), ())), preferred_element_type=F32)
    high = lax.reduce_precision(grad_part, 8, 7)
    grads = jnp.concatenate([high.astype(BF16), (grad_part - high).astype(BF16)], axis=0)
    cells, grads = lax.optimization_barrier((cells, grads))
    cells = cells + swap(cells, "dp", 1) + swap(cells, "dp", 2) + swap(cells, "dp", 3)
    table = cells[:TEAM, :2].astype(I32).reshape(-1)
    sizes = sorted({s for s in SIZES if s < most - FIRST} | {most - FIRST})
    hand = jax.ShapeDtypeStruct((CAP, depth + 2 * rank), BF16)
    lots, *hands = call(
        functools.partial(deal_kernel, sizes), "deal", [SMEM] * 2 + [VMEM] * 3,
        (jax.ShapeDtypeStruct((3 * TEAM + 2,), I32),) + (hand,) * 3,
        (SMEM,) + (VMEM,) * 3, table, team_at, order, tokens, grads,
    )
    own1, *hands = lax.optimization_barrier((own1, *hands))
    hands = [swap(hand, "dp", k) for k, hand in zip((1, 2, 3), hands)]
    sums_own = sums_of(ids, (0,), (own1,), gate_w, up_w)
    side1, far1, sums_own = lax.optimization_barrier((side1, far1, sums_own))
    ends1 = hop(far1, OUT), hop(side1, MIDDLE)
    hands, side1, far1 = lax.optimization_barrier((hands, side1, far1))
    rows, grads = call(
        place_kernel, "place", [SMEM] * 2 + [VMEM] * 6,
        (
            jax.ShapeDtypeStruct((most - FIRST, depth), BF16),
            jax.ShapeDtypeStruct((rank, most), F32),
        ),
        (VMEM,) * 2, lots, team_at, order, tokens, grads, *hands,
    )
    queries, rows = lax.optimization_barrier((queries, rows))
    all_queries = lax.all_gather(queries, "dp", axis=0)
    grads = lax.psum(grads, "mp")
    padded = jnp.pad(proj_in, ((0, -proj_in.shape[0] % 256), (0, 0)))
    act1, act2 = lax.switch(
        lots[3 * TEAM + 1], [functools.partial(rest_case, s) for s in sizes],
        ids, (side1, far1), ends1, sums_own, rows, gate_w, up_w, padded,
    )
    parts = call(
        sketch_kernel, "sketch", [SMEM] * 3 + [VMEM] * 3, jax.ShapeDtypeStruct((2 * TEAM * rank, rank), F32),
        VMEM, table, lots, team_at, grads, act1, act2,
    )
    parts = parts.reshape(TEAM, 2 * rank, rank)
    me = team_at[0]
    part = lax.dynamic_index_in_dim(parts, me, 0, False)
    for k in (1, 2, 3):
        part = part + swap(lax.dynamic_index_in_dim(parts, me ^ k, 0, False), "dp", k)
    return part + swap(part, "mp", 1) + swap(part, "mp", 2) + swap(part, "mp", 3), all_queries


def sketch_in_general(tokens, grad_out, gate_w, up_w, proj_in, proj_out, lengths, loss_mask, queries):
    roll_count, seq_len = loss_mask.shape
    rank = proj_in.shape[1]
    keep = (jnp.arange(seq_len, dtype=I32)[None, :] < lengths[:, None]) & (loss_mask == 1)
    pieces = gathered(tokens)
    hidden = (jax.nn.silu(dot32(pieces, gate_w)) * dot32(pieces, up_w)).astype(BF16)
    stacked = jnp.concatenate([dot32(grad_out, proj_out), dot32(hidden, proj_in)], axis=1)
    summed = lax.psum(stacked, "mp").reshape(roll_count, seq_len, 2 * rank)
    weighted = summed[:, :, :rank] * keep.astype(F32)[:, :, None]
    sums = jnp.einsum("rti,rtj->rij", weighted, summed[:, :, rank:], precision=lax.Precision.HIGHEST)
    return sums, lax.all_gather(queries, "dp", axis=0)


def local(team, planes, tokens, grad_out, gate_w, up_w, proj_in, proj_out, lengths, loss_mask, queries):
    roll_count, seq_len = loss_mask.shape
    fits = team == TEAM and planes == PLANES and roll_count == 2 and seq_len % 256 == 0
    fits = fits and tokens.shape[1] % 128 == 0 and gate_w.shape[1] % 128 == 0 and proj_in.shape[1] == 64
    form = sketch_of_kept if fits else sketch_in_general
    sketch_sum, all_queries = form(
        tokens, grad_out, gate_w, up_w, proj_in, proj_out, lengths, loss_mask, queries
    )
    norm_factor = 1.0 / jnp.sqrt(jnp.float32(seq_len))
    sketch = (sketch_sum.reshape(roll_count, team, -1) * norm_factor).astype(BF16)
    return jnp.einsum("rdk,dqk->rq", sketch, all_queries, preferred_element_type=F32)


def solution(mesh):
    placed = (
        P(("groups", "dp"), "mp"),
        P(("groups", "dp"), "mp"),
        P(None, "mp"),
        P(None, "mp"),
        P("mp", None),
        P("mp", None),
        P(("groups", "dp")),
        P(("groups", "dp"), None),
        P("mp", "dp"),
    )
    return jax.shard_map(
        functools.partial(local, mesh.shape["dp"], mesh.shape["mp"]),
        mesh=mesh, in_specs=placed, out_specs=P(("groups", "dp"), "mp"), check_vma=False,
    )
```

```python
import functools

import jax
import jax.numpy as jnp
from jax import lax
from jax.experimental import pallas as pl
from jax.experimental.pallas import tpu as pltpu
from jax.sharding import PartitionSpec as P

BF16, F32, I32 = jnp.bfloat16, jnp.float32, jnp.int32
FIRST = 256
SIZES = (160, 208, 256, 304, 400)
CAP = 192
TEAM = 4
PLANES = 4
TILE = 256
MIB = 2**20


def dot32(a, b):
    return jnp.dot(a, b, preferred_element_type=F32)


def dot32_t(a, b):
    return lax.dot_general(a, b, (((1,), (1,)), ((), ())), preferred_element_type=F32)


def iota(shape, axis):
    return lax.broadcasted_iota(I32, shape, axis)


def ones_where(cond):
    return jnp.where(cond, 1.0, 0.0).astype(BF16)


def dealt(rest, most):
    keep = [jnp.minimum(m, most) for m in rest]
    spare_at, room_at, a, b = [], [], 0, 0
    for m, k in zip(rest, keep):
        spare_at.append(a)
        room_at.append(b)
        a, b = a + (m - k), b + (most - k)
    start, moved = {}, {}
    for s in range(TEAM):
        for t in range(TEAM):
            if s != t:
                low = jnp.maximum(spare_at[s], room_at[t])
                high = jnp.minimum(spare_at[s] + rest[s] - keep[s], room_at[t] + most - keep[t])
                start[s, t], moved[s, t] = low, jnp.maximum(high - low, 0)
    return keep, spare_at, room_at, start, moved


def plan(table):
    rest = [jnp.maximum(table[2 * s + 1] - FIRST, 0) for s in range(TEAM)]
    even = (rest[0] + rest[1] + rest[2] + rest[3] + (TEAM - 1)) // TEAM
    most = functools.reduce(jnp.maximum, rest)
    for tried in ((3 * most + even) // 4, (most + even) // 2, even):
        largest = functools.reduce(jnp.maximum, dealt(rest, tried)[4].values())
        most = jnp.where(largest <= CAP, tried, most)
    keep, spare_at, room_at, start, moved = dealt(rest, most)
    lots = {}
    for s in range(TEAM):
        lots[s, s] = (FIRST, 0, keep[s])
        for t in range(TEAM):
            if s != t:
                rank = FIRST + keep[s] + start[s, t] - spare_at[s]
                lots[s, t] = (rank, keep[t] + start[s, t] - room_at[t], moved[s, t])
    return most, lots


def chosen(lots, pairs):
    out = [0, 0, 0]
    for cond, pair in pairs:
        out = [jnp.where(cond, new, old) for new, old in zip(lots[pair], out)]
    return out


def first_kernel(team_at, lengths, loss_mask, tokens, order, table, rows):
    seq_len = loss_mask.shape[1]
    limit = jnp.where(iota(loss_mask.shape, 0) == 0, lengths[0], lengths[1])
    keep = (iota(loss_mask.shape, 1) < limit) & (loss_mask[...] == 1)
    upto = ones_where(iota((seq_len, seq_len), 0) <= iota((seq_len, seq_len), 1))
    kept = jnp.where(keep, 1.0, 0.0)
    place = dot32(kept.astype(BF16), upto)
    before = jnp.sum(kept[0:1], axis=1, keepdims=True)
    total = before + jnp.sum(kept[1:2], axis=1, keepdims=True)
    place = place - 1.0 + jnp.where(iota(place.shape, 0) == 0, 0.0, before)
    ranks = jnp.where(keep, place, -1.0).astype(I32)
    order[...] = ranks
    cell = jnp.where(iota(table.shape, 1) == 0, before, total)
    table[...] = jnp.where(iota(table.shape, 0) == team_at[0], cell, 0.0)
    at = iota((FIRST, seq_len), 0)
    found = dot32(ones_where(ranks[0:1] == at), tokens[:seq_len])
    found += dot32(ones_where(ranks[1:2] == at), tokens[seq_len:])
    rows[...] = found.astype(BF16)


def deal_kernel(sizes, table, team_at, order, tokens, grads, lots_to_me, *hands):
    me, seq_len = team_at[0], order.shape[1]
    most, lots = plan(table)
    lots_to_me[3 * TEAM] = most
    lots_to_me[3 * TEAM + 1] = sum((most > size).astype(I32) for size in sizes[:-1])
    for s in range(TEAM):
        for i, value in enumerate(chosen(lots, [(me == t, (s, t)) for t in range(TEAM)])):
            lots_to_me[3 * s + i] = value
    depth = tokens.shape[1]
    at = iota((CAP, seq_len), 0)
    for k, hand in zip(range(1, TEAM), hands):
        rank, _, number = chosen(lots, [(me == s, (s, s ^ k)) for s in range(TEAM)])
        valid = at < number
        for side in range(2):
            pick = ones_where((order[side : side + 1] - rank == at) & valid)
            span = slice(side * seq_len, (side + 1) * seq_len)
            found, grad = dot32(pick, tokens[span]), dot32_t(pick, grads[:, span])
            if side == 0:
                hand[:, :depth], hand[:, depth:] = found.astype(BF16), grad.astype(BF16)
            else:
                hand[:, :depth] += found.astype(BF16)
                hand[:, depth:] += grad.astype(BF16)


def place_kernel(lots_to_me, team_at, order, tokens, grads, hand1, hand2, hand3, rows, grads_here):
    me, seq_len = team_at[0], order.shape[1]
    depth, rank_size = tokens.shape[1], grads_here.shape[0]
    kept = lots_to_me[3 * me + 2]
    step = FIRST
    at = iota((step, seq_len), 0)
    for base in range(-FIRST, rows.shape[0], step):
        valid = None if base < 0 else at + base < kept
        found, grad = 0.0, 0.0
        for side in range(2):
            hit = order[side : side + 1] - (FIRST + base) == at
            pick = ones_where(hit if valid is None else hit & valid)
            span = slice(side * seq_len, (side + 1) * seq_len)
            if base >= 0:
                found += dot32(pick, tokens[span])
            grad += dot32_t(grads[:, span], pick)
        if base >= 0:
            dealt_grad = 0.0
            for k, hand in ((1, hand1), (2, hand2), (3, hand3)):
                row, number = lots_to_me[3 * (me ^ k) + 1], lots_to_me[3 * (me ^ k) + 2]
                source = iota((step, CAP), 1)
                put = ones_where((iota((step, CAP), 0) + base - row == source) & (source < number))
                found += dot32(put, hand[:, :depth])
                dealt_grad += dot32(put, hand[:, depth:])
            grad += dealt_grad.T
            rows[base : base + step] = found.astype(BF16)
        grads_here[:, FIRST + base : FIRST + base + step] = grad[:rank_size] + grad[rank_size:]


def sums_kernel(slots, ids, *refs):
    del ids
    xs, gates, ups = refs[:slots], refs[slots : 2 * slots], refs[2 * slots : 3 * slots]
    gate_sum, up_sum = refs[3 * slots :]
    gate_sum[...] = sum(dot32(x[...], w[...]) for x, w in zip(xs, gates))
    up_sum[...] = sum(dot32(x[...], w[...]) for x, w in zip(xs, ups))


def sketch_kernel(table, lots_to_me, team_at, grads, act1, act2, out):
    me, size = team_at[0], lots_to_me[3 * TEAM]

    def product(grad, lane, act):
        parts = []
        for s in range(TEAM):
            rank, row, number = lots_to_me[3 * s], lots_to_me[3 * s + 1] + FIRST, lots_to_me[3 * s + 2]
            edge = jnp.clip(row + table[2 * s] - rank, row, row + number)
            own = (me == s) & (lane < FIRST)
            cut = table[2 * s]
            for low, high, early in ((row, edge, lane < cut), (edge, row + number, lane >= cut)):
                mine = ((lane >= low) & (lane < high)) | (own & early)
                parts.append(jnp.where(mine, grad, 0.0))
        return jnp.dot(
            jnp.concatenate(parts, axis=0), act, precision=lax.Precision.HIGHEST, preferred_element_type=F32
        )

    out[...] = product(grads[:, :FIRST], iota((1, FIRST), 1), act1[...])

    def step(chunk, carry):
        base = pl.multiple_of(chunk * FIRST, FIRST)
        act = act2[pl.ds(base, FIRST), :]
        act = jnp.where(iota(act.shape, 0) + base < size, act, 0.0)
        lane = iota((1, FIRST), 1) + base + FIRST
        out[...] += product(grads[:, pl.ds(base + FIRST, FIRST)], lane, act)
        return carry

    lax.fori_loop(0, (size + FIRST - 1) // FIRST, step, 0)


ANY = pl.BlockSpec(memory_space=pl.ANY)
VMEM = pl.BlockSpec(memory_space=pltpu.VMEM)
SMEM = pl.BlockSpec(memory_space=pltpu.SMEM)


def call(kernel, name, specs, out_shape, out_specs, *args):
    return pl.pallas_call(
        kernel, out_shape=out_shape, in_specs=specs, out_specs=out_specs, name=name,
        compiler_params=pltpu.CompilerParams(vmem_limit_bytes=32 * MIB),
    )(*args)


def weight_specs(ids, slots, depth, tile):
    deep = pl.Buffered(2 if len(slots) > 1 else 3)
    return [pl.BlockSpec((depth, tile), lambda j, s=s: (ids[s], j), pipeline_mode=deep) for s in slots] * 2


def tiled(rows, tile):
    return pl.BlockSpec((rows, tile), lambda j: (0, j))


def kernel_call(kernel, name, ids, operands, specs, out_shape, out_specs, scratch, flops, moved):
    return pl.pallas_call(
        kernel,
        in_specs=[SMEM] + specs, out_specs=out_specs, out_shape=out_shape, scratch_shapes=scratch, name=name,
        compiler_params=pltpu.CompilerParams(vmem_limit_bytes=38 * MIB),
        cost_estimate=pl.CostEstimate(flops=flops, bytes_accessed=moved, transcendentals=0),
    )(ids, *operands)


def halves(tile, body):
    def step(part, carry):
        body(part, pl.ds(pl.multiple_of(part * TILE, TILE), TILE))
        return carry

    lax.fori_loop(0, tile // TILE, step, 0)


def sums_of(ids, slots, xs, gate_w, up_w, tile=2 * TILE):
    (rows, depth), units, count = xs[0].shape, gate_w.shape[1], len(xs)
    steps = -(-units // tile)

    def kernel(ids, *refs):
        x_refs, (gate_w, up_w, gate_sum, up_sum) = refs[:count], refs[count:]

        def step(*tiles):
            gates, ups, (gate, up) = tiles[:count], tiles[count : 2 * count], tiles[2 * count :]

            def part(_, span):
                gate[:, span] = sum(dot32(x[...], w[:, span]) for x, w in zip(x_refs, gates))
                up[:, span] = sum(dot32(x[...], w[:, span]) for x, w in zip(x_refs, ups))

            halves(tile, part)

        pltpu.emit_pipeline(
            step, grid=(steps,), in_specs=weight_specs(ids, slots, depth, tile), out_specs=[tiled(rows, tile)] * 2
        )(*[gate_w] * count, *[up_w] * count, gate_sum, up_sum)

    out = jax.ShapeDtypeStruct((rows, steps * tile), F32)
    return kernel_call(
        kernel, "sums", ids, [*xs, gate_w, up_w], [VMEM] * count + [ANY] * 2, (out, out), (ANY, ANY), (),
        4 * count * rows * depth * units, 4 * count * depth * units,
    )


def projected(ids, slots, xs, at_side, at_middle, sums, gate_w, up_w, proj_in, most, tile=2 * TILE):
    (rows, depth), units, rank, count = at_side.shape, gate_w.shape[1], proj_in.shape[1], len(slots)
    steps, last = proj_in.shape[0] // tile, proj_in.shape[0] // TILE - 1

    def kernel(ids, at_side, at_middle, gate_w, up_w, proj, gate_sum, up_sum, *refs):
        x_refs, (act, x, gate, up) = refs[: count - 1], refs[count - 1 :]
        middle = (ids[0] == 1) | (ids[0] == 2)
        x[...] = jnp.where(middle, at_middle[...], at_side[...])
        act[:rows] = jnp.zeros((rows, rank), F32)

        half = -(-rows // 32) * 16
        chunks = [(at, min(half, rows - at)) for at in range(0, rows, half)]

        def hidden_of(j, chunk):
            span = pl.ds(*chunk)
            v = 0.5 * gate[span, :]
            hidden = (v + v * jnp.tanh(v)) * up[span, :]
            column = iota(hidden.shape, 1) + j * TILE
            return jnp.where((column >= 0) & (column < units), hidden, 0.0).astype(BF16)

        def project(j, parts):
            at = pl.multiple_of(jnp.maximum(j, 0) * TILE, TILE)
            act[:rows] += dot32(jnp.concatenate(parts, axis=0), proj[pl.ds(at, TILE), :])

        def step(*tiles):
            gates, ups, (gate_tile, up_tile) = tiles[:count], tiles[count : 2 * count], tiles[2 * count :]
            first = pl.program_id(0) * (tile // TILE) - 1
            blocks = [*x_refs, x]

            def part(i, span):
                parts = [hidden_of(first + i, chunk) for chunk in chunks]
                new_gate = sum((dot32(b[...], w[:, span]) for b, w in zip(blocks, gates)), gate_tile[:, span])
                new_up = sum((dot32(b[...], w[:, span]) for b, w in zip(blocks, ups)), up_tile[:, span])
                project(first + i, parts)
                gate[...], up[...] = new_gate, new_up

            halves(tile, part)

        pltpu.emit_pipeline(
            step, grid=(steps,),
            in_specs=weight_specs(ids, slots, depth, tile) + [tiled(rows, tile)] * 2, out_specs=[],
        )(*[gate_w] * count, *[up_w] * count, gate_sum, up_sum)
        project(last, [hidden_of(last, chunk) for chunk in chunks])

    return kernel_call(
        kernel, "late", ids, [at_side, at_middle, gate_w, up_w, proj_in, *sums, *xs],
        [VMEM] * 2 + [ANY] * 2 + [VMEM] + [ANY] * 2 + [VMEM] * len(xs),
        jax.ShapeDtypeStruct((most, rank), F32), VMEM,
        [pltpu.VMEM((rows, depth), BF16)] + [pltpu.VMEM((rows, TILE), F32)] * 2,
        4 * count * rows * depth * units, 4 * count * depth * units,
    )


MIDDLE, OUT = [(1, 2), (2, 1)], [(1, 0), (2, 3)]


def gathered(x):
    return lax.all_gather(x, "mp", axis=1, tiled=True)


def hop(x, pairs):
    return lax.ppermute(x, "mp", pairs)


def rest_case(size, ids, xs1, ends1, sums_own, rows, gate_w, up_w, proj_in):
    x = rows[:size]
    side, far = swap(x, "mp", 1), swap(x, "mp", 3)
    act1 = projected(ids, (1, 3, 2), xs1, *ends1, sums_own, gate_w, up_w, proj_in, FIRST)
    side, far, act1 = lax.optimization_barrier((side, far, act1))
    at_side, at_middle = hop(far, OUT), hop(side, MIDDLE)
    sums = sums_of(ids, (0, 1, 3), (x, side, far), gate_w, up_w)
    act2 = projected(ids, (2,), (), at_side, at_middle, sums, gate_w, up_w, proj_in, rows.shape[0])
    return act1, act2


def swap(x, axis, k, size=4):
    return lax.ppermute(x, axis, [(s, s ^ k) for s in range(size)])


def sketch_of_kept(tokens, grad_out, gate_w, up_w, proj_in, proj_out, lengths, loss_mask, queries):
    most, depth = tokens.shape
    rank = proj_in.shape[1]
    team_at = lax.axis_index("dp").astype(I32).reshape(1)
    order, cells, own1 = call(
        first_kernel, "first", [SMEM] * 2 + [VMEM] * 2,
        (
            jax.ShapeDtypeStruct(loss_mask.shape, I32),
            jax.ShapeDtypeStruct((8, 128), F32),
            jax.ShapeDtypeStruct((FIRST, depth), BF16),
        ),
        (VMEM,) * 3, team_at, lengths, loss_mask, tokens,
    )
    queries = lax.optimization_barrier((queries, own1))[0]
    all_queries = lax.all_gather(queries, "dp", axis=0)
    side1, far1 = swap(own1, "mp", 1), swap(own1, "mp", 3)
    me = lax.axis_index("mp").astype(I32)
    ids = jnp.stack([me, me ^ 1, me ^ 2, me ^ 3])
    grad_part = lax.dot_general(proj_out, grad_out, (((0,), (1,)), ((), ())), preferred_element_type=F32)
    high = lax.reduce_precision(grad_part, 8, 7)
    grads = jnp.concatenate([high.astype(BF16), (grad_part - high).astype(BF16)], axis=0)
    cells, grads = lax.optimization_barrier((cells, grads))
    cells = cells + swap(cells, "dp", 1) + swap(cells, "dp", 2) + swap(cells, "dp", 3)
    table = cells[:TEAM, :2].astype(I32).reshape(-1)
    sizes = sorted({s for s in SIZES if s < most - FIRST} | {most - FIRST})
    hand = jax.ShapeDtypeStruct((CAP, depth + 2 * rank), BF16)
    lots, *hands = call(
        functools.partial(deal_kernel, sizes), "deal", [SMEM] * 2 + [VMEM] * 3,
        (jax.ShapeDtypeStruct((3 * TEAM + 2,), I32),) + (hand,) * 3,
        (SMEM,) + (VMEM,) * 3, table, team_at, order, tokens, grads,
    )
    own1, *hands = lax.optimization_barrier((own1, *hands))
    hands = [swap(hand, "dp", k) for k, hand in zip((1, 2, 3), hands)]
    sums_own = sums_of(ids, (0,), (own1,), gate_w, up_w)
    side1, far1, sums_own = lax.optimization_barrier((side1, far1, sums_own))
    ends1 = hop(far1, OUT), hop(side1, MIDDLE)
    hands, side1, far1 = lax.optimization_barrier((hands, side1, far1))
    rows, grads = call(
        place_kernel, "place", [SMEM] * 2 + [VMEM] * 6,
        (
            jax.ShapeDtypeStruct((most - FIRST, depth), BF16),
            jax.ShapeDtypeStruct((rank, most), F32),
        ),
        (VMEM,) * 2, lots, team_at, order, tokens, grads, *hands,
    )
    rows, all_queries = lax.optimization_barrier((rows, all_queries))
    grads = lax.psum(grads, "mp")
    padded = jnp.pad(proj_in, ((0, -proj_in.shape[0] % (2 * TILE)), (0, 0)))
    act1, act2 = lax.switch(
        lots[3 * TEAM + 1], [functools.partial(rest_case, s) for s in sizes],
        ids, (side1, far1), ends1, sums_own, rows, gate_w, up_w, padded,
    )
    parts = call(
        sketch_kernel, "sketch", [SMEM] * 3 + [VMEM] * 3, jax.ShapeDtypeStruct((2 * TEAM * rank, rank), F32),
        VMEM, table, lots, team_at, grads, act1, act2,
    )
    parts = parts.reshape(TEAM, 2 * rank, rank)
    me = team_at[0]
    part = lax.dynamic_index_in_dim(parts, me, 0, False)
    for k in (1, 2, 3):
        part = part + swap(lax.dynamic_index_in_dim(parts, me ^ k, 0, False), "dp", k)
    return part + swap(part, "mp", 1) + swap(part, "mp", 2) + swap(part, "mp", 3), all_queries


def sketch_in_general(tokens, grad_out, gate_w, up_w, proj_in, proj_out, lengths, loss_mask, queries):
    roll_count, seq_len = loss_mask.shape
    rank = proj_in.shape[1]
    keep = (jnp.arange(seq_len, dtype=I32)[None, :] < lengths[:, None]) & (loss_mask == 1)
    pieces = gathered(tokens)
    hidden = (jax.nn.silu(dot32(pieces, gate_w)) * dot32(pieces, up_w)).astype(BF16)
    stacked = jnp.concatenate([dot32(grad_out, proj_out), dot32(hidden, proj_in)], axis=1)
    summed = lax.psum(stacked, "mp").reshape(roll_count, seq_len, 2 * rank)
    weighted = summed[:, :, :rank] * keep.astype(F32)[:, :, None]
    sums = jnp.einsum("rti,rtj->rij", weighted, summed[:, :, rank:], precision=lax.Precision.HIGHEST)
    return sums, lax.all_gather(queries, "dp", axis=0)


def local(team, planes, tokens, grad_out, gate_w, up_w, proj_in, proj_out, lengths, loss_mask, queries):
    roll_count, seq_len = loss_mask.shape
    fits = team == TEAM and planes == PLANES and roll_count == 2 and seq_len % 256 == 0
    fits = fits and tokens.shape[1] % 128 == 0 and gate_w.shape[1] % 128 == 0 and proj_in.shape[1] == 64
    form = sketch_of_kept if fits else sketch_in_general
    sketch_sum, all_queries = form(
        tokens, grad_out, gate_w, up_w, proj_in, proj_out, lengths, loss_mask, queries
    )
    norm_factor = 1.0 / jnp.sqrt(jnp.float32(seq_len))
    sketch = (sketch_sum.reshape(roll_count, team, -1) * norm_factor).astype(BF16)
    return jnp.einsum("rdk,dqk->rq", sketch, all_queries, preferred_element_type=F32)


def solution(mesh):
    placed = (
        P(("groups", "dp"), "mp"),
        P(("groups", "dp"), "mp"),
        P(None, "mp"),
        P(None, "mp"),
        P("mp", None),
        P("mp", None),
        P(("groups", "dp")),
        P(("groups", "dp"), None),
        P("mp", "dp"),
    )
    return jax.shard_map(
        functools.partial(local, mesh.shape["dp"], mesh.shape["mp"]),
        mesh=mesh, in_specs=placed, out_specs=P(("groups", "dp"), "mp"), check_vma=False,
    )
```

```python
import functools

import jax
import jax.numpy as jnp
from jax import lax
from jax.experimental import pallas as pl
from jax.experimental.pallas import tpu as pltpu
from jax.sharding import PartitionSpec as P

BF16, F32, I32 = jnp.bfloat16, jnp.float32, jnp.int32
FIRST = 256
SIZES = (176, 208, 240, 272, 320, 400)
CAP = 192
TEAM = 4
PLANES = 4
TILE = 256
MIB = 2**20


def dot32(a, b):
    return jnp.dot(a, b, preferred_element_type=F32)


def dot32_t(a, b):
    return lax.dot_general(a, b, (((1,), (1,)), ((), ())), preferred_element_type=F32)


def iota(shape, axis):
    return lax.broadcasted_iota(I32, shape, axis)


def ones_where(cond):
    return jnp.where(cond, 1.0, 0.0).astype(BF16)


def dealt(rest, most):
    keep = [jnp.minimum(m, most) for m in rest]
    spare_at, room_at, a, b = [], [], 0, 0
    for m, k in zip(rest, keep):
        spare_at.append(a)
        room_at.append(b)
        a, b = a + (m - k), b + (most - k)
    start, moved = {}, {}
    for s in range(TEAM):
        for t in range(TEAM):
            if s != t:
                low = jnp.maximum(spare_at[s], room_at[t])
                high = jnp.minimum(spare_at[s] + rest[s] - keep[s], room_at[t] + most - keep[t])
                start[s, t], moved[s, t] = low, jnp.maximum(high - low, 0)
    return keep, spare_at, room_at, start, moved


def plan(table):
    rest = [jnp.maximum(table[2 * s + 1] - FIRST, 0) for s in range(TEAM)]
    even = (rest[0] + rest[1] + rest[2] + rest[3] + (TEAM - 1)) // TEAM
    most = functools.reduce(jnp.maximum, rest)
    for tried in ((3 * most + even) // 4, (most + even) // 2, even):
        largest = functools.reduce(jnp.maximum, dealt(rest, tried)[4].values())
        most = jnp.where(largest <= CAP, tried, most)
    keep, spare_at, room_at, start, moved = dealt(rest, most)
    lots = {}
    for s in range(TEAM):
        lots[s, s] = (FIRST, 0, keep[s])
        for t in range(TEAM):
            if s != t:
                rank = FIRST + keep[s] + start[s, t] - spare_at[s]
                lots[s, t] = (rank, keep[t] + start[s, t] - room_at[t], moved[s, t])
    return most, lots


def chosen(lots, pairs):
    out = [0, 0, 0]
    for cond, pair in pairs:
        out = [jnp.where(cond, new, old) for new, old in zip(lots[pair], out)]
    return out


def first_kernel(team_at, lengths, loss_mask, tokens, order, table, rows):
    seq_len = loss_mask.shape[1]
    limit = jnp.where(iota(loss_mask.shape, 0) == 0, lengths[0], lengths[1])
    keep = (iota(loss_mask.shape, 1) < limit) & (loss_mask[...] == 1)
    upto = ones_where(iota((seq_len, seq_len), 0) <= iota((seq_len, seq_len), 1))
    kept = jnp.where(keep, 1.0, 0.0)
    place = dot32(kept.astype(BF16), upto)
    before = jnp.sum(kept[0:1], axis=1, keepdims=True)
    total = before + jnp.sum(kept[1:2], axis=1, keepdims=True)
    place = place - 1.0 + jnp.where(iota(place.shape, 0) == 0, 0.0, before)
    ranks = jnp.where(keep, place, -1.0).astype(I32)
    order[...] = ranks
    cell = jnp.where(iota(table.shape, 1) == 0, before, total)
    table[...] = jnp.where(iota(table.shape, 0) == team_at[0], cell, 0.0)
    at = iota((FIRST, seq_len), 0)
    found = dot32(ones_where(ranks[0:1] == at), tokens[:seq_len])
    found += dot32(ones_where(ranks[1:2] == at), tokens[seq_len:])
    rows[...] = found.astype(BF16)


def deal_kernel(sizes, table, team_at, order, tokens, grads, lots_to_me, *hands):
    me, seq_len = team_at[0], order.shape[1]
    most, lots = plan(table)
    lots_to_me[3 * TEAM] = most
    lots_to_me[3 * TEAM + 1] = sum((most > size).astype(I32) for size in sizes[:-1])
    for s in range(TEAM):
        for i, value in enumerate(chosen(lots, [(me == t, (s, t)) for t in range(TEAM)])):
            lots_to_me[3 * s + i] = value
    depth = tokens.shape[1]
    at = iota((CAP, seq_len), 0)
    for k, hand in zip(range(1, TEAM), hands):
        rank, _, number = chosen(lots, [(me == s, (s, s ^ k)) for s in range(TEAM)])
        valid = at < number
        for side in range(2):
            pick = ones_where((order[side : side + 1] - rank == at) & valid)
            span = slice(side * seq_len, (side + 1) * seq_len)
            found, grad = dot32(pick, tokens[span]), dot32_t(pick, grads[:, span])
            if side == 0:
                hand[:, :depth], hand[:, depth:] = found.astype(BF16), grad.astype(BF16)
            else:
                hand[:, :depth] += found.astype(BF16)
                hand[:, depth:] += grad.astype(BF16)


def place_kernel(lots_to_me, team_at, order, tokens, grads, hand1, hand2, hand3, rows, grads_here):
    me, seq_len = team_at[0], order.shape[1]
    depth, rank_size = tokens.shape[1], grads_here.shape[0]
    kept, size = lots_to_me[3 * me + 2], lots_to_me[3 * TEAM]
    at = iota((FIRST, seq_len), 0)

    def picked(base, valid):
        hits = [order[side : side + 1] - base == at for side in range(2)]
        return [ones_where(hit if valid is None else hit & valid) for hit in hits]

    def grad_of(picks):
        return dot32_t(grads[:, :seq_len], picks[0]) + dot32_t(grads[:, seq_len:], picks[1])

    grad = grad_of(picked(0, None))
    grads_here[:, :FIRST] = grad[:rank_size] + grad[rank_size:]

    def block(i, carry):
        base = pl.multiple_of(i * FIRST, FIRST)
        picks = picked(base + FIRST, at + base < kept)
        found = dot32(picks[0], tokens[:seq_len]) + dot32(picks[1], tokens[seq_len:])
        source, target = iota((FIRST, CAP), 1), iota((FIRST, CAP), 0) + base
        dealt_grad = 0.0
        for k, hand in ((1, hand1), (2, hand2), (3, hand3)):
            row, number = lots_to_me[3 * (me ^ k) + 1], lots_to_me[3 * (me ^ k) + 2]
            put = ones_where((target - row == source) & (source < number))
            found += dot32(put, hand[:, :depth])
            dealt_grad += dot32(put, hand[:, depth:])
        grad = grad_of(picks) + dealt_grad.T
        rows[pl.ds(base, FIRST), :] = found.astype(BF16)
        grads_here[:, pl.ds(base + FIRST, FIRST)] = grad[:rank_size] + grad[rank_size:]
        return carry

    lax.fori_loop(0, (size + FIRST - 1) // FIRST, block, 0)


def sketch_kernel(table, lots_to_me, team_at, grads, act1, act2, out):
    me, size = team_at[0], lots_to_me[3 * TEAM]

    def product(grad, lane, act):
        parts = []
        for s in range(TEAM):
            rank, row, number = lots_to_me[3 * s], lots_to_me[3 * s + 1] + FIRST, lots_to_me[3 * s + 2]
            edge = jnp.clip(row + table[2 * s] - rank, row, row + number)
            own = (me == s) & (lane < FIRST)
            cut = table[2 * s]
            for low, high, early in ((row, edge, lane < cut), (edge, row + number, lane >= cut)):
                mine = ((lane >= low) & (lane < high)) | (own & early)
                parts.append(jnp.where(mine, grad, 0.0))
        return jnp.dot(
            jnp.concatenate(parts, axis=0), act, precision=lax.Precision.HIGHEST, preferred_element_type=F32
        )

    out[...] = product(grads[:, :FIRST], iota((1, FIRST), 1), act1[...])

    def step(chunk, carry):
        base = pl.multiple_of(chunk * FIRST, FIRST)
        act = act2[pl.ds(base, FIRST), :]
        act = jnp.where(iota(act.shape, 0) + base < size, act, 0.0)
        lane = iota((1, FIRST), 1) + base + FIRST
        out[...] += product(grads[:, pl.ds(base + FIRST, FIRST)], lane, act)
        return carry

    lax.fori_loop(0, (size + FIRST - 1) // FIRST, step, 0)


ANY = pl.BlockSpec(memory_space=pl.ANY)
VMEM = pl.BlockSpec(memory_space=pltpu.VMEM)
SMEM = pl.BlockSpec(memory_space=pltpu.SMEM)


def call(kernel, name, specs, out_shape, out_specs, *args):
    return pl.pallas_call(
        kernel, out_shape=out_shape, in_specs=specs, out_specs=out_specs, name=name,
        compiler_params=pltpu.CompilerParams(vmem_limit_bytes=32 * MIB),
    )(*args)


def weight_specs(ids, slots, depth, tile):
    deep = pl.Buffered(2 if len(slots) > 1 and tile > TILE else 3)
    return [pl.BlockSpec((depth, tile), lambda j, s=s: (ids[s], j), pipeline_mode=deep) for s in slots] * 2


def tiled(rows, tile):
    return pl.BlockSpec((rows, tile), lambda j: (0, j))


def kernel_call(kernel, name, ids, operands, specs, out_shape, out_specs, scratch, flops, moved):
    return pl.pallas_call(
        kernel,
        in_specs=[SMEM] + specs, out_specs=out_specs, out_shape=out_shape, scratch_shapes=scratch, name=name,
        compiler_params=pltpu.CompilerParams(vmem_limit_bytes=38 * MIB),
        cost_estimate=pl.CostEstimate(flops=flops, bytes_accessed=moved, transcendentals=0),
    )(ids, *operands)


def halves(tile, body):
    def step(part, carry):
        body(part, pl.ds(pl.multiple_of(part * TILE, TILE), TILE))
        return carry

    lax.fori_loop(0, tile // TILE, step, 0)


def sums_of(ids, slots, xs, gate_w, up_w, tile=TILE):
    (rows, depth), units, count = xs[0].shape, gate_w.shape[1], len(xs)
    steps = -(-units // tile)

    def kernel(ids, *refs):
        x_refs, (gate_w, up_w, gate_sum, up_sum) = refs[:count], refs[count:]

        def step(*tiles):
            gates, ups, (gate, up) = tiles[:count], tiles[count : 2 * count], tiles[2 * count :]
            gate[...] = sum(dot32(x[...], w[...]) for x, w in zip(x_refs, gates))
            up[...] = sum(dot32(x[...], w[...]) for x, w in zip(x_refs, ups))

        pltpu.emit_pipeline(
            step, grid=(steps,), in_specs=weight_specs(ids, slots, depth, tile), out_specs=[tiled(rows, tile)] * 2
        )(*[gate_w] * count, *[up_w] * count, gate_sum, up_sum)

    out = jax.ShapeDtypeStruct((rows, steps * tile), F32)
    return kernel_call(
        kernel, "sums", ids, [*xs, gate_w, up_w], [VMEM] * count + [ANY] * 2, (out, out), (ANY, ANY), (),
        4 * count * rows * depth * units, 4 * count * depth * units,
    )


def projected(ids, slots, xs, at_side, at_middle, sums, gate_w, up_w, proj_in, most, tile=2 * TILE):
    (rows, depth), units, rank, count = at_side.shape, gate_w.shape[1], proj_in.shape[1], len(slots)
    steps, last = proj_in.shape[0] // tile, proj_in.shape[0] // TILE - 1

    def kernel(ids, at_side, at_middle, gate_w, up_w, proj, gate_sum, up_sum, *refs):
        x_refs, (act, x, gate, up) = refs[: count - 1], refs[count - 1 :]
        middle = (ids[0] == 1) | (ids[0] == 2)
        x[...] = jnp.where(middle, at_middle[...], at_side[...])
        act[:rows] = jnp.zeros((rows, rank), F32)

        half = -(-rows // 32) * 16
        chunks = [(at, min(half, rows - at)) for at in range(0, rows, half)]

        def hidden_of(j, chunk):
            span = pl.ds(*chunk)
            v = 0.5 * gate[span, :]
            hidden = (v + v * jnp.tanh(v)) * up[span, :]
            column = iota(hidden.shape, 1) + j * TILE
            return jnp.where((column >= 0) & (column < units), hidden, 0.0).astype(BF16)

        def project(j, parts):
            at = pl.multiple_of(jnp.maximum(j, 0) * TILE, TILE)
            act[:rows] += dot32(jnp.concatenate(parts, axis=0), proj[pl.ds(at, TILE), :])

        def step(*tiles):
            gates, ups, (gate_tile, up_tile) = tiles[:count], tiles[count : 2 * count], tiles[2 * count :]
            first = pl.program_id(0) * (tile // TILE) - 1
            blocks = [*x_refs, x]

            def part(i, span):
                parts = [hidden_of(first + i, chunk) for chunk in chunks]
                new_gate = sum((dot32(b[...], w[:, span]) for b, w in zip(blocks, gates)), gate_tile[:, span])
                new_up = sum((dot32(b[...], w[:, span]) for b, w in zip(blocks, ups)), up_tile[:, span])
                project(first + i, parts)
                gate[...], up[...] = new_gate, new_up

            halves(tile, part)

        pltpu.emit_pipeline(
            step, grid=(steps,),
            in_specs=weight_specs(ids, slots, depth, tile) + [tiled(rows, tile)] * 2, out_specs=[],
        )(*[gate_w] * count, *[up_w] * count, gate_sum, up_sum)
        project(last, [hidden_of(last, chunk) for chunk in chunks])

    return kernel_call(
        kernel, "late", ids, [at_side, at_middle, gate_w, up_w, proj_in, *sums, *xs],
        [VMEM] * 2 + [ANY] * 2 + [VMEM] + [ANY] * 2 + [VMEM] * len(xs),
        jax.ShapeDtypeStruct((most, rank), F32), VMEM,
        [pltpu.VMEM((rows, depth), BF16)] + [pltpu.VMEM((rows, TILE), F32)] * 2,
        4 * count * rows * depth * units, 4 * count * depth * units,
    )


MIDDLE, OUT = [(1, 2), (2, 1)], [(1, 0), (2, 3)]


def gathered(x):
    return lax.all_gather(x, "mp", axis=1, tiled=True)


def hop(x, pairs):
    return lax.ppermute(x, "mp", pairs)


def rest_case(size, ids, xs1, ends1, sums_own, rows, gate_w, up_w, proj_in):
    x = rows[:size]
    side, far = swap(x, "mp", 1), swap(x, "mp", 3)
    act1 = projected(ids, (1, 3, 2), xs1, *ends1, sums_own, gate_w, up_w, proj_in, FIRST)
    side, far, act1 = lax.optimization_barrier((side, far, act1))
    at_side, at_middle = hop(far, OUT), hop(side, MIDDLE)
    sums = sums_of(ids, (0, 1, 3), (x, side, far), gate_w, up_w)
    act2 = projected(ids, (2,), (), at_side, at_middle, sums, gate_w, up_w, proj_in, rows.shape[0])
    return act1, act2


def swap(x, axis, k, size=4):
    return lax.ppermute(x, axis, [(s, s ^ k) for s in range(size)])


def sketch_of_kept(tokens, grad_out, gate_w, up_w, proj_in, proj_out, lengths, loss_mask, queries):
    most, depth = tokens.shape
    rank = proj_in.shape[1]
    team_at = lax.axis_index("dp").astype(I32).reshape(1)
    order, cells, own1 = call(
        first_kernel, "first", [SMEM] * 2 + [VMEM] * 2,
        (
            jax.ShapeDtypeStruct(loss_mask.shape, I32),
            jax.ShapeDtypeStruct((8, 128), F32),
            jax.ShapeDtypeStruct((FIRST, depth), BF16),
        ),
        (VMEM,) * 3, team_at, lengths, loss_mask, tokens,
    )
    queries = lax.optimization_barrier((queries, own1))[0]
    all_queries = lax.all_gather(queries, "dp", axis=0)
    side1, far1 = swap(own1, "mp", 1), swap(own1, "mp", 3)
    me = lax.axis_index("mp").astype(I32)
    ids = jnp.stack([me, me ^ 1, me ^ 2, me ^ 3])
    grad_part = lax.dot_general(proj_out, grad_out, (((0,), (1,)), ((), ())), preferred_element_type=F32)
    high = lax.reduce_precision(grad_part, 8, 7)
    grads = jnp.concatenate([high.astype(BF16), (grad_part - high).astype(BF16)], axis=0)
    cells, grads = lax.optimization_barrier((cells, grads))
    cells = cells + swap(cells, "dp", 1) + swap(cells, "dp", 2) + swap(cells, "dp", 3)
    table = cells[:TEAM, :2].astype(I32).reshape(-1)
    sizes = sorted({s for s in SIZES if s < most - FIRST} | {most - FIRST})
    hand = jax.ShapeDtypeStruct((CAP, depth + 2 * rank), BF16)
    lots, *hands = call(
        functools.partial(deal_kernel, sizes), "deal", [SMEM] * 2 + [VMEM] * 3,
        (jax.ShapeDtypeStruct((3 * TEAM + 2,), I32),) + (hand,) * 3,
        (SMEM,) + (VMEM,) * 3, table, team_at, order, tokens, grads,
    )
    own1, *hands = lax.optimization_barrier((own1, *hands))
    hands = [swap(hand, "dp", k) for k, hand in zip((1, 2, 3), hands)]
    sums_own = sums_of(ids, (0,), (own1,), gate_w, up_w)
    side1, far1, sums_own = lax.optimization_barrier((side1, far1, sums_own))
    ends1 = hop(far1, OUT), hop(side1, MIDDLE)
    hands, side1, far1 = lax.optimization_barrier((hands, side1, far1))
    rows, grads = call(
        place_kernel, "place", [SMEM] * 2 + [VMEM] * 6,
        (
            jax.ShapeDtypeStruct((most - FIRST, depth), BF16),
            jax.ShapeDtypeStruct((rank, most), F32),
        ),
        (VMEM,) * 2, lots, team_at, order, tokens, grads, *hands,
    )
    rows, all_queries = lax.optimization_barrier((rows, all_queries))
    grads = lax.psum(grads, "mp")
    padded = jnp.pad(proj_in, ((0, -proj_in.shape[0] % (2 * TILE)), (0, 0)))
    act1, act2 = lax.switch(
        lots[3 * TEAM + 1], [functools.partial(rest_case, s) for s in sizes],
        ids, (side1, far1), ends1, sums_own, rows, gate_w, up_w, padded,
    )
    parts = call(
        sketch_kernel, "sketch", [SMEM] * 3 + [VMEM] * 3, jax.ShapeDtypeStruct((2 * TEAM * rank, rank), F32),
        VMEM, table, lots, team_at, grads, act1, act2,
    )
    parts = parts.reshape(TEAM, 2 * rank, rank)
    me = team_at[0]
    part = lax.dynamic_index_in_dim(parts, me, 0, False)
    for k in (1, 2, 3):
        part = part + swap(lax.dynamic_index_in_dim(parts, me ^ k, 0, False), "dp", k)
    return part + swap(part, "mp", 1) + swap(part, "mp", 2) + swap(part, "mp", 3), all_queries


def sketch_in_general(tokens, grad_out, gate_w, up_w, proj_in, proj_out, lengths, loss_mask, queries):
    roll_count, seq_len = loss_mask.shape
    rank = proj_in.shape[1]
    keep = (jnp.arange(seq_len, dtype=I32)[None, :] < lengths[:, None]) & (loss_mask == 1)
    pieces = gathered(tokens)
    hidden = (jax.nn.silu(dot32(pieces, gate_w)) * dot32(pieces, up_w)).astype(BF16)
    stacked = jnp.concatenate([dot32(grad_out, proj_out), dot32(hidden, proj_in)], axis=1)
    summed = lax.psum(stacked, "mp").reshape(roll_count, seq_len, 2 * rank)
    weighted = summed[:, :, :rank] * keep.astype(F32)[:, :, None]
    sums = jnp.einsum("rti,rtj->rij", weighted, summed[:, :, rank:], precision=lax.Precision.HIGHEST)
    return sums, lax.all_gather(queries, "dp", axis=0)


def local(team, planes, tokens, grad_out, gate_w, up_w, proj_in, proj_out, lengths, loss_mask, queries):
    roll_count, seq_len = loss_mask.shape
    fits = team == TEAM and planes == PLANES and roll_count == 2 and seq_len % 256 == 0
    fits = fits and tokens.shape[1] % 128 == 0 and gate_w.shape[1] % 128 == 0 and proj_in.shape[1] == 64
    form = sketch_of_kept if fits else sketch_in_general
    sketch_sum, all_queries = form(
        tokens, grad_out, gate_w, up_w, proj_in, proj_out, lengths, loss_mask, queries
    )
    norm_factor = 1.0 / jnp.sqrt(jnp.float32(seq_len))
    sketch = (sketch_sum.reshape(roll_count, team, -1) * norm_factor).astype(BF16)
    return jnp.einsum("rdk,dqk->rq", sketch, all_queries, preferred_element_type=F32)


def solution(mesh):
    placed = (
        P(("groups", "dp"), "mp"),
        P(("groups", "dp"), "mp"),
        P(None, "mp"),
        P(None, "mp"),
        P("mp", None),
        P("mp", None),
        P(("groups", "dp")),
        P(("groups", "dp"), None),
        P("mp", "dp"),
    )
    return jax.shard_map(
        functools.partial(local, mesh.shape["dp"], mesh.shape["mp"]),
        mesh=mesh, in_specs=placed, out_specs=P(("groups", "dp"), "mp"), check_vma=False,
    )
```

```python
import functools

import jax
import jax.numpy as jnp
from jax import lax
from jax.experimental import pallas as pl
from jax.experimental.pallas import tpu as pltpu
from jax.sharding import PartitionSpec as P

BF16, F32, I32 = jnp.bfloat16, jnp.float32, jnp.int32
FIRST = 256
SIZES = (176, 224, 272, 320, 400)
CAP = 192
TEAM = 4
PLANES = 4
TILE = 256
MIB = 2**20


def dot32(a, b):
    return jnp.dot(a, b, preferred_element_type=F32)


def dot32_t(a, b):
    return lax.dot_general(a, b, (((1,), (1,)), ((), ())), preferred_element_type=F32)


def iota(shape, axis):
    return lax.broadcasted_iota(I32, shape, axis)


def ones_where(cond):
    return jnp.where(cond, 1.0, 0.0).astype(BF16)


def dealt(rest, most):
    keep = [jnp.minimum(m, most) for m in rest]
    spare_at, room_at, a, b = [], [], 0, 0
    for m, k in zip(rest, keep):
        spare_at.append(a)
        room_at.append(b)
        a, b = a + (m - k), b + (most - k)
    start, moved = {}, {}
    for s in range(TEAM):
        for t in range(TEAM):
            if s != t:
                low = jnp.maximum(spare_at[s], room_at[t])
                high = jnp.minimum(spare_at[s] + rest[s] - keep[s], room_at[t] + most - keep[t])
                start[s, t], moved[s, t] = low, jnp.maximum(high - low, 0)
    return keep, spare_at, room_at, start, moved


def plan(table):
    rest = [jnp.maximum(table[2 * s + 1] - FIRST, 0) for s in range(TEAM)]
    even = (rest[0] + rest[1] + rest[2] + rest[3] + (TEAM - 1)) // TEAM
    most = functools.reduce(jnp.maximum, rest)
    for tried in ((3 * most + even) // 4, (most + even) // 2, even):
        largest = functools.reduce(jnp.maximum, dealt(rest, tried)[4].values())
        most = jnp.where(largest <= CAP, tried, most)
    keep, spare_at, room_at, start, moved = dealt(rest, most)
    lots = {}
    for s in range(TEAM):
        lots[s, s] = (FIRST, 0, keep[s])
        for t in range(TEAM):
            if s != t:
                rank = FIRST + keep[s] + start[s, t] - spare_at[s]
                lots[s, t] = (rank, keep[t] + start[s, t] - room_at[t], moved[s, t])
    return most, lots


def chosen(lots, pairs):
    out = [0, 0, 0]
    for cond, pair in pairs:
        out = [jnp.where(cond, new, old) for new, old in zip(lots[pair], out)]
    return out


def first_kernel(team_at, lengths, loss_mask, tokens, order, table, rows):
    seq_len = loss_mask.shape[1]
    limit = jnp.where(iota(loss_mask.shape, 0) == 0, lengths[0], lengths[1])
    keep = (iota(loss_mask.shape, 1) < limit) & (loss_mask[...] == 1)
    upto = ones_where(iota((seq_len, seq_len), 0) <= iota((seq_len, seq_len), 1))
    kept = jnp.where(keep, 1.0, 0.0)
    place = dot32(kept.astype(BF16), upto)
    before = jnp.sum(kept[0:1], axis=1, keepdims=True)
    total = before + jnp.sum(kept[1:2], axis=1, keepdims=True)
    place = place - 1.0 + jnp.where(iota(place.shape, 0) == 0, 0.0, before)
    ranks = jnp.where(keep, place, -1.0).astype(I32)
    order[...] = ranks
    cell = jnp.where(iota(table.shape, 1) == 0, before, total)
    table[...] = jnp.where(iota(table.shape, 0) == team_at[0], cell, 0.0)
    at = iota((FIRST, seq_len), 0)
    found = dot32(ones_where(ranks[0:1] == at), tokens[:seq_len])
    found += dot32(ones_where(ranks[1:2] == at), tokens[seq_len:])
    rows[...] = found.astype(BF16)


def deal_kernel(sizes, table, team_at, order, tokens, grads, lots_to_me, *hands):
    me, seq_len = team_at[0], order.shape[1]
    most, lots = plan(table)
    lots_to_me[3 * TEAM] = most
    lots_to_me[3 * TEAM + 1] = sum((most > size).astype(I32) for size in sizes[:-1])
    for s in range(TEAM):
        for i, value in enumerate(chosen(lots, [(me == t, (s, t)) for t in range(TEAM)])):
            lots_to_me[3 * s + i] = value
    depth = tokens.shape[1]
    at = iota((CAP, seq_len), 0)
    for k, hand in zip(range(1, TEAM), hands):
        rank, _, number = chosen(lots, [(me == s, (s, s ^ k)) for s in range(TEAM)])
        valid = at < number
        for side in range(2):
            pick = ones_where((order[side : side + 1] - rank == at) & valid)
            span = slice(side * seq_len, (side + 1) * seq_len)
            found, grad = dot32(pick, tokens[span]), dot32_t(pick, grads[:, span])
            if side == 0:
                hand[:, :depth], hand[:, depth:] = found.astype(BF16), grad.astype(BF16)
            else:
                hand[:, :depth] += found.astype(BF16)
                hand[:, depth:] += grad.astype(BF16)


def place_kernel(lots_to_me, team_at, order, tokens, grads, hand1, hand2, hand3, rows, grads_here):
    me, seq_len = team_at[0], order.shape[1]
    depth, rank_size = tokens.shape[1], grads_here.shape[0]
    kept, size = lots_to_me[3 * me + 2], lots_to_me[3 * TEAM]
    at = iota((FIRST, seq_len), 0)

    def picked(base, valid):
        hits = [order[side : side + 1] - base == at for side in range(2)]
        return [ones_where(hit if valid is None else hit & valid) for hit in hits]

    def grad_of(picks):
        return dot32_t(grads[:, :seq_len], picks[0]) + dot32_t(grads[:, seq_len:], picks[1])

    grad = grad_of(picked(0, None))
    grads_here[:, :FIRST] = grad[:rank_size] + grad[rank_size:]

    def block(i, carry):
        base = pl.multiple_of(i * FIRST, FIRST)
        picks = picked(base + FIRST, at + base < kept)
        found = dot32(picks[0], tokens[:seq_len]) + dot32(picks[1], tokens[seq_len:])
        source, target = iota((FIRST, CAP), 1), iota((FIRST, CAP), 0) + base
        dealt_grad = 0.0
        for k, hand in ((1, hand1), (2, hand2), (3, hand3)):
            row, number = lots_to_me[3 * (me ^ k) + 1], lots_to_me[3 * (me ^ k) + 2]
            put = ones_where((target - row == source) & (source < number))
            found += dot32(put, hand[:, :depth])
            dealt_grad += dot32(put, hand[:, depth:])
        grad = grad_of(picks) + dealt_grad.T
        rows[pl.ds(base, FIRST), :] = found.astype(BF16)
        grads_here[:, pl.ds(base + FIRST, FIRST)] = grad[:rank_size] + grad[rank_size:]
        return carry

    lax.fori_loop(0, (size + FIRST - 1) // FIRST, block, 0)


def sketch_kernel(table, lots_to_me, team_at, grads, act1, act2, out):
    me, size = team_at[0], lots_to_me[3 * TEAM]

    def product(grad, lane, act):
        parts = []
        for s in range(TEAM):
            rank, row, number = lots_to_me[3 * s], lots_to_me[3 * s + 1] + FIRST, lots_to_me[3 * s + 2]
            edge = jnp.clip(row + table[2 * s] - rank, row, row + number)
            own = (me == s) & (lane < FIRST)
            cut = table[2 * s]
            for low, high, early in ((row, edge, lane < cut), (edge, row + number, lane >= cut)):
                mine = ((lane >= low) & (lane < high)) | (own & early)
                parts.append(jnp.where(mine, grad, 0.0))
        return jnp.dot(
            jnp.concatenate(parts, axis=0), act, precision=lax.Precision.HIGHEST, preferred_element_type=F32
        )

    out[...] = product(grads[:, :FIRST], iota((1, FIRST), 1), act1[...])

    def step(chunk, carry):
        base = pl.multiple_of(chunk * FIRST, FIRST)
        act = act2[pl.ds(base, FIRST), :]
        act = jnp.where(iota(act.shape, 0) + base < size, act, 0.0)
        lane = iota((1, FIRST), 1) + base + FIRST
        out[...] += product(grads[:, pl.ds(base + FIRST, FIRST)], lane, act)
        return carry

    lax.fori_loop(0, (size + FIRST - 1) // FIRST, step, 0)


ANY = pl.BlockSpec(memory_space=pl.ANY)
VMEM = pl.BlockSpec(memory_space=pltpu.VMEM)
SMEM = pl.BlockSpec(memory_space=pltpu.SMEM)


def call(kernel, name, specs, out_shape, out_specs, *args):
    return pl.pallas_call(
        kernel, out_shape=out_shape, in_specs=specs, out_specs=out_specs, name=name,
        compiler_params=pltpu.CompilerParams(vmem_limit_bytes=32 * MIB),
    )(*args)


def weight_specs(ids, slots, depth, tile):
    deep = pl.Buffered(2 if len(slots) > 1 and tile > TILE else 3)
    return [pl.BlockSpec((depth, tile), lambda j, s=s: (ids[s], j), pipeline_mode=deep) for s in slots] * 2


def tiled(rows, tile):
    return pl.BlockSpec((rows, tile), lambda j: (0, j))


def kernel_call(kernel, name, ids, operands, specs, out_shape, out_specs, scratch, flops, moved):
    return pl.pallas_call(
        kernel,
        in_specs=[SMEM] + specs, out_specs=out_specs, out_shape=out_shape, scratch_shapes=scratch, name=name,
        compiler_params=pltpu.CompilerParams(vmem_limit_bytes=38 * MIB),
        cost_estimate=pl.CostEstimate(flops=flops, bytes_accessed=moved, transcendentals=0),
    )(ids, *operands)


def halves(tile, body):
    def step(part, carry):
        body(part, pl.ds(pl.multiple_of(part * TILE, TILE), TILE))
        return carry

    lax.fori_loop(0, tile // TILE, step, 0)


def sums_of(ids, slots, xs, gate_w, up_w, tile=TILE):
    (rows, depth), units, count = xs[0].shape, gate_w.shape[1], len(xs)
    steps = -(-units // tile)

    def kernel(ids, *refs):
        x_refs, (gate_w, up_w, gate_sum, up_sum) = refs[:count], refs[count:]

        def step(*tiles):
            gates, ups, (gate, up) = tiles[:count], tiles[count : 2 * count], tiles[2 * count :]
            gate[...] = sum(dot32(x[...], w[...]) for x, w in zip(x_refs, gates))
            up[...] = sum(dot32(x[...], w[...]) for x, w in zip(x_refs, ups))

        pltpu.emit_pipeline(
            step, grid=(steps,), in_specs=weight_specs(ids, slots, depth, tile), out_specs=[tiled(rows, tile)] * 2
        )(*[gate_w] * count, *[up_w] * count, gate_sum, up_sum)

    out = jax.ShapeDtypeStruct((rows, steps * tile), F32)
    return kernel_call(
        kernel, "sums", ids, [*xs, gate_w, up_w], [VMEM] * count + [ANY] * 2, (out, out), (ANY, ANY), (),
        4 * count * rows * depth * units, 4 * count * depth * units,
    )


def projected(ids, slots, xs, at_side, at_middle, sums, gate_w, up_w, proj_in, most, tile=2 * TILE):
    (rows, depth), units, rank, count = at_side.shape, gate_w.shape[1], proj_in.shape[1], len(slots)
    steps, last = proj_in.shape[0] // tile, proj_in.shape[0] // TILE - 1

    def kernel(ids, at_side, at_middle, gate_w, up_w, proj, gate_sum, up_sum, *refs):
        x_refs, (act, x, gate, up) = refs[: count - 1], refs[count - 1 :]
        middle = (ids[0] == 1) | (ids[0] == 2)
        x[...] = jnp.where(middle, at_middle[...], at_side[...])
        act[:rows] = jnp.zeros((rows, rank), F32)

        half = -(-rows // 32) * 16
        chunks = [(at, min(half, rows - at)) for at in range(0, rows, half)]

        def hidden_of(j, chunk):
            span = pl.ds(*chunk)
            v = 0.5 * gate[span, :]
            hidden = (v + v * jnp.tanh(v)) * up[span, :]
            column = iota(hidden.shape, 1) + j * TILE
            return jnp.where((column >= 0) & (column < units), hidden, 0.0).astype(BF16)

        def project(j, parts):
            at = pl.multiple_of(jnp.maximum(j, 0) * TILE, TILE)
            act[:rows] += dot32(jnp.concatenate(parts, axis=0), proj[pl.ds(at, TILE), :])

        def step(*tiles):
            gates, ups, (gate_tile, up_tile) = tiles[:count], tiles[count : 2 * count], tiles[2 * count :]
            first = pl.program_id(0) * (tile // TILE) - 1
            blocks = [*x_refs, x]

            def part(i, span):
                parts = [hidden_of(first + i, chunk) for chunk in chunks]
                new_gate = sum((dot32(b[...], w[:, span]) for b, w in zip(blocks, gates)), gate_tile[:, span])
                new_up = sum((dot32(b[...], w[:, span]) for b, w in zip(blocks, ups)), up_tile[:, span])
                project(first + i, parts)
                gate[...], up[...] = new_gate, new_up

            halves(tile, part)

        pltpu.emit_pipeline(
            step, grid=(steps,),
            in_specs=weight_specs(ids, slots, depth, tile) + [tiled(rows, tile)] * 2, out_specs=[],
        )(*[gate_w] * count, *[up_w] * count, gate_sum, up_sum)
        project(last, [hidden_of(last, chunk) for chunk in chunks])

    return kernel_call(
        kernel, "late", ids, [at_side, at_middle, gate_w, up_w, proj_in, *sums, *xs],
        [VMEM] * 2 + [ANY] * 2 + [VMEM] + [ANY] * 2 + [VMEM] * len(xs),
        jax.ShapeDtypeStruct((most, rank), F32), VMEM,
        [pltpu.VMEM((rows, depth), BF16)] + [pltpu.VMEM((rows, TILE), F32)] * 2,
        4 * count * rows * depth * units, 4 * count * depth * units,
    )


MIDDLE, OUT = [(1, 2), (2, 1)], [(1, 0), (2, 3)]


def gathered(x):
    return lax.all_gather(x, "mp", axis=1, tiled=True)


def hop(x, pairs):
    return lax.ppermute(x, "mp", pairs)


def rest_case(size, ids, xs1, ends1, sums_own, rows, grads, gate_w, up_w, proj_in):
    x = rows[:size]
    used = FIRST + size
    total = lax.psum(grads[:, :used], "mp")
    side, far = swap(x, "mp", 1), swap(x, "mp", 3)
    act1 = projected(ids, (1, 3, 2), xs1, *ends1, sums_own, gate_w, up_w, proj_in, FIRST)
    side, far, act1 = lax.optimization_barrier((side, far, act1))
    at_side, at_middle = hop(far, OUT), hop(side, MIDDLE)
    sums = sums_of(ids, (0, 1, 3), (x, side, far), gate_w, up_w)
    total = jnp.pad(total, ((0, 0), (0, grads.shape[1] - used)))
    at_side, total = lax.optimization_barrier((at_side, total))
    act2 = projected(ids, (2,), (), at_side, at_middle, sums, gate_w, up_w, proj_in, rows.shape[0])
    return act1, act2, total


def swap(x, axis, k, size=4):
    return lax.ppermute(x, axis, [(s, s ^ k) for s in range(size)])


def sketch_of_kept(tokens, grad_out, gate_w, up_w, proj_in, proj_out, lengths, loss_mask, queries):
    most, depth = tokens.shape
    rank = proj_in.shape[1]
    team_at = lax.axis_index("dp").astype(I32).reshape(1)
    order, cells, own1 = call(
        first_kernel, "first", [SMEM] * 2 + [VMEM] * 2,
        (
            jax.ShapeDtypeStruct(loss_mask.shape, I32),
            jax.ShapeDtypeStruct((8, 128), F32),
            jax.ShapeDtypeStruct((FIRST, depth), BF16),
        ),
        (VMEM,) * 3, team_at, lengths, loss_mask, tokens,
    )
    queries = lax.optimization_barrier((queries, own1))[0]
    all_queries = lax.all_gather(queries, "dp", axis=0)
    side1, far1 = swap(own1, "mp", 1), swap(own1, "mp", 3)
    me = lax.axis_index("mp").astype(I32)
    ids = jnp.stack([me, me ^ 1, me ^ 2, me ^ 3])
    grad_part = lax.dot_general(proj_out, grad_out, (((0,), (1,)), ((), ())), preferred_element_type=F32)
    high = lax.reduce_precision(grad_part, 8, 7)
    grads = jnp.concatenate([high.astype(BF16), (grad_part - high).astype(BF16)], axis=0)
    cells, grads = lax.optimization_barrier((cells, grads))
    cells = cells + swap(cells, "dp", 1) + swap(cells, "dp", 2) + swap(cells, "dp", 3)
    table = cells[:TEAM, :2].astype(I32).reshape(-1)
    sizes = sorted({s for s in SIZES if s < most - FIRST} | {most - FIRST})
    hand = jax.ShapeDtypeStruct((CAP, depth + 2 * rank), BF16)
    lots, *hands = call(
        functools.partial(deal_kernel, sizes), "deal", [SMEM] * 2 + [VMEM] * 3,
        (jax.ShapeDtypeStruct((3 * TEAM + 2,), I32),) + (hand,) * 3,
        (SMEM,) + (VMEM,) * 3, table, team_at, order, tokens, grads,
    )
    own1, *hands = lax.optimization_barrier((own1, *hands))
    hands = [swap(hand, "dp", k) for k, hand in zip((1, 2, 3), hands)]
    sums_own = sums_of(ids, (0,), (own1,), gate_w, up_w)
    side1, far1, sums_own = lax.optimization_barrier((side1, far1, sums_own))
    ends1 = hop(far1, OUT), hop(side1, MIDDLE)
    hands, side1, far1 = lax.optimization_barrier((hands, side1, far1))
    rows, grads = call(
        place_kernel, "place", [SMEM] * 2 + [VMEM] * 6,
        (
            jax.ShapeDtypeStruct((most - FIRST, depth), BF16),
            jax.ShapeDtypeStruct((rank, most), F32),
        ),
        (VMEM,) * 2, lots, team_at, order, tokens, grads, *hands,
    )
    rows, all_queries = lax.optimization_barrier((rows, all_queries))
    padded = jnp.pad(proj_in, ((0, -proj_in.shape[0] % (2 * TILE)), (0, 0)))
    act1, act2, grads = lax.switch(
        lots[3 * TEAM + 1], [functools.partial(rest_case, s) for s in sizes],
        ids, (side1, far1), ends1, sums_own, rows, grads, gate_w, up_w, padded,
    )
    parts = call(
        sketch_kernel, "sketch", [SMEM] * 3 + [VMEM] * 3, jax.ShapeDtypeStruct((2 * TEAM * rank, rank), F32),
        VMEM, table, lots, team_at, grads, act1, act2,
    )
    parts = parts.reshape(TEAM, 2 * rank, rank)
    me = team_at[0]
    part = lax.dynamic_index_in_dim(parts, me, 0, False)
    for k in (1, 2, 3):
        part = part + swap(lax.dynamic_index_in_dim(parts, me ^ k, 0, False), "dp", k)
    return part + swap(part, "mp", 1) + swap(part, "mp", 2) + swap(part, "mp", 3), all_queries


def sketch_in_general(tokens, grad_out, gate_w, up_w, proj_in, proj_out, lengths, loss_mask, queries):
    roll_count, seq_len = loss_mask.shape
    rank = proj_in.shape[1]
    keep = (jnp.arange(seq_len, dtype=I32)[None, :] < lengths[:, None]) & (loss_mask == 1)
    pieces = gathered(tokens)
    hidden = (jax.nn.silu(dot32(pieces, gate_w)) * dot32(pieces, up_w)).astype(BF16)
    stacked = jnp.concatenate([dot32(grad_out, proj_out), dot32(hidden, proj_in)], axis=1)
    summed = lax.psum(stacked, "mp").reshape(roll_count, seq_len, 2 * rank)
    weighted = summed[:, :, :rank] * keep.astype(F32)[:, :, None]
    sums = jnp.einsum("rti,rtj->rij", weighted, summed[:, :, rank:], precision=lax.Precision.HIGHEST)
    return sums, lax.all_gather(queries, "dp", axis=0)


def local(team, planes, tokens, grad_out, gate_w, up_w, proj_in, proj_out, lengths, loss_mask, queries):
    roll_count, seq_len = loss_mask.shape
    fits = team == TEAM and planes == PLANES and roll_count == 2 and seq_len % 256 == 0
    fits = fits and tokens.shape[1] % 128 == 0 and gate_w.shape[1] % 128 == 0 and proj_in.shape[1] == 64
    form = sketch_of_kept if fits else sketch_in_general
    sketch_sum, all_queries = form(
        tokens, grad_out, gate_w, up_w, proj_in, proj_out, lengths, loss_mask, queries
    )
    norm_factor = 1.0 / jnp.sqrt(jnp.float32(seq_len))
    sketch = (sketch_sum.reshape(roll_count, team, -1) * norm_factor).astype(BF16)
    return jnp.einsum("rdk,dqk->rq", sketch, all_queries, preferred_element_type=F32)


def solution(mesh):
    placed = (
        P(("groups", "dp"), "mp"),
        P(("groups", "dp"), "mp"),
        P(None, "mp"),
        P(None, "mp"),
        P("mp", None),
        P("mp", None),
        P(("groups", "dp")),
        P(("groups", "dp"), None),
        P("mp", "dp"),
    )
    return jax.shard_map(
        functools.partial(local, mesh.shape["dp"], mesh.shape["mp"]),
        mesh=mesh, in_specs=placed, out_specs=P(("groups", "dp"), "mp"), check_vma=False,
    )
```

```python
import functools

import jax
import jax.numpy as jnp
from jax import lax
from jax.experimental import pallas as pl
from jax.experimental.pallas import tpu as pltpu
from jax.sharding import PartitionSpec as P

BF16, F32, I32 = jnp.bfloat16, jnp.float32, jnp.int32
FIRST = 256
SIZES = (176, 208, 240, 272, 320, 400)
CAP = 192
TEAM = 4
PLANES = 4
TILE = 256
MIB = 2**20


def dot32(a, b):
    return jnp.dot(a, b, preferred_element_type=F32)


def dot32_t(a, b):
    return lax.dot_general(a, b, (((1,), (1,)), ((), ())), preferred_element_type=F32)


def iota(shape, axis):
    return lax.broadcasted_iota(I32, shape, axis)


def ones_where(cond):
    return jnp.where(cond, 1.0, 0.0).astype(BF16)


def dealt(rest, most):
    keep = [jnp.minimum(m, most) for m in rest]
    spare_at, room_at, a, b = [], [], 0, 0
    for m, k in zip(rest, keep):
        spare_at.append(a)
        room_at.append(b)
        a, b = a + (m - k), b + (most - k)
    start, moved = {}, {}
    for s in range(TEAM):
        for t in range(TEAM):
            if s != t:
                low = jnp.maximum(spare_at[s], room_at[t])
                high = jnp.minimum(spare_at[s] + rest[s] - keep[s], room_at[t] + most - keep[t])
                start[s, t], moved[s, t] = low, jnp.maximum(high - low, 0)
    return keep, spare_at, room_at, start, moved


def plan(table):
    rest = [jnp.maximum(table[2 * s + 1] - FIRST, 0) for s in range(TEAM)]
    even = (rest[0] + rest[1] + rest[2] + rest[3] + (TEAM - 1)) // TEAM
    most = functools.reduce(jnp.maximum, rest)
    for tried in ((3 * most + even) // 4, (most + even) // 2, even):
        largest = functools.reduce(jnp.maximum, dealt(rest, tried)[4].values())
        most = jnp.where(largest <= CAP, tried, most)
    keep, spare_at, room_at, start, moved = dealt(rest, most)
    lots = {}
    for s in range(TEAM):
        lots[s, s] = (FIRST, 0, keep[s])
        for t in range(TEAM):
            if s != t:
                rank = FIRST + keep[s] + start[s, t] - spare_at[s]
                lots[s, t] = (rank, keep[t] + start[s, t] - room_at[t], moved[s, t])
    return most, lots


def chosen(lots, pairs):
    out = [0, 0, 0]
    for cond, pair in pairs:
        out = [jnp.where(cond, new, old) for new, old in zip(lots[pair], out)]
    return out


def first_kernel(team_at, lengths, loss_mask, tokens, order, table, rows):
    seq_len = loss_mask.shape[1]
    limit = jnp.where(iota(loss_mask.shape, 0) == 0, lengths[0], lengths[1])
    keep = (iota(loss_mask.shape, 1) < limit) & (loss_mask[...] == 1)
    upto = ones_where(iota((seq_len, seq_len), 0) <= iota((seq_len, seq_len), 1))
    kept = jnp.where(keep, 1.0, 0.0)
    place = dot32(kept.astype(BF16), upto)
    before = jnp.sum(kept[0:1], axis=1, keepdims=True)
    total = before + jnp.sum(kept[1:2], axis=1, keepdims=True)
    place = place - 1.0 + jnp.where(iota(place.shape, 0) == 0, 0.0, before)
    ranks = jnp.where(keep, place, -1.0).astype(I32)
    order[...] = ranks
    cell = jnp.where(iota(table.shape, 1) == 0, before, total)
    table[...] = jnp.where(iota(table.shape, 0) == team_at[0], cell, 0.0)
    at = iota((FIRST, seq_len), 0)
    found = dot32(ones_where(ranks[0:1] == at), tokens[:seq_len])
    found += dot32(ones_where(ranks[1:2] == at), tokens[seq_len:])
    rows[...] = found.astype(BF16)


def deal_kernel(sizes, table, team_at, order, tokens, grads, lots_to_me, *hands):
    me, seq_len = team_at[0], order.shape[1]
    most, lots = plan(table)
    lots_to_me[3 * TEAM] = most
    lots_to_me[3 * TEAM + 1] = sum((most > size).astype(I32) for size in sizes[:-1])
    for s in range(TEAM):
        for i, value in enumerate(chosen(lots, [(me == t, (s, t)) for t in range(TEAM)])):
            lots_to_me[3 * s + i] = value
    depth = tokens.shape[1]
    at = iota((CAP, seq_len), 0)
    for k, hand in zip(range(1, TEAM), hands):
        rank, _, number = chosen(lots, [(me == s, (s, s ^ k)) for s in range(TEAM)])
        valid = at < number
        for side in range(2):
            pick = ones_where((order[side : side + 1] - rank == at) & valid)
            span = slice(side * seq_len, (side + 1) * seq_len)
            found, grad = dot32(pick, tokens[span]), dot32_t(pick, grads[:, span])
            if side == 0:
                hand[:, :depth], hand[:, depth:] = found.astype(BF16), grad.astype(BF16)
            else:
                hand[:, :depth] += found.astype(BF16)
                hand[:, depth:] += grad.astype(BF16)


def place_kernel(lots_to_me, team_at, order, tokens, grads, hand1, hand2, hand3, rows, grads_here):
    me, seq_len = team_at[0], order.shape[1]
    depth, rank_size = tokens.shape[1], grads_here.shape[0]
    kept, size = lots_to_me[3 * me + 2], lots_to_me[3 * TEAM]
    at = iota((FIRST, seq_len), 0)

    def picked(base, valid):
        hits = [order[side : side + 1] - base == at for side in range(2)]
        return [ones_where(hit if valid is None else hit & valid) for hit in hits]

    def grad_of(picks):
        return dot32_t(grads[:, :seq_len], picks[0]) + dot32_t(grads[:, seq_len:], picks[1])

    grad = grad_of(picked(0, None))
    grads_here[:, :FIRST] = grad[:rank_size] + grad[rank_size:]

    def block(i, carry):
        base = pl.multiple_of(i * FIRST, FIRST)
        picks = picked(base + FIRST, at + base < kept)
        found = dot32(picks[0], tokens[:seq_len]) + dot32(picks[1], tokens[seq_len:])
        source, target = iota((FIRST, CAP), 1), iota((FIRST, CAP), 0) + base
        dealt_grad = 0.0
        for k, hand in ((1, hand1), (2, hand2), (3, hand3)):
            row, number = lots_to_me[3 * (me ^ k) + 1], lots_to_me[3 * (me ^ k) + 2]
            put = ones_where((target - row == source) & (source < number))
            found += dot32(put, hand[:, :depth])
            dealt_grad += dot32(put, hand[:, depth:])
        grad = grad_of(picks) + dealt_grad.T
        rows[pl.ds(base, FIRST), :] = found.astype(BF16)
        grads_here[:, pl.ds(base + FIRST, FIRST)] = grad[:rank_size] + grad[rank_size:]
        return carry

    lax.fori_loop(0, (size + FIRST - 1) // FIRST, block, 0)


def sketch_kernel(table, lots_to_me, team_at, grads, act1, act2, out):
    me, size = team_at[0], lots_to_me[3 * TEAM]

    def product(grad, lane, act):
        parts = []
        for s in range(TEAM):
            rank, row, number = lots_to_me[3 * s], lots_to_me[3 * s + 1] + FIRST, lots_to_me[3 * s + 2]
            edge = jnp.clip(row + table[2 * s] - rank, row, row + number)
            own = (me == s) & (lane < FIRST)
            cut = table[2 * s]
            for low, high, early in ((row, edge, lane < cut), (edge, row + number, lane >= cut)):
                mine = ((lane >= low) & (lane < high)) | (own & early)
                parts.append(jnp.where(mine, grad, 0.0))
        return jnp.dot(
            jnp.concatenate(parts, axis=0), act, precision=lax.Precision.HIGHEST, preferred_element_type=F32
        )

    out[...] = product(grads[:, :FIRST], iota((1, FIRST), 1), act1[...])

    def step(chunk, carry):
        base = pl.multiple_of(chunk * FIRST, FIRST)
        act = act2[pl.ds(base, FIRST), :]
        act = jnp.where(iota(act.shape, 0) + base < size, act, 0.0)
        lane = iota((1, FIRST), 1) + base + FIRST
        out[...] += product(grads[:, pl.ds(base + FIRST, FIRST)], lane, act)
        return carry

    lax.fori_loop(0, (size + FIRST - 1) // FIRST, step, 0)


ANY = pl.BlockSpec(memory_space=pl.ANY)
VMEM = pl.BlockSpec(memory_space=pltpu.VMEM)
SMEM = pl.BlockSpec(memory_space=pltpu.SMEM)


def call(kernel, name, specs, out_shape, out_specs, *args):
    return pl.pallas_call(
        kernel, out_shape=out_shape, in_specs=specs, out_specs=out_specs, name=name,
        compiler_params=pltpu.CompilerParams(vmem_limit_bytes=32 * MIB),
    )(*args)


def weight_specs(ids, slots, depth, tile):
    deep = pl.Buffered(2 if len(slots) > 1 and tile > TILE else 3)
    return [pl.BlockSpec((depth, tile), lambda j, s=s: (ids[s], j), pipeline_mode=deep) for s in slots] * 2


def tiled(rows, tile):
    return pl.BlockSpec((rows, tile), lambda j: (0, j))


def kernel_call(kernel, name, ids, operands, specs, out_shape, out_specs, scratch, flops, moved):
    return pl.pallas_call(
        kernel,
        in_specs=[SMEM] + specs, out_specs=out_specs, out_shape=out_shape, scratch_shapes=scratch, name=name,
        compiler_params=pltpu.CompilerParams(vmem_limit_bytes=38 * MIB),
        cost_estimate=pl.CostEstimate(flops=flops, bytes_accessed=moved, transcendentals=0),
    )(ids, *operands)


def halves(tile, body):
    def step(part, carry):
        body(part, pl.ds(pl.multiple_of(part * TILE, TILE), TILE))
        return carry

    lax.fori_loop(0, tile // TILE, step, 0)


def sums_of(ids, slots, xs, gate_w, up_w, tile=TILE):
    (rows, depth), units, count = xs[0].shape, gate_w.shape[1], len(xs)
    steps = -(-units // tile)

    def kernel(ids, *refs):
        x_refs, (gate_w, up_w, gate_sum, up_sum) = refs[:count], refs[count:]

        def step(*tiles):
            gates, ups, (gate, up) = tiles[:count], tiles[count : 2 * count], tiles[2 * count :]
            gate[...] = sum(dot32(x[...], w[...]) for x, w in zip(x_refs, gates))
            up[...] = sum(dot32(x[...], w[...]) for x, w in zip(x_refs, ups))

        pltpu.emit_pipeline(
            step, grid=(steps,), in_specs=weight_specs(ids, slots, depth, tile), out_specs=[tiled(rows, tile)] * 2
        )(*[gate_w] * count, *[up_w] * count, gate_sum, up_sum)

    out = jax.ShapeDtypeStruct((rows, steps * tile), F32)
    return kernel_call(
        kernel, "sums", ids, [*xs, gate_w, up_w], [VMEM] * count + [ANY] * 2, (out, out), (ANY, ANY), (),
        4 * count * rows * depth * units, 4 * count * depth * units,
    )


def projected(ids, slots, xs, at_side, at_middle, sums, gate_w, up_w, proj_in, most, tile=2 * TILE):
    (rows, depth), units, rank, count = at_side.shape, gate_w.shape[1], proj_in.shape[1], len(slots)
    steps, last = proj_in.shape[0] // tile, proj_in.shape[0] // TILE - 1

    def kernel(ids, at_side, at_middle, gate_w, up_w, proj, gate_sum, up_sum, *refs):
        x_refs, (act, x, gate, up) = refs[: count - 1], refs[count - 1 :]
        middle = (ids[0] == 1) | (ids[0] == 2)
        x[...] = jnp.where(middle, at_middle[...], at_side[...])
        act[:rows] = jnp.zeros((rows, rank), F32)

        half = -(-rows // 32) * 16
        chunks = [(at, min(half, rows - at)) for at in range(0, rows, half)]

        def hidden_of(j, chunk):
            span = pl.ds(*chunk)
            v = 0.5 * gate[span, :]
            hidden = (v + v * jnp.tanh(v)) * up[span, :]
            column = iota(hidden.shape, 1) + j * TILE
            return jnp.where((column >= 0) & (column < units), hidden, 0.0).astype(BF16)

        def project(j, parts):
            at = pl.multiple_of(jnp.maximum(j, 0) * TILE, TILE)
            act[:rows] += dot32(jnp.concatenate(parts, axis=0), proj[pl.ds(at, TILE), :])

        def step(*tiles):
            gates, ups, (gate_tile, up_tile) = tiles[:count], tiles[count : 2 * count], tiles[2 * count :]
            first = pl.program_id(0) * (tile // TILE) - 1
            blocks = [*x_refs, x]

            def part(i, span):
                parts = [hidden_of(first + i, chunk) for chunk in chunks]
                new_gate = sum((dot32(b[...], w[:, span]) for b, w in zip(blocks, gates)), gate_tile[:, span])
                new_up = sum((dot32(b[...], w[:, span]) for b, w in zip(blocks, ups)), up_tile[:, span])
                project(first + i, parts)
                gate[...], up[...] = new_gate, new_up

            halves(tile, part)

        pltpu.emit_pipeline(
            step, grid=(steps,),
            in_specs=weight_specs(ids, slots, depth, tile) + [tiled(rows, tile)] * 2, out_specs=[],
        )(*[gate_w] * count, *[up_w] * count, gate_sum, up_sum)
        project(last, [hidden_of(last, chunk) for chunk in chunks])

    return kernel_call(
        kernel, "late", ids, [at_side, at_middle, gate_w, up_w, proj_in, *sums, *xs],
        [VMEM] * 2 + [ANY] * 2 + [VMEM] + [ANY] * 2 + [VMEM] * len(xs),
        jax.ShapeDtypeStruct((most, rank), F32), VMEM,
        [pltpu.VMEM((rows, depth), BF16)] + [pltpu.VMEM((rows, TILE), F32)] * 2,
        4 * count * rows * depth * units, 4 * count * depth * units,
    )


MIDDLE, OUT = [(1, 2), (2, 1)], [(1, 0), (2, 3)]


def gathered(x):
    return lax.all_gather(x, "mp", axis=1, tiled=True)


def hop(x, pairs):
    return lax.ppermute(x, "mp", pairs)


def rest_case(size, ids, xs1, ends1, sums_own, rows, gate_w, up_w, proj_in):
    x = rows[:size]
    side, far = swap(x, "mp", 1), swap(x, "mp", 3)
    act1 = projected(ids, (1, 3, 2), xs1, *ends1, sums_own, gate_w, up_w, proj_in, FIRST)
    side, far, act1 = lax.optimization_barrier((side, far, act1))
    at_side, at_middle = hop(far, OUT), hop(side, MIDDLE)
    sums = sums_of(ids, (0, 1, 3), (x, side, far), gate_w, up_w)
    act2 = projected(ids, (2,), (), at_side, at_middle, sums, gate_w, up_w, proj_in, rows.shape[0])
    return act1, act2


def swap(x, axis, k, size=4):
    return lax.ppermute(x, axis, [(s, s ^ k) for s in range(size)])


def sketch_of_kept(tokens, grad_out, gate_w, up_w, proj_in, proj_out, lengths, loss_mask, queries):
    most, depth = tokens.shape
    rank = proj_in.shape[1]
    team_at = lax.axis_index("dp").astype(I32).reshape(1)
    order, cells, own1 = call(
        first_kernel, "first", [SMEM] * 2 + [VMEM] * 2,
        (
            jax.ShapeDtypeStruct(loss_mask.shape, I32),
            jax.ShapeDtypeStruct((8, 128), F32),
            jax.ShapeDtypeStruct((FIRST, depth), BF16),
        ),
        (VMEM,) * 3, team_at, lengths, loss_mask, tokens,
    )
    side1, far1 = swap(own1, "mp", 1), swap(own1, "mp", 3)
    me = lax.axis_index("mp").astype(I32)
    ids = jnp.stack([me, me ^ 1, me ^ 2, me ^ 3])
    grad_part = lax.dot_general(proj_out, grad_out, (((0,), (1,)), ((), ())), preferred_element_type=F32)
    high = lax.reduce_precision(grad_part, 8, 7)
    grads = jnp.concatenate([high.astype(BF16), (grad_part - high).astype(BF16)], axis=0)
    cells, grads = lax.optimization_barrier((cells, grads))
    cells = cells + swap(cells, "dp", 1) + swap(cells, "dp", 2) + swap(cells, "dp", 3)
    table = cells[:TEAM, :2].astype(I32).reshape(-1)
    sizes = sorted({s for s in SIZES if s < most - FIRST} | {most - FIRST})
    hand = jax.ShapeDtypeStruct((CAP, depth + 2 * rank), BF16)
    lots, *hands = call(
        functools.partial(deal_kernel, sizes), "deal", [SMEM] * 2 + [VMEM] * 3,
        (jax.ShapeDtypeStruct((3 * TEAM + 2,), I32),) + (hand,) * 3,
        (SMEM,) + (VMEM,) * 3, table, team_at, order, tokens, grads,
    )
    own1, *hands = lax.optimization_barrier((own1, *hands))
    hands = [swap(hand, "dp", k) for k, hand in zip((1, 2, 3), hands)]
    sums_own = sums_of(ids, (0,), (own1,), gate_w, up_w)
    side1, far1, sums_own, queries, *hands = lax.optimization_barrier((side1, far1, sums_own, queries, *hands))
    all_queries = lax.all_gather(queries, "dp", axis=0)
    ends1 = hop(far1, OUT), hop(side1, MIDDLE)
    rows, grads = call(
        place_kernel, "place", [SMEM] * 2 + [VMEM] * 6,
        (
            jax.ShapeDtypeStruct((most - FIRST, depth), BF16),
            jax.ShapeDtypeStruct((rank, most), F32),
        ),
        (VMEM,) * 2, lots, team_at, order, tokens, grads, *hands,
    )
    grads, *ends1 = lax.optimization_barrier((grads, *ends1))
    grads = lax.psum(grads, "mp")
    padded = jnp.pad(proj_in, ((0, -proj_in.shape[0] % (2 * TILE)), (0, 0)))
    act1, act2 = lax.switch(
        lots[3 * TEAM + 1], [functools.partial(rest_case, s) for s in sizes],
        ids, (side1, far1), ends1, sums_own, rows, gate_w, up_w, padded,
    )
    parts = call(
        sketch_kernel, "sketch", [SMEM] * 3 + [VMEM] * 3, jax.ShapeDtypeStruct((2 * TEAM * rank, rank), F32),
        VMEM, table, lots, team_at, grads, act1, act2,
    )
    parts = parts.reshape(TEAM, 2 * rank, rank)
    me = team_at[0]
    part = lax.dynamic_index_in_dim(parts, me, 0, False)
    for k in (1, 2, 3):
        part = part + swap(lax.dynamic_index_in_dim(parts, me ^ k, 0, False), "dp", k)
    return part + swap(part, "mp", 1) + swap(part, "mp", 2) + swap(part, "mp", 3), all_queries


def sketch_in_general(tokens, grad_out, gate_w, up_w, proj_in, proj_out, lengths, loss_mask, queries):
    roll_count, seq_len = loss_mask.shape
    rank = proj_in.shape[1]
    keep = (jnp.arange(seq_len, dtype=I32)[None, :] < lengths[:, None]) & (loss_mask == 1)
    pieces = gathered(tokens)
    hidden = (jax.nn.silu(dot32(pieces, gate_w)) * dot32(pieces, up_w)).astype(BF16)
    stacked = jnp.concatenate([dot32(grad_out, proj_out), dot32(hidden, proj_in)], axis=1)
    summed = lax.psum(stacked, "mp").reshape(roll_count, seq_len, 2 * rank)
    weighted = summed[:, :, :rank] * keep.astype(F32)[:, :, None]
    sums = jnp.einsum("rti,rtj->rij", weighted, summed[:, :, rank:], precision=lax.Precision.HIGHEST)
    return sums, lax.all_gather(queries, "dp", axis=0)


def local(team, planes, tokens, grad_out, gate_w, up_w, proj_in, proj_out, lengths, loss_mask, queries):
    roll_count, seq_len = loss_mask.shape
    fits = team == TEAM and planes == PLANES and roll_count == 2 and seq_len % 256 == 0
    fits = fits and tokens.shape[1] % 128 == 0 and gate_w.shape[1] % 128 == 0 and proj_in.shape[1] == 64
    form = sketch_of_kept if fits else sketch_in_general
    sketch_sum, all_queries = form(
        tokens, grad_out, gate_w, up_w, proj_in, proj_out, lengths, loss_mask, queries
    )
    norm_factor = 1.0 / jnp.sqrt(jnp.float32(seq_len))
    sketch = (sketch_sum.reshape(roll_count, team, -1) * norm_factor).astype(BF16)
    return jnp.einsum("rdk,dqk->rq", sketch, all_queries, preferred_element_type=F32)


def solution(mesh):
    placed = (
        P(("groups", "dp"), "mp"),
        P(("groups", "dp"), "mp"),
        P(None, "mp"),
        P(None, "mp"),
        P("mp", None),
        P("mp", None),
        P(("groups", "dp")),
        P(("groups", "dp"), None),
        P("mp", "dp"),
    )
    return jax.shard_map(
        functools.partial(local, mesh.shape["dp"], mesh.shape["mp"]),
        mesh=mesh, in_specs=placed, out_specs=P(("groups", "dp"), "mp"), check_vma=False,
    )
```

```python
import functools

import jax
import jax.numpy as jnp
from jax import lax
from jax.experimental import pallas as pl
from jax.experimental.pallas import tpu as pltpu
from jax.sharding import PartitionSpec as P

BF16, F32, I32 = jnp.bfloat16, jnp.float32, jnp.int32
FIRST = 256
SIZES = (176, 208, 240, 272, 320, 400)
CAP = 192
TEAM = 4
PLANES = 4
TILE = 256
MIB = 2**20


def dot32(a, b):
    return jnp.dot(a, b, preferred_element_type=F32)


def dot32_t(a, b):
    return lax.dot_general(a, b, (((1,), (1,)), ((), ())), preferred_element_type=F32)


def iota(shape, axis):
    return lax.broadcasted_iota(I32, shape, axis)


def ones_where(cond):
    return jnp.where(cond, 1.0, 0.0).astype(BF16)


def dealt(rest, most):
    keep = [jnp.minimum(m, most) for m in rest]
    spare_at, room_at, a, b = [], [], 0, 0
    for m, k in zip(rest, keep):
        spare_at.append(a)
        room_at.append(b)
        a, b = a + (m - k), b + (most - k)
    start, moved = {}, {}
    for s in range(TEAM):
        for t in range(TEAM):
            if s != t:
                low = jnp.maximum(spare_at[s], room_at[t])
                high = jnp.minimum(spare_at[s] + rest[s] - keep[s], room_at[t] + most - keep[t])
                start[s, t], moved[s, t] = low, jnp.maximum(high - low, 0)
    return keep, spare_at, room_at, start, moved


def plan(table):
    rest = [jnp.maximum(table[2 * s + 1] - FIRST, 0) for s in range(TEAM)]
    even = (rest[0] + rest[1] + rest[2] + rest[3] + (TEAM - 1)) // TEAM
    most = functools.reduce(jnp.maximum, rest)
    for tried in ((3 * most + even) // 4, (most + even) // 2, even):
        largest = functools.reduce(jnp.maximum, dealt(rest, tried)[4].values())
        most = jnp.where(largest <= CAP, tried, most)
    keep, spare_at, room_at, start, moved = dealt(rest, most)
    lots = {}
    for s in range(TEAM):
        lots[s, s] = (FIRST, 0, keep[s])
        for t in range(TEAM):
            if s != t:
                rank = FIRST + keep[s] + start[s, t] - spare_at[s]
                lots[s, t] = (rank, keep[t] + start[s, t] - room_at[t], moved[s, t])
    return most, lots


def chosen(lots, pairs):
    out = [0, 0, 0]
    for cond, pair in pairs:
        out = [jnp.where(cond, new, old) for new, old in zip(lots[pair], out)]
    return out


def first_kernel(team_at, lengths, loss_mask, tokens, order, table, rows):
    seq_len = loss_mask.shape[1]
    limit = jnp.where(iota(loss_mask.shape, 0) == 0, lengths[0], lengths[1])
    keep = (iota(loss_mask.shape, 1) < limit) & (loss_mask[...] == 1)
    upto = ones_where(iota((seq_len, seq_len), 0) <= iota((seq_len, seq_len), 1))
    kept = jnp.where(keep, 1.0, 0.0)
    place = dot32(kept.astype(BF16), upto)
    before = jnp.sum(kept[0:1], axis=1, keepdims=True)
    total = before + jnp.sum(kept[1:2], axis=1, keepdims=True)
    place = place - 1.0 + jnp.where(iota(place.shape, 0) == 0, 0.0, before)
    ranks = jnp.where(keep, place, -1.0).astype(I32)
    order[...] = ranks
    cell = jnp.where(iota(table.shape, 1) == 0, before, total)
    table[...] = jnp.where(iota(table.shape, 0) == team_at[0], cell, 0.0)
    at = iota((FIRST, seq_len), 0)
    found = dot32(ones_where(ranks[0:1] == at), tokens[:seq_len])
    found += dot32(ones_where(ranks[1:2] == at), tokens[seq_len:])
    rows[...] = found.astype(BF16)


def deal_kernel(sizes, table, team_at, order, tokens, grads, lots_to_me, *hands):
    me, seq_len = team_at[0], order.shape[1]
    most, lots = plan(table)
    lots_to_me[3 * TEAM] = most
    lots_to_me[3 * TEAM + 1] = sum((most > size).astype(I32) for size in sizes[:-1])
    for s in range(TEAM):
        for i, value in enumerate(chosen(lots, [(me == t, (s, t)) for t in range(TEAM)])):
            lots_to_me[3 * s + i] = value
    depth = tokens.shape[1]
    at = iota((CAP, seq_len), 0)
    for k, hand in zip(range(1, TEAM), hands):
        rank, _, number = chosen(lots, [(me == s, (s, s ^ k)) for s in range(TEAM)])
        valid = at < number
        for side in range(2):
            pick = ones_where((order[side : side + 1] - rank == at) & valid)
            span = slice(side * seq_len, (side + 1) * seq_len)
            found, grad = dot32(pick, tokens[span]), dot32_t(pick, grads[:, span])
            if side == 0:
                hand[:, :depth], hand[:, depth:] = found.astype(BF16), grad.astype(BF16)
            else:
                hand[:, :depth] += found.astype(BF16)
                hand[:, depth:] += grad.astype(BF16)


def place_kernel(lots_to_me, team_at, order, tokens, grads, hand1, hand2, hand3, rows, grads_here):
    me, seq_len = team_at[0], order.shape[1]
    depth, rank_size = tokens.shape[1], grads_here.shape[0]
    kept, size = lots_to_me[3 * me + 2], lots_to_me[3 * TEAM]
    at = iota((FIRST, seq_len), 0)

    def picked(base, valid):
        hits = [order[side : side + 1] - base == at for side in range(2)]
        return [ones_where(hit if valid is None else hit & valid) for hit in hits]

    def grad_of(picks):
        return dot32_t(grads[:, :seq_len], picks[0]) + dot32_t(grads[:, seq_len:], picks[1])

    grad = grad_of(picked(0, None))
    grads_here[:, :FIRST] = grad[:rank_size] + grad[rank_size:]

    def block(i, carry):
        base = pl.multiple_of(i * FIRST, FIRST)
        picks = picked(base + FIRST, at + base < kept)
        found = dot32(picks[0], tokens[:seq_len]) + dot32(picks[1], tokens[seq_len:])
        source, target = iota((FIRST, CAP), 1), iota((FIRST, CAP), 0) + base
        dealt_grad = 0.0
        for k, hand in ((1, hand1), (2, hand2), (3, hand3)):
            row, number = lots_to_me[3 * (me ^ k) + 1], lots_to_me[3 * (me ^ k) + 2]
            put = ones_where((target - row == source) & (source < number))
            found += dot32(put, hand[:, :depth])
            dealt_grad += dot32(put, hand[:, depth:])
        grad = grad_of(picks) + dealt_grad.T
        rows[pl.ds(base, FIRST), :] = found.astype(BF16)
        grads_here[:, pl.ds(base + FIRST, FIRST)] = grad[:rank_size] + grad[rank_size:]
        return carry

    lax.fori_loop(0, (size + FIRST - 1) // FIRST, block, 0)


def sketch_kernel(table, lots_to_me, team_at, grads, act1, act2, out):
    me, size = team_at[0], lots_to_me[3 * TEAM]

    def product(grad, lane, act):
        parts = []
        for s in range(TEAM):
            rank, row, number = lots_to_me[3 * s], lots_to_me[3 * s + 1] + FIRST, lots_to_me[3 * s + 2]
            edge = jnp.clip(row + table[2 * s] - rank, row, row + number)
            own = (me == s) & (lane < FIRST)
            cut = table[2 * s]
            for low, high, early in ((row, edge, lane < cut), (edge, row + number, lane >= cut)):
                mine = ((lane >= low) & (lane < high)) | (own & early)
                parts.append(jnp.where(mine, grad, 0.0))
        return jnp.dot(
            jnp.concatenate(parts, axis=0), act, precision=lax.Precision.HIGHEST, preferred_element_type=F32
        )

    out[...] = product(grads[:, :FIRST], iota((1, FIRST), 1), act1[...])

    def step(chunk, carry):
        base = pl.multiple_of(chunk * FIRST, FIRST)
        act = act2[pl.ds(base, FIRST), :]
        act = jnp.where(iota(act.shape, 0) + base < size, act, 0.0)
        lane = iota((1, FIRST), 1) + base + FIRST
        out[...] += product(grads[:, pl.ds(base + FIRST, FIRST)], lane, act)
        return carry

    lax.fori_loop(0, (size + FIRST - 1) // FIRST, step, 0)


ANY = pl.BlockSpec(memory_space=pl.ANY)
VMEM = pl.BlockSpec(memory_space=pltpu.VMEM)
SMEM = pl.BlockSpec(memory_space=pltpu.SMEM)


def call(kernel, name, specs, out_shape, out_specs, *args):
    return pl.pallas_call(
        kernel, out_shape=out_shape, in_specs=specs, out_specs=out_specs, name=name,
        compiler_params=pltpu.CompilerParams(vmem_limit_bytes=32 * MIB),
    )(*args)


def weight_specs(ids, slots, depth, tile):
    deep = pl.Buffered(2 if len(slots) > 1 and tile > TILE else 3)
    return [pl.BlockSpec((depth, tile), lambda j, s=s: (ids[s], j), pipeline_mode=deep) for s in slots] * 2


def tiled(rows, tile):
    return pl.BlockSpec((rows, tile), lambda j: (0, j))


def kernel_call(kernel, name, ids, operands, specs, out_shape, out_specs, scratch, flops, moved):
    return pl.pallas_call(
        kernel,
        in_specs=[SMEM] + specs, out_specs=out_specs, out_shape=out_shape, scratch_shapes=scratch, name=name,
        compiler_params=pltpu.CompilerParams(vmem_limit_bytes=38 * MIB),
        cost_estimate=pl.CostEstimate(flops=flops, bytes_accessed=moved, transcendentals=0),
    )(ids, *operands)


def halves(tile, body):
    def step(part, carry):
        body(part, pl.ds(pl.multiple_of(part * TILE, TILE), TILE))
        return carry

    lax.fori_loop(0, tile // TILE, step, 0)


def sums_of(ids, slots, xs, gate_w, up_w, tile=TILE):
    (rows, depth), units, count = xs[0].shape, gate_w.shape[1], len(xs)
    steps = -(-units // tile)

    def kernel(ids, *refs):
        x_refs, (gate_w, up_w, gate_sum, up_sum) = refs[:count], refs[count:]

        def step(*tiles):
            gates, ups, (gate, up) = tiles[:count], tiles[count : 2 * count], tiles[2 * count :]
            gate[...] = sum(dot32(x[...], w[...]) for x, w in zip(x_refs, gates))
            up[...] = sum(dot32(x[...], w[...]) for x, w in zip(x_refs, ups))

        pltpu.emit_pipeline(
            step, grid=(steps,), in_specs=weight_specs(ids, slots, depth, tile), out_specs=[tiled(rows, tile)] * 2
        )(*[gate_w] * count, *[up_w] * count, gate_sum, up_sum)

    out = jax.ShapeDtypeStruct((rows, steps * tile), F32)
    return kernel_call(
        kernel, "sums", ids, [*xs, gate_w, up_w], [VMEM] * count + [ANY] * 2, (out, out), (ANY, ANY), (),
        4 * count * rows * depth * units, 4 * count * depth * units,
    )


def projected(ids, slots, xs, at_side, at_middle, sums, gate_w, up_w, proj_in, most, tile=2 * TILE):
    (rows, depth), units, rank, count = at_side.shape, gate_w.shape[1], proj_in.shape[1], len(slots)
    steps, last = proj_in.shape[0] // tile, proj_in.shape[0] // TILE - 1

    def kernel(ids, at_side, at_middle, gate_w, up_w, proj, gate_sum, up_sum, *refs):
        x_refs, (act, x, gate, up) = refs[: count - 1], refs[count - 1 :]
        middle = (ids[0] == 1) | (ids[0] == 2)
        x[...] = jnp.where(middle, at_middle[...], at_side[...])
        act[:rows] = jnp.zeros((rows, rank), F32)

        half = -(-rows // 32) * 16
        chunks = [(at, min(half, rows - at)) for at in range(0, rows, half)]

        def hidden_of(j, chunk):
            span = pl.ds(*chunk)
            v = 0.5 * gate[span, :]
            hidden = (v + v * jnp.tanh(v)) * up[span, :]
            column = iota(hidden.shape, 1) + j * TILE
            return jnp.where((column >= 0) & (column < units), hidden, 0.0).astype(BF16)

        def project(j, parts):
            at = pl.multiple_of(jnp.maximum(j, 0) * TILE, TILE)
            act[:rows] += dot32(jnp.concatenate(parts, axis=0), proj[pl.ds(at, TILE), :])

        def step(*tiles):
            gates, ups, (gate_tile, up_tile) = tiles[:count], tiles[count : 2 * count], tiles[2 * count :]
            first = pl.program_id(0) * (tile // TILE) - 1
            blocks = [*x_refs, x]

            def part(i, span):
                parts = [hidden_of(first + i, chunk) for chunk in chunks]
                new_gate = sum((dot32(b[...], w[:, span]) for b, w in zip(blocks, gates)), gate_tile[:, span])
                new_up = sum((dot32(b[...], w[:, span]) for b, w in zip(blocks, ups)), up_tile[:, span])
                project(first + i, parts)
                gate[...], up[...] = new_gate, new_up

            halves(tile, part)

        pltpu.emit_pipeline(
            step, grid=(steps,),
            in_specs=weight_specs(ids, slots, depth, tile) + [tiled(rows, tile)] * 2, out_specs=[],
        )(*[gate_w] * count, *[up_w] * count, gate_sum, up_sum)
        project(last, [hidden_of(last, chunk) for chunk in chunks])

    return kernel_call(
        kernel, "late", ids, [at_side, at_middle, gate_w, up_w, proj_in, *sums, *xs],
        [VMEM] * 2 + [ANY] * 2 + [VMEM] + [ANY] * 2 + [VMEM] * len(xs),
        jax.ShapeDtypeStruct((most, rank), F32), VMEM,
        [pltpu.VMEM((rows, depth), BF16)] + [pltpu.VMEM((rows, TILE), F32)] * 2,
        4 * count * rows * depth * units, 4 * count * depth * units,
    )


MIDDLE, OUT = [(1, 2), (2, 1)], [(1, 0), (2, 3)]


def gathered(x):
    return lax.all_gather(x, "mp", axis=1, tiled=True)


def hop(x, pairs):
    return lax.ppermute(x, "mp", pairs)


def rest_case(size, ids, xs1, ends1, sums_own, rows, gate_w, up_w, proj_in):
    x = rows[:size]
    side, far = swap(x, "mp", 1), swap(x, "mp", 3)
    act1 = projected(ids, (1, 3, 2), xs1, *ends1, sums_own, gate_w, up_w, proj_in, FIRST)
    side, far, act1 = lax.optimization_barrier((side, far, act1))
    at_side, at_middle = hop(far, OUT), hop(side, MIDDLE)
    sums = sums_of(ids, (0, 1, 3), (x, side, far), gate_w, up_w)
    act2 = projected(ids, (2,), (), at_side, at_middle, sums, gate_w, up_w, proj_in, rows.shape[0])
    return act1, act2


def swap(x, axis, k, size=4):
    return lax.ppermute(x, axis, [(s, s ^ k) for s in range(size)])


def sketch_of_kept(tokens, grad_out, gate_w, up_w, proj_in, proj_out, lengths, loss_mask, queries):
    most, depth = tokens.shape
    rank = proj_in.shape[1]
    team_at = lax.axis_index("dp").astype(I32).reshape(1)
    order, cells, own1 = call(
        first_kernel, "first", [SMEM] * 2 + [VMEM] * 2,
        (
            jax.ShapeDtypeStruct(loss_mask.shape, I32),
            jax.ShapeDtypeStruct((8, 128), F32),
            jax.ShapeDtypeStruct((FIRST, depth), BF16),
        ),
        (VMEM,) * 3, team_at, lengths, loss_mask, tokens,
    )
    side1, far1 = swap(own1, "mp", 1), swap(own1, "mp", 3)
    me = lax.axis_index("mp").astype(I32)
    ids = jnp.stack([me, me ^ 1, me ^ 2, me ^ 3])
    grad_part = lax.dot_general(proj_out, grad_out, (((0,), (1,)), ((), ())), preferred_element_type=F32)
    high = lax.reduce_precision(grad_part, 8, 7)
    grads = jnp.concatenate([high.astype(BF16), (grad_part - high).astype(BF16)], axis=0)
    cells, grads = lax.optimization_barrier((cells, grads))
    cells = cells + swap(cells, "dp", 1) + swap(cells, "dp", 2) + swap(cells, "dp", 3)
    table = cells[:TEAM, :2].astype(I32).reshape(-1)
    sizes = sorted({s for s in SIZES if s < most - FIRST} | {most - FIRST})
    hand = jax.ShapeDtypeStruct((CAP, depth + 2 * rank), BF16)
    lots, *hands = call(
        functools.partial(deal_kernel, sizes), "deal", [SMEM] * 2 + [VMEM] * 3,
        (jax.ShapeDtypeStruct((3 * TEAM + 2,), I32),) + (hand,) * 3,
        (SMEM,) + (VMEM,) * 3, table, team_at, order, tokens, grads,
    )
    own1, *hands = lax.optimization_barrier((own1, *hands))
    hands = [swap(hand, "dp", k) for k, hand in zip((1, 2, 3), hands)]
    sums_own = sums_of(ids, (0,), (own1,), gate_w, up_w)
    padded, case = jnp.pad(proj_in, ((0, -proj_in.shape[0] % (2 * TILE)), (0, 0))), lots[3 * TEAM + 1]
    side1, far1, sums_own, queries, padded, case, *hands = lax.optimization_barrier(
        (side1, far1, sums_own, queries, padded, case, *hands)
    )
    all_queries = lax.all_gather(queries, "dp", axis=0)
    ends1 = hop(far1, OUT), hop(side1, MIDDLE)
    rows, grads = call(
        place_kernel, "place", [SMEM] * 2 + [VMEM] * 6,
        (
            jax.ShapeDtypeStruct((most - FIRST, depth), BF16),
            jax.ShapeDtypeStruct((rank, most), F32),
        ),
        (VMEM,) * 2, lots, team_at, order, tokens, grads, *hands,
    )
    grads, *ends1 = lax.optimization_barrier((grads, *ends1))
    grads = lax.psum(grads, "mp")
    act1, act2 = lax.switch(
        case, [functools.partial(rest_case, s) for s in sizes],
        ids, (side1, far1), ends1, sums_own, rows, gate_w, up_w, padded,
    )
    parts = call(
        sketch_kernel, "sketch", [SMEM] * 3 + [VMEM] * 3, jax.ShapeDtypeStruct((2 * TEAM * rank, rank), F32),
        VMEM, table, lots, team_at, grads, act1, act2,
    )
    parts = parts.reshape(TEAM, 2 * rank, rank)
    me = team_at[0]
    part = lax.dynamic_index_in_dim(parts, me, 0, False)
    for k in (1, 2, 3):
        part = part + swap(lax.dynamic_index_in_dim(parts, me ^ k, 0, False), "dp", k)
    return part + swap(part, "mp", 1) + swap(part, "mp", 2) + swap(part, "mp", 3), all_queries


def sketch_in_general(tokens, grad_out, gate_w, up_w, proj_in, proj_out, lengths, loss_mask, queries):
    roll_count, seq_len = loss_mask.shape
    rank = proj_in.shape[1]
    keep = (jnp.arange(seq_len, dtype=I32)[None, :] < lengths[:, None]) & (loss_mask == 1)
    pieces = gathered(tokens)
    hidden = (jax.nn.silu(dot32(pieces, gate_w)) * dot32(pieces, up_w)).astype(BF16)
    stacked = jnp.concatenate([dot32(grad_out, proj_out), dot32(hidden, proj_in)], axis=1)
    summed = lax.psum(stacked, "mp").reshape(roll_count, seq_len, 2 * rank)
    weighted = summed[:, :, :rank] * keep.astype(F32)[:, :, None]
    sums = jnp.einsum("rti,rtj->rij", weighted, summed[:, :, rank:], precision=lax.Precision.HIGHEST)
    return sums, lax.all_gather(queries, "dp", axis=0)


def local(team, planes, tokens, grad_out, gate_w, up_w, proj_in, proj_out, lengths, loss_mask, queries):
    roll_count, seq_len = loss_mask.shape
    fits = team == TEAM and planes == PLANES and roll_count == 2 and seq_len % 256 == 0
    fits = fits and tokens.shape[1] % 128 == 0 and gate_w.shape[1] % 128 == 0 and proj_in.shape[1] == 64
    form = sketch_of_kept if fits else sketch_in_general
    sketch_sum, all_queries = form(
        tokens, grad_out, gate_w, up_w, proj_in, proj_out, lengths, loss_mask, queries
    )
    norm_factor = 1.0 / jnp.sqrt(jnp.float32(seq_len))
    sketch = (sketch_sum.reshape(roll_count, team, -1) * norm_factor).astype(BF16)
    return jnp.einsum("rdk,dqk->rq", sketch, all_queries, preferred_element_type=F32)


def solution(mesh):
    placed = (
        P(("groups", "dp"), "mp"),
        P(("groups", "dp"), "mp"),
        P(None, "mp"),
        P(None, "mp"),
        P("mp", None),
        P("mp", None),
        P(("groups", "dp")),
        P(("groups", "dp"), None),
        P("mp", "dp"),
    )
    return jax.shard_map(
        functools.partial(local, mesh.shape["dp"], mesh.shape["mp"]),
        mesh=mesh, in_specs=placed, out_specs=P(("groups", "dp"), "mp"), check_vma=False,
    )
```
